32 devices in a mesh: dp: 8 (over z, x), row: 2 (over y), col: 2 (over core).
Axes of the slice: x: 2, y: 2, z: 4, core: 2. Of those that a mesh axis runs over, the one named last changes fastest.
Arguments:
- tokens: bfloat16 [4096, 768], P(('dp', 'col'), 'row'), may hold values from -6 to 6
- out_grad: bfloat16 [4096, 768], P(('dp', 'col'), 'row'), may hold values from -6 to 6
- seq_lengths: int32 [8, 2], P('dp'), may hold values from 0 to 512, as said below
- w_query: bfloat16 [768, 768], P('row', 'col'), may hold values from -0.21875 to 0.21875
- w_key: bfloat16 [768, 768], P('row', 'col'), may hold values from -0.21875 to 0.21875
- w_value: bfloat16 [768, 768], P('row', 'col'), may hold values from -0.21875 to 0.21875
- w_out: bfloat16 [768, 768], P('col', 'row'), may hold values from -1.75 to 1.75
- w_up: bfloat16 [768, 3072], P('row', 'col'), may hold values from -0.21875 to 0.21875
- w_down: bfloat16 [3072, 768], P('col', 'row'), may hold values from -0.109375 to 0.109375
- b_query: bfloat16 [768], P(('col', 'row')), may hold values from -3 to 3
- b_value: bfloat16 [768], P(('col', 'row')), may hold values from -3 to 3
- b_out: bfloat16 [768], P('row'), may hold values from -3 to 3
- b_up: bfloat16 [3072], P(('col', 'row')), may hold values from -3 to 3
- b_down: bfloat16 [768], P('row'), may hold values from -3 to 3
- gain_attn: bfloat16 [768], P('row'), may hold values from 0.25 to 1.75
- shift_attn: bfloat16 [768], P('row'), may hold values from -2 to 2
- gain_mlp: bfloat16 [768], P('row'), may hold values from 0.25 to 1.75
- shift_mlp: bfloat16 [768], P('row'), may hold values from -2 to 2
Outputs:
- output: bfloat16 [4096, 768], P(('dp', 'col'), 'row')
- input_grad: bfloat16 [4096, 768], P(('dp', 'col'), 'row')
- grad_query: float32 [768, 768], P('row', 'col')
- grad_key: float32 [768, 768], P('row', 'col')
- grad_value: float32 [768, 768], P('row', 'col')
- grad_out: float32 [768, 768], P('col', 'row')
- grad_up: float32 [768, 3072], P('row', 'col')
- grad_down: float32 [3072, 768], P('col', 'row')
- grad_b_query: float32 [768], P(('col', 'row'))
- grad_b_value: float32 [768], P(('col', 'row'))
- grad_b_out: float32 [768], P('row')
- grad_b_up: float32 [3072], P(('col', 'row'))
- grad_b_down: float32 [768], P('row')
- grad_gain_attn: float32 [768], P('row')
- grad_shift_attn: float32 [768], P('row')
- grad_gain_mlp: float32 [768], P('row')
- grad_shift_mlp: float32 [768], P('row')
The draws below stay inside these ranges and needn't reach their ends.
Inputs may be any that keep to these rules, and one draw needn't show every extreme that they name: `seq_lengths`: row g: the first sequence has 128 or more tokens, the two lengths sum to at most 512, the rest of the group's slots is padding; in some row the first length is 512 and the second 0.
All inputs are finite; a program needn't handle non-finite values.
Results may differ from the reference program's by a relative error of at most 0.014.
Values may be sent and summed in bfloat16 or wider, within the bound.
No kernel may reach another device: no remote copies, remote signals or barrier semaphores. Data moves between devices by JAX's collectives and lax.ppermute only.
A program may use at most 128 MiB of HBM per device.

```python
import jax
import jax.numpy as jnp
from jax import lax

D = 768
HEADS = 12
HEAD_DIM = 64
FF = 3072
TOK_DEV = 512
GROUPS = 8
TOKENS = 4096


def draw_seq_lengths(key, part):
    key = jax.random.fold_in(key, 11)
    first_key, second_key, chosen_key = jax.random.split(key, 3)
    first_len = jax.random.randint(first_key, (GROUPS,), TOK_DEV // 4, TOK_DEV + 1)
    second_len = jax.random.randint(second_key, (GROUPS,), 0, TOK_DEV + 1) % (TOK_DEV - first_len + 1)
    chosen = jax.random.randint(chosen_key, (), 0, GROUPS)
    groups_idx = jnp.arange(GROUPS, dtype=jnp.int32)
    first_len = jnp.where(groups_idx == chosen, TOK_DEV, first_len)
    second_len = jnp.where(groups_idx == chosen, 0, second_len)
    return jnp.stack([first_len, second_len], axis=1).astype(jnp.int32)


def levels(own_key, extent, shards, low, top_value):
    loudness, own = 1.0, jax.random.fold_in(own_key, 6)
    for dim, blocks in shards:
        steps = jnp.exp(jax.random.uniform(jax.random.fold_in(own, dim), (blocks,), jnp.float32, low / len(shards), top_value / len(shards)))
        loudness = loudness * jnp.repeat(steps, extent[dim] // blocks).reshape([-1 if axis == dim else 1 for axis in range(len(extent))])
    return loudness


def bell_draw(rng, dims, scale, bound, pieces=(), kind=jnp.bfloat16):
    entries = jax.random.normal(rng, dims, jnp.float32) * scale
    if len(pieces) > 0:
        entries = levels(rng, dims, pieces, -0.22, 0.18) * entries
    return jnp.clip(entries, min=-bound, max=bound).astype(kind)


def setup_inputs(seed: int = 0) -> dict:
    streams_of = jax.random.split(jax.random.key(seed), 19)
    return {
        "tokens": bell_draw(streams_of[0], (TOKENS, D), 1.0, 6.0, ((0, 16), (1, 2))),
        "out_grad": bell_draw(streams_of[1], (TOKENS, D), 1.0, 6.0, ((0, 16), (1, 2))),
        "seq_lengths": draw_seq_lengths(jax.random.fold_in(streams_of[18], 71), 0),
        "w_query": bell_draw(streams_of[3], (D, D), D ** -0.5, 0.21875, ((0, 2), (1, 2))),
        "w_key": bell_draw(streams_of[4], (D, D), D ** -0.5, 0.21875, ((0, 2), (1, 2))),
        "w_value": bell_draw(streams_of[5], (D, D), D ** -0.5, 0.21875, ((0, 2), (1, 2))),
        "w_out": bell_draw(streams_of[6], (D, D), (D // 64) ** -0.5, 1.75, ((0, 2), (1, 2))),
        "w_up": bell_draw(streams_of[7], (D, FF), D ** -0.5, 0.21875, ((0, 2), (1, 2))),
        "w_down": bell_draw(streams_of[8], (FF, D), FF ** -0.5, 0.109375, ((0, 2), (1, 2))),
        "b_query": bell_draw(streams_of[9], (D,), 0.5, 3.0, ((0, 4),)),
        "b_value": bell_draw(streams_of[10], (D,), 0.5, 3.0, ((0, 4),)),
        "b_out": bell_draw(streams_of[11], (D,), 0.5, 3.0, ((0, 2),)),
        "b_up": bell_draw(streams_of[12], (FF,), 0.5, 3.0, ((0, 4),)),
        "b_down": bell_draw(streams_of[13], (D,), 0.5, 3.0, ((0, 2),)),
        "gain_attn": jnp.clip(1.0 + 0.15 * jax.random.normal(streams_of[14], (D,), jnp.float32), 0.25, 1.75).astype(jnp.bfloat16),
        "shift_attn": bell_draw(streams_of[15], (D,), 0.3, 2.0, ((0, 2),)),
        "gain_mlp": jnp.clip(1.0 + 0.15 * jax.random.normal(streams_of[16], (D,), jnp.float32), 0.25, 1.75).astype(jnp.bfloat16),
        "shift_mlp": bell_draw(streams_of[17], (D,), 0.3, 2.0, ((0, 2),)),
    }


@jax.custom_vjp
def low(v):
    return lax.optimization_barrier(v.astype(jnp.bfloat16)).astype(jnp.float32)

@jax.custom_vjp
def low_back(v):
    return v

def low_keep(v):
    return (low(v), None)

def low_pass(kept, grad):
    return (grad,)

def back_keep(v):
    return (v, None)

def back_low(kept, grad):
    return (low(grad),)
low.defvjp(low_keep, low_pass)
low_back.defvjp(back_keep, back_low)
HIGHEST = lax.Precision.HIGHEST
EPSILON = 1e-05

def product(left, right):
    return jnp.dot(left, right, precision=HIGHEST)

def layer_norm(values, gain_vec, shift_vec):
    row_mean = lax.optimization_barrier(jnp.mean(values, axis=-1, keepdims=True))
    centered = values - row_mean
    variance = lax.optimization_barrier(jnp.mean(centered * centered, axis=-1, keepdims=True))
    return centered * lax.rsqrt(variance + EPSILON) * gain_vec + shift_vec

def split_heads(values):
    return values.reshape(TOK_DEV, HEADS, HEAD_DIM)

def group_layer(stream, lengths, parameters):
    w_query, w_key, w_value, w_out, w_up, w_down, b_query, b_value, b_out, b_up, b_down, gain_attn, shift_attn, gain_mlp, shift_mlp = parameters
    positions = jnp.arange(TOK_DEV, dtype=jnp.int32)
    live_total = lengths[0] + lengths[1]
    documents = (positions >= lengths[0]).astype(jnp.int32) + (positions >= live_total).astype(jnp.int32)
    allowed = (documents[:, None] == documents[None, :]) & (positions[None, :] <= positions[:, None])
    normed = low(layer_norm(stream, gain_attn, shift_attn))
    query = low(low_back(product(normed, w_query) + b_query))
    keys_all = low(low_back(product(normed, w_key)))
    values_all = low(low_back(product(normed, w_value) + b_value))
    raw_scores = jnp.einsum('qhd,khd->hqk', split_heads(query), split_heads(keys_all), precision=HIGHEST)
    scores = low_back(raw_scores) * HEAD_DIM ** (-0.5)
    scores = jnp.where(allowed[None], scores, -1e+30)
    probs = low(jax.nn.softmax(scores, axis=-1))
    mixed = jnp.einsum('hqk,khd->qhd', probs, split_heads(values_all), precision=HIGHEST)
    mixed = low(low_back(mixed.reshape(TOK_DEV, D)))
    middle = stream + low_back(product(mixed, w_out) + b_out)
    normed_mlp = low(layer_norm(middle, gain_mlp, shift_mlp))
    pre_act = low_back(product(normed_mlp, w_up) + b_up)
    hidden = low(jax.nn.gelu(pre_act, approximate=True))
    return middle + low_back(product(hidden, w_down) + b_down)

def full_layer(stream, parameters, seq_lengths):
    group_step = jax.checkpoint(group_layer)

    def visit_group(carried, members):
        return (carried, group_step(members[0], members[1], parameters))
    _, result = lax.scan(visit_group, jnp.zeros((), jnp.float32), (stream.reshape(GROUPS, TOK_DEV, D), seq_lengths))
    return result.reshape(GROUPS * TOK_DEV, D)

def reference(tokens, out_grad, seq_lengths, w_query, w_key, w_value, w_out, w_up, w_down, b_query, b_value, b_out, b_up, b_down, gain_attn, shift_attn, gain_mlp, shift_mlp):
    parameters = tuple((item.astype(jnp.float32) for item in (w_query, w_key, w_value, w_out, w_up, w_down, b_query, b_value, b_out, b_up, b_down, gain_attn, shift_attn, gain_mlp, shift_mlp)))
    stream = tokens.astype(jnp.float32)

    def forward(stream_in, params_in):
        return full_layer(stream_in, params_in, seq_lengths)
    result, pullback = jax.vjp(forward, stream, parameters)
    positions = jnp.arange(TOK_DEV, dtype=jnp.int32)
    live_rows = (positions[None, :] < (seq_lengths[:, 0] + seq_lengths[:, 1])[:, None]).astype(jnp.float32)
    cotangent = out_grad.astype(jnp.float32) * live_rows.reshape(GROUPS * TOK_DEV, 1)
    grad_stream, grads = pullback(cotangent)
    return (result.astype(jnp.bfloat16), grad_stream.astype(jnp.bfloat16), grads[0], grads[1], grads[2], grads[3], grads[4], grads[5], grads[6], grads[7], grads[8], grads[9], grads[10], grads[11], grads[12], grads[13], grads[14])
```

```python
import jax
import jax.numpy as jnp
from jax import lax
from jax.sharding import PartitionSpec as P

HEAD_DIM = 64
EPSILON = 1e-05
MASKED = -1e30
F32 = jnp.float32
BF16 = jnp.bfloat16
SWAP = ((0, 1), (1, 0))


def dot(left, right):
    return jnp.dot(left, right, preferred_element_type=F32)


def dot_nt(left, right):
    return lax.dot_general(left, right, (((1,), (1,)), ((), ())), preferred_element_type=F32)


def dot_tn(left, right):
    return lax.dot_general(left, right, (((0,), (0,)), ((), ())), preferred_element_type=F32)


def from_row(values):
    return lax.ppermute(values, "row", SWAP)


def from_col(values):
    return lax.ppermute(values, "col", SWAP)


def pick(first, values, axis):
    size = values.shape[axis] // 2
    low = lax.slice_in_dim(values, 0, size, axis=axis)
    high = lax.slice_in_dim(values, size, 2 * size, axis=axis)
    return jnp.where(first == 0, low, high), jnp.where(first == 0, high, low)


def ordered(index, mine, other, axis):
    return jnp.where(
        index == 0,
        jnp.concatenate([mine, other], axis=axis),
        jnp.concatenate([other, mine], axis=axis),
    )


def both_tokens(col, own):
    return ordered(col, own, from_col(own), 0)


def swap_halves(values):
    half = values.shape[1] // 2
    return jnp.concatenate([values[:, half:], values[:, :half]], axis=1)


def own_token_sum(col, partial_sum):
    keep, send = pick(col, partial_sum, 0)
    return keep + from_col(send.astype(BF16)).astype(F32)


def dp_pairs(bit):
    count = lax.axis_size("dp")
    return [(i, i ^ (1 << bit)) for i in range(count)]


def halving(values, axis, bits):
    index = lax.axis_index("dp")
    for bit in bits:
        own = (index >> bit) & 1
        half = values.shape[axis] // 2
        send = lax.dynamic_slice_in_dim(values, (1 - own) * half, half, axis)
        keep = lax.dynamic_slice_in_dim(values, own * half, half, axis)
        received = lax.ppermute(send, "dp", dp_pairs(bit))
        values = (keep.astype(F32) + received.astype(F32)).astype(BF16)
    return values


def doubling(values, axis, bits):
    index = lax.axis_index("dp")
    for bit in reversed(bits):
        received = lax.ppermute(values, "dp", dp_pairs(bit))
        values = ordered((index >> bit) & 1, values, received, axis)
    return values


def bit_orders():
    count = lax.axis_size("dp").bit_length() - 1
    first = list(range(count))
    second = [1, 0] + first[2:] if count > 1 else first
    return first, second


def parts_of(values, axis):
    size = values.shape[axis]
    cut = size * 2 // 3
    orders = bit_orders()
    return (
        (lax.slice_in_dim(values, 0, cut, axis=axis), orders[0]),
        (lax.slice_in_dim(values, cut, size, axis=axis), orders[1]),
    )


def reduce_rows_first(values):
    done = []
    for part, order in parts_of(values, 1):
        reduced = halving(part, 1, order)
        both = jnp.stack([reduced[0], from_row(reduced[1])])
        done.append(doubling(both, 1, order))
    return jnp.concatenate(done, axis=1)


def reduce_columns(values):
    half = values.shape[1] // 2
    done = []
    for part, order in parts_of(values, 0):
        reduced = halving(part, 0, order)
        both = jnp.stack([reduced[:, :half], from_row(reduced[:, half:])])
        done.append(doubling(both, 1, order))
    return jnp.concatenate(done, axis=1)


def reduce_small(values):
    for bit in bit_orders()[0]:
        values = values + lax.ppermute(values, "dp", dp_pairs(bit))
    return values


def norm_forward(values, gain_vec, shift_vec):
    mean = jnp.mean(values, axis=1, keepdims=True)
    centered = values - mean
    variance = jnp.mean(centered * centered, axis=1, keepdims=True)
    inverse = lax.rsqrt(variance + EPSILON)
    unit = centered * inverse
    return (unit * gain_vec + shift_vec).astype(BF16), unit, inverse


def heads_of(values):
    return values.reshape(values.shape[0], -1, HEAD_DIM)


def scores_of(query, keys_all, allowed):
    raw = jnp.einsum("qhd,khd->hqk", query, keys_all, preferred_element_type=F32)
    return jnp.where(allowed[None], raw * HEAD_DIM ** (-0.5), MASKED)


def attention_forward(query, keys_all, values_all, allowed):
    scores = scores_of(query, keys_all, allowed)
    largest = jnp.max(scores, axis=-1, keepdims=True)
    weights = jnp.exp(scores - largest)
    summed = jnp.sum(weights, axis=-1, keepdims=True)
    probs = (weights / summed).astype(BF16)
    mixed = jnp.einsum("hqk,khd->qhd", probs, values_all, preferred_element_type=F32)
    return mixed, largest + jnp.log(summed)


def attention_backward(query, keys_all, values_all, grad_mixed, allowed, log_totals):
    scores = scores_of(query, keys_all, allowed)
    probs = jnp.exp(scores - log_totals)
    grad_probs = jnp.einsum("qhd,khd->hqk", grad_mixed, values_all, preferred_element_type=F32)
    inner = jnp.sum(probs * grad_probs, axis=-1, keepdims=True)
    grad_raw = (probs * (grad_probs - inner) * HEAD_DIM ** (-0.5)).astype(BF16)
    grad_q = jnp.einsum("hqk,khd->qhd", grad_raw, keys_all, preferred_element_type=F32)
    grad_k = jnp.einsum("hqk,qhd->khd", grad_raw, query, preferred_element_type=F32)
    grad_v = jnp.einsum(
        "hqk,qhd->khd", probs.astype(BF16), grad_mixed, preferred_element_type=F32
    )
    return grad_q, grad_k, grad_v


def body(
    tokens,
    out_grad,
    seq_lengths,
    w_query,
    w_key,
    w_value,
    w_out,
    w_up,
    w_down,
    b_query,
    b_value,
    b_out,
    b_up,
    b_down,
    gain_attn,
    shift_attn,
    gain_mlp,
    shift_mlp,
):
    row = lax.axis_index("row")
    col = lax.axis_index("col")
    own_rows, half = tokens.shape
    width = 2 * half
    group_rows = 2 * own_rows

    positions = jnp.arange(group_rows, dtype=jnp.int32)
    lengths = seq_lengths[0]
    live_total = lengths[0] + lengths[1]
    documents = (positions >= lengths[0]).astype(jnp.int32) + (positions >= live_total).astype(
        jnp.int32
    )
    allowed = (documents[:, None] == documents[None, :]) & (
        positions[None, :] <= positions[:, None]
    )
    own_positions = col * own_rows + jnp.arange(own_rows, dtype=jnp.int32)
    live_rows = (own_positions < live_total)[:, None]

    vectors = jnp.stack([gain_attn, shift_attn, b_out, gain_mlp, shift_mlp])
    tokens_other = from_row(tokens)
    vectors = jnp.concatenate([vectors, from_row(vectors)], axis=1).astype(F32)
    gain_a, shift_a, bias_o, gain_m, shift_m = [vectors[i : i + 1] for i in range(5)]

    kept, sent = zip(*[pick(row, w, 1) for w in (w_query, w_key, w_value)])
    kept, sent = jnp.concatenate(kept, axis=1), jnp.concatenate(sent, axis=1)
    w_qkv = jnp.concatenate([kept, from_row(sent)], axis=0)
    kept, sent = pick(row, w_out, 0)
    w_o = jnp.concatenate([kept, from_row(sent)], axis=1)
    kept, sent = pick(row, w_up, 1)
    w_u = jnp.concatenate([kept, from_row(sent)], axis=0)
    grad_other = from_row(out_grad)
    kept, sent = pick(row, w_down, 0)
    w_d = jnp.concatenate([kept, from_row(sent)], axis=1)

    residual = jnp.concatenate([tokens, tokens_other], axis=1).astype(F32)
    normed, unit_attn, inverse_attn = norm_forward(residual, gain_a, shift_a)
    normed_all = both_tokens(col, normed)

    third = w_query.shape[1] // 2
    zeros = jnp.zeros_like(b_query)
    projected = dot(normed_all, w_qkv) + jnp.concatenate([b_query, zeros, b_value]).astype(F32)
    projected = projected.astype(BF16)
    query, keys_all, values_all = [
        heads_of(projected[:, i * third : (i + 1) * third]) for i in range(3)
    ]
    mixed, log_totals = attention_forward(query, keys_all, values_all, allowed)
    mixed = mixed.astype(BF16).reshape(group_rows, -1)

    branch = own_token_sum(col, dot(mixed, w_o))
    middle = residual + (branch + swap_halves(from_row(branch.astype(BF16))).astype(F32) + bias_o)
    normed_mlp, unit_mlp, inverse_mlp = norm_forward(middle, gain_m, shift_m)
    normed_mlp_all = both_tokens(col, normed_mlp)
    pre_act = dot(normed_mlp_all, w_u) + b_up.astype(F32)
    hidden_wide, gelu_pullback = jax.vjp(lambda u: jax.nn.gelu(u, approximate=True), pre_act)
    hidden = hidden_wide.astype(BF16)

    top = jnp.where(live_rows, jnp.concatenate([out_grad, grad_other], axis=1), 0)
    top_all = both_tokens(col, top)
    grad_down = reduce_columns(dot_tn(hidden, top_all).astype(BF16))

    grad_pre = gelu_pullback(dot_nt(top_all, w_d))[0].astype(BF16)
    grad_up = dot_tn(normed_mlp_all, grad_pre).astype(BF16)
    grad_up = reduce_rows_first(grad_up.reshape(2, half, -1))

    grad_normed = own_token_sum(col, dot_nt(grad_pre, w_u))
    grad_normed = grad_normed + swap_halves(from_row(grad_normed.astype(BF16))).astype(F32)
    scaled = grad_normed * gain_m
    mean_plain = jnp.mean(scaled, axis=1, keepdims=True)
    mean_unit = jnp.mean(scaled * unit_mlp, axis=1, keepdims=True)
    grad_middle = top.astype(F32) + inverse_mlp * (scaled - mean_plain - unit_mlp * mean_unit)
    grad_gain_mlp = jnp.sum((grad_normed * unit_mlp)[:, :half], axis=0)
    grad_shift_mlp = jnp.sum(grad_normed[:, :half], axis=0)

    branch_grad = grad_middle.astype(BF16)
    branch_all = both_tokens(col, branch_grad)
    grad_out = dot_tn(branch_all, mixed)
    grad_mixed = heads_of(dot_nt(branch_all, w_o).astype(BF16))
    grad_q, grad_k, grad_v = attention_backward(
        query, keys_all, values_all, grad_mixed, allowed, log_totals
    )
    grad_qkv = jnp.concatenate(
        [part.astype(BF16).reshape(group_rows, -1) for part in (grad_q, grad_k, grad_v)], axis=1
    )
    attention_grads = jnp.concatenate([dot_tn(normed_all, grad_qkv), grad_out], axis=1)
    attention_grads = reduce_rows_first(attention_grads.astype(BF16).reshape(2, half, -1))

    grad_normed = own_token_sum(col, dot_nt(grad_qkv, w_qkv))
    scaled = grad_normed * gain_a
    sums = jnp.stack([jnp.sum(scaled, axis=1), jnp.sum(scaled * unit_attn, axis=1)])
    sums = (sums + from_row(sums)) / width
    grad_normed = grad_normed[:, :half] + from_row(grad_normed[:, half:].astype(BF16)).astype(F32)
    unit_own = unit_attn[:, :half]
    grad_in = inverse_attn * (
        grad_normed * gain_a[:, :half] - sums[0][:, None] - unit_own * sums[1][:, None]
    )
    input_grad = (grad_middle[:, :half] + grad_in).astype(BF16)
    grad_gain_attn = jnp.sum(grad_normed * unit_own, axis=0)
    grad_shift_attn = jnp.sum(grad_normed, axis=0)

    raised = own_token_sum(col, dot(hidden, w_d))
    raised = raised[:, :half] + from_row(raised[:, half:].astype(BF16)).astype(F32)
    output = (middle[:, :half] + raised + b_down.astype(F32)).astype(BF16)

    halves = jnp.concatenate([grad_gain_attn, grad_shift_attn, grad_gain_mlp, grad_shift_mlp])
    halves = halves + from_col(halves)
    wide_sums = jnp.sum(grad_qkv.astype(F32), axis=0)
    small = jnp.concatenate(
        [
            halves,
            wide_sums[:third],
            wide_sums[2 * third :],
            jnp.sum(branch_all[:, :half].astype(F32), axis=0),
            jnp.sum(grad_pre.astype(F32), axis=0),
            jnp.sum(top_all[:, :half].astype(F32), axis=0),
        ]
    )
    small = reduce_small(small)
    sizes = [half] * 4 + [third, third, half, b_up.shape[0], half]
    vectors, begin = [], 0
    for size in sizes:
        vectors.append(small[begin : begin + size])
        begin += size
    g_gain_a, g_shift_a, g_gain_m, g_shift_m, g_b_query, g_b_value, g_b_out, g_b_up, g_b_down = (
        vectors
    )

    def side_by_side(values):
        return ordered(row, values[0], values[1], 1).astype(F32)

    grad_query, grad_key, grad_value, grad_out = [
        side_by_side(attention_grads[:, :, i * third : (i + 1) * third]) for i in range(4)
    ]
    return (
        output,
        input_grad,
        grad_query,
        grad_key,
        grad_value,
        grad_out.T,
        side_by_side(grad_up),
        ordered(row, grad_down[0], grad_down[1], 0).astype(F32),
        g_b_query,
        g_b_value,
        g_b_out,
        g_b_up,
        g_b_down,
        g_gain_a,
        g_shift_a,
        g_gain_m,
        g_shift_m,
    )


def solution(mesh):
    return jax.shard_map(
        body,
        mesh=mesh,
        in_specs=(
            P(("dp", "col"), "row"),
            P(("dp", "col"), "row"),
            P("dp", None),
            P("row", "col"),
            P("row", "col"),
            P("row", "col"),
            P("col", "row"),
            P("row", "col"),
            P("col", "row"),
            P(("col", "row")),
            P(("col", "row")),
            P("row"),
            P(("col", "row")),
            P("row"),
            P("row"),
            P("row"),
            P("row"),
            P("row"),
        ),
        out_specs=(
            P(("dp", "col"), "row"),
            P(("dp", "col"), "row"),
            P("row", "col"),
            P("row", "col"),
            P("row", "col"),
            P("col", "row"),
            P("row", "col"),
            P("col", "row"),
            P(("col", "row")),
            P(("col", "row")),
            P("row"),
            P(("col", "row")),
            P("row"),
            P("row"),
            P("row"),
            P("row"),
            P("row"),
        ),
        check_vma=False,
    )
```

```python
import jax
import jax.numpy as jnp
from jax import lax
from jax.experimental import pallas as pl
from jax.experimental.pallas import tpu as pltpu
from jax.sharding import PartitionSpec as P

HEAD_DIM = 64
EPSILON = 1e-05
MASKED = -1e30
F32 = jnp.float32
BF16 = jnp.bfloat16
SWAP = ((0, 1), (1, 0))
CUBIC = 0.044715
ROOT = 0.7978845608028654
MIB = 1024 * 1024


def dot(left, right):
    return jnp.dot(left, right, preferred_element_type=F32)


def dot_nt(left, right):
    return lax.dot_general(left, right, (((1,), (1,)), ((), ())), preferred_element_type=F32)


def dot_tn(left, right):
    return lax.dot_general(left, right, (((0,), (0,)), ((), ())), preferred_element_type=F32)


def from_row(values):
    return lax.ppermute(values, "row", SWAP)


def from_col(values):
    return lax.ppermute(values, "col", SWAP)


def dp_pairs(bit):
    count = lax.axis_size("dp")
    return [(i, i ^ (1 << bit)) for i in range(count)]


def from_dp(values, bit):
    return lax.ppermute(values, "dp", dp_pairs(bit))


def hold(*values):
    return lax.optimization_barrier(values)


def shape(dims, kind):
    return jax.ShapeDtypeStruct(tuple(dims), kind)


def call(kernel, out_shape, *operands, flops=0, scratch=(), smem=(), vmem=16):
    spaces = [pltpu.SMEM if i in smem else pltpu.VMEM for i in range(len(operands))]
    moved = sum(x.size * x.dtype.itemsize for x in operands)
    return pl.pallas_call(
        kernel,
        out_shape=out_shape,
        in_specs=[pl.BlockSpec(memory_space=space) for space in spaces],
        scratch_shapes=list(scratch),
        compiler_params=pltpu.CompilerParams(vmem_limit_bytes=vmem * MIB),
        cost_estimate=pl.CostEstimate(flops=flops, bytes_accessed=moved, transcendentals=0),
    )(*operands)


def half_rows(index, size):
    return pl.ds(pl.multiple_of(index * size, size), size)


def pack_kernel(gain_a, shift_a, bias, gain_m, shift_m, w_q, w_k, w_v, b_q, b_v, b_u, b_d, vec, loc, kept, sent):
    vec[...] = jnp.zeros_like(vec)
    loc[...] = jnp.zeros_like(loc)
    for i, ref in enumerate((gain_a, shift_a, bias, gain_m, shift_m)):
        vec[i : i + 1] = ref[...].astype(F32).reshape(1, -1)
    third = w_q.shape[1] // 2
    loc[0:1, :third] = b_q[...].astype(F32).reshape(1, -1)
    loc[0:1, 2 * third : 3 * third] = b_v[...].astype(F32).reshape(1, -1)
    loc[1:2, : b_u.shape[0]] = b_u[...].astype(F32).reshape(1, -1)
    loc[2:3, : b_d.shape[0]] = b_d[...].astype(F32).reshape(1, -1)
    first = lax.axis_index("row") == 0
    keeps, sends = [], []
    for ref in (w_q, w_k, w_v):
        low, high = ref[:, :third], ref[:, third:]
        keeps.append(jnp.where(first, low, high))
        sends.append(jnp.where(first, high, low))
    kept[...] = jnp.concatenate(keeps, axis=1)
    sent[...] = jnp.concatenate(sends, axis=1)


def normed_parts(values):
    mean = jnp.mean(values, axis=1, keepdims=True)
    centered = values - mean
    variance = jnp.mean(centered * centered, axis=1, keepdims=True)
    inverse = lax.rsqrt(variance + EPSILON)
    return centered * inverse, inverse


def wide_vector(vec, vec_other, i):
    return jnp.concatenate([vec[i : i + 1], vec_other[i : i + 1]], axis=1)


def first_norm_kernel(tokens, tokens_other, vec, vec_other, normed, unit_out, inverse_out):
    values = jnp.concatenate([tokens[...], tokens_other[...]], axis=1).astype(F32)
    unit, inverse = normed_parts(values)
    gain, shift = wide_vector(vec, vec_other, 0), wide_vector(vec, vec_other, 1)
    normed[...] = (unit * gain + shift).astype(BF16)
    unit_out[...] = unit
    inverse_out[...] = jnp.broadcast_to(inverse, inverse_out.shape)


def head_mask(width, head):
    lanes = lax.broadcasted_iota(jnp.int32, (1, width), 1)
    return lanes // HEAD_DIM == head


def allowed_block(lengths, keys, first_query, count):
    first, second = lengths[0, 0], lengths[0, 0] + lengths[0, 1]
    query = first_query + lax.broadcasted_iota(jnp.int32, (1, count), 1)
    begin = jnp.where(query >= second, second, jnp.where(query >= first, first, 0))
    key = lax.broadcasted_iota(jnp.int32, (keys, count), 0)
    return (key >= begin) & (key <= query)


def forward_kernel(lengths, own, other, w_kept, w_got, loc, norm_out, q_out, k_out, v_out, o_out, lse):
    own_rows, width = own.shape
    half = width // 2
    third = q_out.shape[1]
    col = lax.axis_index("col")
    for ref, at in ((own, col), (other, 1 - col)):
        where = half_rows(at, own_rows)
        values = ref[...]
        norm_out[where] = values
        total = dot(values[:, :half], w_kept[...]) + dot(values[:, half:], w_got[...])
        total = (total + loc[0:1, : 3 * third]).astype(BF16)
        q_out[where] = total[:, :third]
        k_out[where] = total[:, third : 2 * third]
        v_out[where] = total[:, 2 * third :]
    lse[...] = jnp.zeros_like(lse)
    values_t = v_out[...].T
    for begin in (0, own_rows):
        keys = begin + own_rows
        allowed = allowed_block(lengths, keys, begin, own_rows)
        query = q_out[begin:keys] * BF16(HEAD_DIM ** (-0.5))
        parts = []
        for head in range(third // HEAD_DIM):
            key = jnp.where(head_mask(third, head), k_out[:keys], BF16(0))
            scores = jnp.where(allowed, dot_nt(key, query), MASKED)
            largest = jnp.max(scores, axis=0, keepdims=True)
            weights = jnp.exp(scores - largest)
            summed = jnp.sum(weights, axis=0, keepdims=True)
            lse[head : head + 1, begin:keys] = largest + jnp.log(summed)
            mixed = dot(
                values_t[head * HEAD_DIM : (head + 1) * HEAD_DIM, :keys], weights.astype(BF16)
            )
            parts.append(mixed / summed)
        o_out[begin:keys] = jnp.concatenate(parts, axis=0).T.astype(BF16)


def split_tokens(total_of, keep, send, own_rows, col):
    keep[...] = total_of(half_rows(col, own_rows))
    send[...] = total_of(half_rows(1 - col, own_rows)).astype(BF16)


def branch_kernel(mixed, mixed_other, w_mine, w_other, keep, send):
    row, col = lax.axis_index("row"), lax.axis_index("col")
    third = mixed.shape[1]
    own, far = half_rows(row, third), half_rows(1 - row, third)

    def total_of(rows):
        near_rows, far_rows = mixed[rows], mixed_other[rows]
        return jnp.concatenate(
            [dot(near_rows, w[own]) + dot(far_rows, w[far]) for w in (w_mine, w_other)], axis=1
        )

    split_tokens(total_of, keep, send, keep.shape[0], col)


def second_norm_kernel(tokens, tokens_other, keep, got, vec, vec_other, middle, normed, unit_out, inverse_out):
    values = jnp.concatenate([tokens[...], tokens_other[...]], axis=1).astype(F32)
    values = values + (keep[...] + got[...].astype(F32) + wide_vector(vec, vec_other, 2))
    middle[...] = values[:, : middle.shape[1]]
    unit, inverse = normed_parts(values)
    gain, shift = wide_vector(vec, vec_other, 3), wide_vector(vec, vec_other, 4)
    normed[...] = (unit * gain + shift).astype(BF16)
    unit_out[...] = unit
    inverse_out[...] = jnp.broadcast_to(inverse, inverse_out.shape)


def both_sides(got, got_side, axis):
    first = lax.axis_index("dp") % 2 == 0
    low = jnp.where(first, got[...], got_side[...])
    high = jnp.where(first, got_side[...], got[...])
    return jnp.concatenate([low, high], axis=axis)


def up_kernel(own, other, w_up, got, got_side, loc, norm_out, hidden_out, slope_out, w_other_out):
    own_rows, width = own.shape
    half = width // 2
    units = got.shape[1]
    row, col = lax.axis_index("row"), lax.axis_index("col")
    w_mine = w_up[:, pl.ds(pl.multiple_of(row * units, units), units)]
    w_other = both_sides(got, got_side, 0)
    w_other_out[...] = w_other
    for ref, at in ((own, col), (other, 1 - col)):
        where = half_rows(at, own_rows)
        values = ref[...]
        norm_out[where] = values
        u = dot(values[:, :half], w_mine) + dot(values[:, half:], w_other) + loc[1:2, :units]
        squared = u * u
        bent = jnp.tanh(ROOT * (u + CUBIC * (squared * u)))
        raised = 0.5 * (1.0 + bent)
        hidden_out[where] = (u * raised).astype(BF16)
        slope_out[where] = raised + 0.5 * u * (1.0 - bent * bent) * (
            ROOT * (1.0 + (3.0 * CUBIC) * squared)
        )


def split_rows(total, keep, send, bit):
    own = (lax.axis_index("dp") // (1 << bit)) % 2 == 0
    half = keep.shape[-2]
    low, high = total[..., :half, :], total[..., half:, :]
    keep[...] = jnp.where(own, low, high)
    send[...] = jnp.where(own, high, low)


def masked_top(lengths, mine, far, at):
    live = lengths[0, 0] + lengths[0, 1]
    own_rows = mine.shape[0]
    position = at * own_rows + lax.broadcasted_iota(jnp.int32, (own_rows, 1), 0)
    values = jnp.concatenate([mine[...], far[...]], axis=1)
    return jnp.where(position < live, values, BF16(0))


def down_kernel(bit_down, bit_up, lengths, top, top_far, top_col, top_far_col, hidden, slope, normed, w_down, got, got_side,
                w_up, w_up_other, down_keep, down_send, up_keep, up_send, keep, send, sums, w_other_out, top_all, grad_pre):
    own_rows, half = top.shape
    units = hidden.shape[1]
    row, col = lax.axis_index("row"), lax.axis_index("col")
    top_all[half_rows(col, own_rows)] = masked_top(lengths, top, top_far, col)
    top_all[half_rows(1 - col, own_rows)] = masked_top(lengths, top_col, top_far_col, 1 - col)
    top_rows = top_all[...]
    split_rows(dot_tn(hidden[...], top_rows).astype(BF16), down_keep, down_send, bit_down)
    w_other = both_sides(got, got_side, 0)
    w_other_out[...] = w_other
    grad_hidden = dot_nt(top_rows[:, :half], w_down[half_rows(row, units)]) + dot_nt(
        top_rows[:, half:], w_other
    )
    grads = (grad_hidden * slope[...]).astype(BF16)
    grad_pre[...] = grads
    w_mine = w_up[:, pl.ds(pl.multiple_of(row * units, units), units)]

    def total_of(rows):
        values = grad_pre[rows]
        return jnp.concatenate([dot_nt(values, w_mine), dot_nt(values, w_up_other[...])], axis=1)

    split_tokens(total_of, keep, send, own_rows, col)
    total = dot_tn(normed[...], grads).astype(BF16)
    split_rows(total.reshape(2, half, units), up_keep, up_send, bit_up)
    sums[...] = jnp.zeros_like(sums)
    sums[0:1] = jnp.sum(grads.astype(F32), axis=0, keepdims=True)
    sums[1:2, :half] = jnp.sum(top_rows[:, :half].astype(F32), axis=0, keepdims=True)


def output_kernel(hidden, w_down, w_other, keep, send):
    units = hidden.shape[1]
    row, col = lax.axis_index("row"), lax.axis_index("col")
    w_mine = w_down[half_rows(row, units)]

    def total_of(rows):
        values = hidden[rows]
        return jnp.concatenate([dot(values, w_mine), dot(values, w_other[...])], axis=1)

    split_tokens(total_of, keep, send, keep.shape[0], col)


def second_back_kernel(lengths, total, total_far, unit_ref, inverse_ref, vec, vec_other, top, top_far, middle_out, datt, sums):
    half = top.shape[1]
    got = total_far[...].astype(F32)
    grads = total[...].astype(F32) + jnp.concatenate([got[:, half:], got[:, :half]], axis=1)
    unit = unit_ref[...]
    scaled = grads * wide_vector(vec, vec_other, 3)
    mean_plain = jnp.mean(scaled, axis=1, keepdims=True)
    mean_unit = jnp.mean(scaled * unit, axis=1, keepdims=True)
    own = masked_top(lengths, top, top_far, lax.axis_index("col")).astype(F32)
    result = own + inverse_ref[:, :1] * (scaled - mean_plain - unit * mean_unit)
    middle_out[...] = result[:, :half]
    datt[...] = result.astype(BF16)
    sums[...] = jnp.zeros_like(sums)
    sums[0:1] = jnp.sum((grads * unit)[:, :half], axis=0, keepdims=True)
    sums[1:2] = jnp.sum(grads[:, :half], axis=0, keepdims=True)


def backward_kernel(bit_first, bit_second, lengths, own, other, w_mine, w_other, q_ref, k_ref, v_ref, o_ref, lse, normed, w_kept, w_got,
                    first_keep, first_send, second_keep, second_send, keep, send, sums, datt, out, acc_k, acc_v, do_ref):
    own_rows, width = own.shape
    half = width // 2
    third = q_ref.shape[1]
    row, col = lax.axis_index("row"), lax.axis_index("col")
    quarter = half_rows(row, third)
    for ref, at in ((own, col), (other, 1 - col)):
        where = half_rows(at, own_rows)
        values = ref[...]
        datt[where] = values
        do_ref[where] = (
            dot_nt(values[:, :half], w_mine[quarter]) + dot_nt(values[:, half:], w_other[quarter])
        ).astype(BF16)
    keys_t = k_ref[...].T
    acc_k[...] = jnp.zeros_like(acc_k)
    acc_v[...] = jnp.zeros_like(acc_v)
    scale = BF16(HEAD_DIM ** (-0.5))
    for begin in (0, own_rows):
        keys = begin + own_rows
        allowed = allowed_block(lengths, keys, begin, own_rows)
        query = q_ref[begin:keys] * scale
        grad_mixed = do_ref[begin:keys]
        parts = []
        for head in range(third // HEAD_DIM):
            mask = head_mask(third, head)
            key = jnp.where(mask, k_ref[:keys], BF16(0))
            scores = jnp.where(allowed, dot_nt(key, query), MASKED)
            probs = jnp.exp(scores - lse[head : head + 1, begin:keys])
            value = jnp.where(mask, v_ref[:keys], BF16(0))
            grad_probs = dot_nt(value, grad_mixed)
            both = probs * grad_probs
            inner = jnp.sum(both, axis=0, keepdims=True)
            grad_raw = (both - probs * inner).astype(BF16) * scale
            acc_v[:keys] += jnp.where(mask, dot(probs.astype(BF16), grad_mixed), 0.0)
            acc_k[:keys] += jnp.where(mask, dot(grad_raw, q_ref[begin:keys]), 0.0)
            parts.append(dot(keys_t[head * HEAD_DIM : (head + 1) * HEAD_DIM, :keys], grad_raw))
        out[begin:keys, :third] = jnp.concatenate(parts, axis=0).T.astype(BF16)
    out[:, third : 2 * third] = acc_k[...].astype(BF16)
    out[:, 2 * third :] = acc_v[...].astype(BF16)
    grads = out[...]
    weights = dot_tn(normed[...], grads).astype(BF16)
    grad_out = dot_tn(datt[...], o_ref[...]).astype(BF16)
    split_rows(weights[:, : 2 * third].reshape(2, half, 2 * third), first_keep, first_send, bit_first)
    last = jnp.concatenate([weights[:, 2 * third :], grad_out], axis=1)
    split_rows(last.reshape(2, half, 2 * third), second_keep, second_send, bit_second)

    def total_of(rows):
        values = out[rows]
        return jnp.concatenate([dot_nt(values, w_kept[...]), dot_nt(values, w_got[...])], axis=1)

    split_tokens(total_of, keep, send, own_rows, col)
    sums[...] = jnp.zeros_like(sums)
    sums[0:1, : 3 * third] = jnp.sum(grads.astype(F32), axis=0, keepdims=True)
    sums[1:2, :half] = jnp.sum(datt[:, :half].astype(F32), axis=0, keepdims=True)


def first_back_kernel(keep, got, unit_ref, vec, vec_other, mine, far, stats):
    half = mine.shape[1]
    grads = keep[...] + got[...].astype(F32)
    mine[...] = grads[:, :half]
    far[...] = grads[:, half:].astype(BF16)
    scaled = grads * wide_vector(vec, vec_other, 0)
    plain = jnp.sum(scaled, axis=1, keepdims=True)
    crossed = jnp.sum(scaled * unit_ref[...], axis=1, keepdims=True)
    lanes = lax.broadcasted_iota(jnp.int32, (1, 128), 1)
    both = jnp.where(lanes == 0, plain, jnp.where(lanes == 1, crossed, 0.0))
    stats[...] = both.T[:8]


def last_kernel(mine, got, stats, stats_far, unit_ref, inverse_ref, vec, middle, result, sums):
    half = mine.shape[1]
    unit = unit_ref[:, :half]
    grads = mine[...] + got[...].astype(F32)
    total = (stats[...] + stats_far[...]) / (2 * half)
    columns = jnp.concatenate([total, jnp.zeros((120, total.shape[1]), F32)], axis=0).T
    grad_in = inverse_ref[:, :1] * (
        grads * vec[0:1] - columns[:, 0:1] - unit * columns[:, 1:2]
    )
    result[...] = (middle[...] + grad_in).astype(BF16)
    sums[...] = jnp.zeros_like(sums)
    sums[0:1] = jnp.sum(grads * unit, axis=0, keepdims=True)
    sums[1:2] = jnp.sum(grads, axis=0, keepdims=True)


def halve_kernel(bit, kept, got, keep, send):
    total = (kept[...].astype(F32) + got[...].astype(F32)).astype(BF16)
    split_rows(total, keep, send, bit)


def turn_kernel(stacked, kept, got, keep, send):
    total = (kept[...].astype(F32) + got[...].astype(F32)).astype(BF16)
    if stacked:
        keep[...], send[...] = total[0], total[1]
    else:
        half = keep.shape[1]
        keep[...], send[...] = total[:, :half], total[:, half:]


def stack_kernel(mine, got, out):
    out[0], out[1] = mine[...], got[...]


def double_kernel(bit, mine, got, out):
    own = (lax.axis_index("dp") // (1 << bit)) % 2 == 0
    half = mine.shape[1]
    out[:, :half] = jnp.where(own, mine[...], got[...])
    out[:, half:] = jnp.where(own, got[...], mine[...])


class Chain:
    def __init__(self, keep, send, bits, stacked):
        self.keep, self.bits, self.stacked = keep, bits, stacked
        self.stage = 0
        self.steps = 2 * len(bits) + 1
        self.got = from_dp(send, bits[0])

    def step(self):
        self.stage += 1
        count, stage = len(self.bits), self.stage
        if stage < count:
            bit = self.bits[stage]
            dims = self.keep.shape[:-2] + (self.keep.shape[-2] // 2, self.keep.shape[-1])
            self.keep, send = call(
                lambda *refs: halve_kernel(bit, *refs), (shape(dims, BF16),) * 2, self.keep, self.got
            )
            self.got = from_dp(send, bit)
        elif stage == count:
            rows, width = self.keep.shape[-2:]
            dims = (rows, width) if self.stacked else (rows, width // 2)
            stacked = self.stacked
            self.keep, send = call(
                lambda *refs: turn_kernel(stacked, *refs),
                (shape(dims, BF16),) * 2,
                self.keep,
                self.got,
            )
            self.got = from_row(send)
        elif stage < self.steps:
            self.gather()
            self.got = from_dp(self.keep, self.bits[2 * count - stage])

    def gather(self):
        count, stage = len(self.bits), self.stage
        if stage == count + 1:
            dims = (2,) + self.keep.shape
            self.keep = call(stack_kernel, shape(dims, BF16), self.keep, self.got)
        else:
            bit = self.bits[2 * count - stage + 1]
            pair, rows, width = self.keep.shape
            self.keep = call(
                lambda *refs: double_kernel(bit, *refs),
                shape((pair, 2 * rows, width), BF16),
                self.keep,
                self.got,
            )

    @property
    def last_bit(self):
        return self.bits[0]


def arrived(chains, *others):
    flat = [(chain.keep, chain.got) for chain in chains]
    flat, others = lax.optimization_barrier((flat, others))
    for chain, (keep, got) in zip(chains, flat):
        chain.keep, chain.got = keep, got
    return others


def advance(chains):
    for chain in chains:
        chain.step()


def ordered_halves(bit, mine, got):
    own = (lax.axis_index("dp") // (1 << bit)) % 2 == 0
    return jnp.concatenate(
        [jnp.where(own, mine, got), jnp.where(own, got, mine)], axis=0
    )


def by_row(mine, far, axis):
    first = lax.axis_index("row") == 0
    return jnp.concatenate(
        [jnp.where(first, mine, far), jnp.where(first, far, mine)], axis=axis
    )


def up_end_kernel(bit, mine, got, out):
    own = (lax.axis_index("dp") // (1 << bit)) % 2
    here = pl.program_id(0) == own
    near = jnp.where(here, mine[0], got[0])
    far = jnp.where(here, mine[1], got[1])
    out[...] = by_row(near, far, 1).astype(F32)


def down_end_kernel(bit, mine, got, out):
    own = (lax.axis_index("dp") // (1 << bit)) % 2
    here = pl.program_id(1) == own
    near = pl.program_id(0) == lax.axis_index("row")
    part = jnp.where(near, jnp.where(here, mine[0], got[0]), jnp.where(here, mine[1], got[1]))
    out[...] = part.astype(F32)


def attention_end_kernel(bit, flip, mine, got, left, right):
    near = ordered_halves(bit, mine[0], got[0])
    far = ordered_halves(bit, mine[1], got[1])
    third = near.shape[1] // 2
    left[...] = by_row(near[:, :third], far[:, :third], 1).astype(F32)
    last = by_row(near[:, third:], far[:, third:], 1).astype(F32)
    right[...] = last.T if flip else last


def end_call(kernel, grid, out_shape, block, index, mine, got):
    whole = pl.BlockSpec(memory_space=pltpu.VMEM)
    return pl.pallas_call(
        kernel,
        grid=grid,
        out_shape=out_shape,
        in_specs=[whole, whole],
        out_specs=pl.BlockSpec(block, index),
        compiler_params=pltpu.CompilerParams(vmem_limit_bytes=16 * MIB),
    )(mine, got)


def body(
    tokens,
    out_grad,
    seq_lengths,
    w_query,
    w_key,
    w_value,
    w_out,
    w_up,
    w_down,
    b_query,
    b_value,
    b_out,
    b_up,
    b_down,
    gain_attn,
    shift_attn,
    gain_mlp,
    shift_mlp,
):
    row = lax.axis_index("row")
    own_rows, half = tokens.shape
    width = 2 * half
    rows = 2 * own_rows
    third = w_query.shape[1] // 2
    units = w_up.shape[1] // 2
    side = lax.axis_index("dp") % 2
    count = lax.axis_size("dp").bit_length() - 1
    bits = list(range(count))
    turned = [1, 0] + bits[2:] if count > 1 else bits
    tall = shape((own_rows, width), F32)
    tall_low = shape((own_rows, width), BF16)
    column = shape((own_rows, 128), F32)
    pair_sums = shape((8, half), F32)

    tokens_far = from_row(tokens)
    operands = (
        gain_attn, shift_attn, b_out, gain_mlp, shift_mlp, w_query, w_key, w_value,
        b_query, b_value, b_up, b_down,
    )
    out_shape = (
        shape((8, half), F32),
        shape((8, units), F32),
        shape((half, 3 * third), BF16),
        shape((half, 3 * third), BF16),
    )
    whole = lambda x: pl.BlockSpec(x.shape, lambda i: (0,) * len(x.shape))
    vec, loc, w_kept, sent = pl.pallas_call(
        pack_kernel,
        grid=(1,),
        out_shape=out_shape,
        in_specs=[whole(x) for x in operands],
        out_specs=tuple(pl.BlockSpec(memory_space=pltpu.VMEM) for _ in out_shape),
        compiler_params=pltpu.CompilerParams(vmem_limit_bytes=16 * MIB),
    )(*operands)
    vec_far = from_row(vec)
    w_got = from_row(sent)
    top_col = from_col(out_grad)
    sent_up = lax.dynamic_slice(
        w_up, (side * (half // 2), (1 - row) * units), (half // 2, units)
    )
    sent_down = lax.dynamic_slice(
        w_down, ((1 - row) * units + side * (units // 2), 0), (units // 2, half)
    )
    tokens_far, vec_far, w_out_send, sent_up = hold(tokens_far, vec_far, w_out, sent_up)

    normed, unit_attn, inverse_attn = call(
        first_norm_kernel, (tall_low, tall, column), tokens, tokens_far, vec, vec_far
    )
    normed_col = from_col(normed)
    w_out_far = from_row(w_out_send)
    up_got = from_row(sent_up)
    normed_col, w_got = hold(normed_col, w_got)

    like = shape((rows, third), BF16)
    normed_all, query, key, value, mixed, lse = call(
        forward_kernel,
        (shape((rows, width), BF16), like, like, like, like, shape((8, rows), F32)),
        seq_lengths,
        normed,
        normed_col,
        w_kept,
        w_got,
        loc,
        flops=2 * rows * third * (3 * width + 2 * rows),
        smem=(0,),
    )
    mixed_far = from_row(mixed)
    mixed_far, w_out_far, out_grad_send, sent_down, up_got = hold(
        mixed_far, w_out_far, out_grad, sent_down, up_got
    )

    keep, send = call(
        branch_kernel, (tall, tall_low), mixed, mixed_far, w_out, w_out_far,
        flops=2 * rows * width * half,
    )
    got = from_col(send)
    up_side = from_dp(up_got, 0)
    top_far = from_row(out_grad_send)
    down_got = from_row(sent_down)
    (got,) = hold(got)

    middle, normed_mlp, unit_mlp, inverse_mlp = call(
        second_norm_kernel,
        (shape((own_rows, half), F32), tall_low, tall, column),
        tokens, tokens_far, keep, got, vec, vec_far,
    )
    normed_mlp_col = from_col(normed_mlp)
    normed_mlp_col, up_side, top_far = hold(normed_mlp_col, up_side, top_far)

    normed_mlp_all, hidden, slope, w_up_far = call(
        up_kernel,
        (
            shape((rows, width), BF16),
            shape((rows, units), BF16),
            shape((rows, units), F32),
            shape((half, units), BF16),
        ),
        normed_mlp, normed_mlp_col, w_up, up_got, up_side, loc,
        flops=2 * rows * width * units,
    )
    top_far_col = from_col(top_far)
    down_side = from_dp(down_got, 0)
    hidden, top_far_col, down_side = hold(hidden, top_far_col, down_side)

    split_down = shape((units // 2, width), BF16)
    split_up = shape((2, half // 2, units), BF16)
    down_keep, down_send, up_keep, up_send, keep, send, mlp_sums, w_down_far = call(
        lambda *refs: down_kernel(bits[0], turned[0], *refs),
        (
            split_down, split_down, split_up, split_up, tall, tall_low,
            shape((8, units), F32), shape((units, half), BF16),
        ),
        seq_lengths, out_grad, top_far, top_col, top_far_col, hidden, slope, normed_mlp_all,
        w_down, down_got, down_side, w_up, w_up_far,
        flops=8 * rows * width * units,
        scratch=[pltpu.VMEM((rows, width), BF16), pltpu.VMEM((rows, units), BF16)],
        smem=(0,),
    )
    got = from_col(send)
    down = Chain(down_keep, down_send, bits, False)
    up = Chain(up_keep, up_send, turned, True)
    (got,) = hold(got)

    total = (keep + got.astype(F32)).astype(BF16)
    total_far = from_row(total)
    keep, send = call(
        output_kernel, (tall, tall_low), hidden, w_down, w_down_far,
        flops=2 * rows * width * units,
    )
    got = from_col(send)
    total_far, got = hold(total_far, got)

    grad_middle, datt, mid_sums = call(
        second_back_kernel,
        (shape((own_rows, half), F32), tall_low, pair_sums),
        seq_lengths, total, total_far, unit_mlp, inverse_mlp, vec, vec_far, out_grad, top_far,
        smem=(0,),
    )
    datt_col = from_col(datt)
    raised = keep + got.astype(F32)
    raised_far = from_row(raised[:, half:].astype(BF16))
    (datt_col,) = arrived([down, up], datt_col)
    advance([down, up])

    split_pair = shape((2, half // 2, 2 * third), BF16)
    first_keep, first_send, second_keep, second_send, keep, send, attn_sums = call(
        lambda *refs: backward_kernel(bits[0], turned[0], *refs),
        (split_pair,) * 4 + (tall, tall_low, shape((8, width), F32)),
        seq_lengths, datt, datt_col, w_out, w_out_far, query, key, value, mixed, lse,
        normed_all, w_kept, w_got,
        flops=2 * rows * third * (5 * width + 5 * rows),
        scratch=[
            pltpu.VMEM((rows, width), BF16),
            pltpu.VMEM((rows, 3 * third), BF16),
            pltpu.VMEM((rows, third), F32),
            pltpu.VMEM((rows, third), F32),
            pltpu.VMEM((rows, third), BF16),
        ],
        smem=(0,),
    )
    keep, send, raised_far = arrived([down, up], keep, send, raised_far)
    got = from_col(send)
    first = Chain(first_keep, first_send, bits, True)
    second = Chain(second_keep, second_send, turned, True)
    advance([down, up])
    output = (middle + raised[:, :half] + raised_far.astype(F32) + loc[2:3, :half]).astype(BF16)
    (got,) = hold(got)

    mine, far, stats = call(
        first_back_kernel,
        (shape((own_rows, half), F32), shape((own_rows, half), BF16), shape((8, own_rows), F32)),
        keep, got, unit_attn, vec, vec_far,
    )
    got = from_row(far)
    stats_far = from_row(stats)
    got, stats_far = arrived([down, up, first, second], got, stats_far)
    advance([down, up, first, second])
    input_grad, in_sums = call(
        last_kernel,
        (shape((own_rows, half), BF16), pair_sums),
        mine, got, stats, stats_far, unit_attn, inverse_attn, vec, grad_middle,
    )

    halves = jnp.concatenate([in_sums, mid_sums], axis=1)
    halves = halves + from_col(halves)
    small = jnp.concatenate(
        [halves[:2], mlp_sums[:2, :width], attn_sums[:2], jnp.zeros((2, width), F32)]
    )
    for bit in bits:
        (small,) = arrived([down, up, first, second], small)
        if first.stage < first.steps - 1:
            advance([down, up, first, second])
        small = small + from_dp(small, bit)
    for chain in (first, second):
        while chain.stage < chain.steps - 1:
            chain.step()
    for chain in (down, up):
        while chain.stage < chain.steps - 1:
            chain.step()

    wide = w_query.shape[1]
    outs = (shape((half, wide), F32),) * 2
    grad_query, grad_key = call(
        lambda *refs: attention_end_kernel(first.last_bit, False, *refs), outs, first.keep, first.got
    )
    grad_value, grad_out = call(
        lambda *refs: attention_end_kernel(second.last_bit, True, *refs), outs, second.keep, second.got
    )
    grad_down = end_call(
        lambda *refs: down_end_kernel(down.last_bit, *refs),
        (2, 2),
        shape((2 * units, half), F32),
        (units // 2, half),
        lambda i, j: (2 * i + j, 0),
        down.keep,
        down.got,
    )
    grad_up = end_call(
        lambda *refs: up_end_kernel(up.last_bit, *refs),
        (2,),
        shape((half, 2 * units), F32),
        (half // 2, 2 * units),
        lambda i: (i, 0),
        up.keep,
        up.got,
    )
    return (
        output,
        input_grad,
        grad_query,
        grad_key,
        grad_value,
        grad_out,
        grad_up,
        grad_down,
        small[4, :third],
        small[4, 2 * third : 3 * third],
        small[5, :half],
        small[2, :units],
        small[3, :half],
        small[0, :half],
        small[1, :half],
        small[0, half:],
        small[1, half:],
    )


def solution(mesh):
    return jax.shard_map(
        body,
        mesh=mesh,
        in_specs=(
            P(("dp", "col"), "row"),
            P(("dp", "col"), "row"),
            P("dp", None),
            P("row", "col"),
            P("row", "col"),
            P("row", "col"),
            P("col", "row"),
            P("row", "col"),
            P("col", "row"),
            P(("col", "row")),
            P(("col", "row")),
            P("row"),
            P(("col", "row")),
            P("row"),
            P("row"),
            P("row"),
            P("row"),
            P("row"),
        ),
        out_specs=(
            P(("dp", "col"), "row"),
            P(("dp", "col"), "row"),
            P("row", "col"),
            P("row", "col"),
            P("row", "col"),
            P("col", "row"),
            P("row", "col"),
            P("col", "row"),
            P(("col", "row")),
            P(("col", "row")),
            P("row"),
            P(("col", "row")),
            P("row"),
            P("row"),
            P("row"),
            P("row"),
            P("row"),
        ),
        check_vma=False,
    )
```

```python
import jax
import jax.numpy as jnp
from jax import lax
from jax.experimental import pallas as pl
from jax.experimental.pallas import tpu as pltpu
from jax.sharding import PartitionSpec as P

HEAD_DIM = 64
EPSILON = 1e-05
MASKED = -1e30
F32 = jnp.float32
BF16 = jnp.bfloat16
SWAP = ((0, 1), (1, 0))
CUBIC = 0.044715
ROOT = 0.7978845608028654
MIB = 1024 * 1024


def dot(left, right):
    return jnp.dot(left, right, preferred_element_type=F32)


def dot_nt(left, right):
    return lax.dot_general(left, right, (((1,), (1,)), ((), ())), preferred_element_type=F32)


def dot_tn(left, right):
    return lax.dot_general(left, right, (((0,), (0,)), ((), ())), preferred_element_type=F32)


def from_row(values):
    return lax.ppermute(values, "row", SWAP)


def from_col(values):
    return lax.ppermute(values, "col", SWAP)


def dp_pairs(bit):
    count = lax.axis_size("dp")
    return [(i, i ^ (1 << bit)) for i in range(count)]


def from_dp(values, bit):
    return lax.ppermute(values, "dp", dp_pairs(bit))


def hold(*values):
    return lax.optimization_barrier(values)


def shape(dims, kind):
    return jax.ShapeDtypeStruct(tuple(dims), kind)


def call(kernel, out_shape, *operands, scratch=(), smem=(), hbm=(), hbm_out=(), vmem=16):
    spaces = [
        pltpu.SMEM if i in smem else pltpu.HBM if i in hbm else pltpu.VMEM
        for i in range(len(operands))
    ]
    out_specs = jax.tree.map(lambda _: pl.BlockSpec(memory_space=pltpu.VMEM), out_shape)
    if hbm_out:
        out_specs = tuple(
            pl.BlockSpec(memory_space=pltpu.HBM if i in hbm_out else pltpu.VMEM)
            for i in range(len(out_shape))
        )
    return pl.pallas_call(
        kernel,
        out_shape=out_shape,
        in_specs=[pl.BlockSpec(memory_space=space) for space in spaces],
        out_specs=out_specs,
        scratch_shapes=list(scratch),
        compiler_params=pltpu.CompilerParams(vmem_limit_bytes=vmem * MIB),
        cost_estimate=pl.CostEstimate(flops=0, bytes_accessed=0, transcendentals=0),
    )(*operands)


def half_rows(index, size):
    return pl.ds(pl.multiple_of(index * size, size), size)


def start_copies(pairs, sems):
    copies = [
        pltpu.make_async_copy(source, target, sems.at[i]) for i, (source, target) in enumerate(pairs)
    ]
    for copy in copies:
        copy.start()
    return copies


def vector_kernel(*refs):
    sources, (vec, loc), held, sems = refs[:9], refs[9:11], refs[11:20], refs[20]
    for copy in start_copies(list(zip(sources, held)), sems):
        copy.wait()
    vec[...] = jnp.zeros_like(vec)
    loc[...] = jnp.zeros_like(loc)
    for i, ref in enumerate(held[:5]):
        vec[i : i + 1] = ref[...].astype(F32).reshape(1, -1)
    b_q, b_v, b_u, b_d = held[5:]
    third = b_q.shape[0]
    loc[0:1, :third] = b_q[...].astype(F32).reshape(1, -1)
    loc[0:1, 2 * third : 3 * third] = b_v[...].astype(F32).reshape(1, -1)
    loc[1:2, : b_u.shape[0]] = b_u[...].astype(F32).reshape(1, -1)
    loc[2:3, : b_d.shape[0]] = b_d[...].astype(F32).reshape(1, -1)


def pack_kernel(w_q, w_k, w_v, w_out, w_up, w_down, loc, kept, sent, out_sent, up_sent, down_sent,
                held_q, held_k, held_v, sems):
    row, side = lax.axis_index("row"), lax.axis_index("dp") % 2
    units = up_sent.shape[1]
    sent_rows = sent.shape[0]
    out_rows, up_rows, down_rows = out_sent.shape[0], up_sent.shape[0], down_sent.shape[0]
    copies = start_copies(
        [
            (w_q, held_q),
            (w_k, held_k),
            (w_v, held_v),
            (w_out.at[half_rows(side, out_rows)], out_sent),
            (w_up.at[half_rows(side, up_rows), half_rows(1 - row, units)], up_sent),
            (w_down.at[half_rows(2 * (1 - row) + side, down_rows)], down_sent),
        ],
        sems,
    )
    first = row == 0
    third = w_q.shape[1] // 2
    keeps, sends = [], []
    for ref, copy in zip((held_q, held_k, held_v), copies):
        copy.wait()
        low, high = ref[:, :third], ref[:, third:]
        keeps.append(jnp.where(first, low, high))
        sends.append(jnp.where(first, high, low))
    kept[...] = jnp.concatenate(keeps, axis=1)
    whole = jnp.concatenate(sends, axis=1)
    sent[...] = jnp.where(side == 0, whole[:sent_rows], whole[sent_rows:])
    for copy in copies[3:]:
        copy.wait()


def normed_parts(values):
    mean = jnp.mean(values, axis=1, keepdims=True)
    centered = values - mean
    variance = jnp.mean(centered * centered, axis=1, keepdims=True)
    inverse = lax.rsqrt(variance + EPSILON)
    return centered * inverse, inverse


def wide_vector(vec, vec_other, i):
    return jnp.concatenate([vec[i : i + 1], vec_other[i : i + 1]], axis=1)


def first_norm_kernel(tokens, tokens_other, vec, vec_other, normed, unit_out, inverse_out):
    values = jnp.concatenate([tokens[...], tokens_other[...]], axis=1).astype(F32)
    unit, inverse = normed_parts(values)
    gain, shift = wide_vector(vec, vec_other, 0), wide_vector(vec, vec_other, 1)
    normed[...] = (unit * gain + shift).astype(BF16)
    unit_out[...] = unit
    inverse_out[...] = jnp.broadcast_to(inverse, inverse_out.shape)


def head_mask(width, head):
    lanes = lax.broadcasted_iota(jnp.int32, (1, width), 1)
    return lanes // HEAD_DIM == head


def allowed_block(lengths, keys, first_query, count):
    first, second = lengths[0, 0], lengths[0, 0] + lengths[0, 1]
    query = first_query + lax.broadcasted_iota(jnp.int32, (1, count), 1)
    begin = jnp.where(query >= second, second, jnp.where(query >= first, first, 0))
    key = lax.broadcasted_iota(jnp.int32, (keys, count), 0)
    return (key >= begin) & (key <= query)


def forward_kernel(lengths, own, other, w_kept, got, got_side, loc, norm_hbm, q_hbm, k_hbm, v_hbm, o_out, lse,
                   norm_out, q_out, k_out, v_out, sems):
    own_rows, width = own.shape
    half = width // 2
    third = q_out.shape[1]
    col = lax.axis_index("col")
    w_got = both_sides(got, got_side, 0)
    for ref, at in ((own, col), (other, 1 - col)):
        where = half_rows(at, own_rows)
        values = ref[...]
        norm_out[where] = values
        total = dot(values[:, :half], w_kept[...]) + dot(values[:, half:], w_got)
        total = (total + loc[0:1, : 3 * third]).astype(BF16)
        q_out[where] = total[:, :third]
        k_out[where] = total[:, third : 2 * third]
        v_out[where] = total[:, 2 * third :]
    copies = start_copies(
        [(norm_out, norm_hbm), (q_out, q_hbm), (k_out, k_hbm), (v_out, v_hbm)], sems
    )
    lse[...] = jnp.zeros_like(lse)
    values_t = v_out[...].T
    for begin in (0, own_rows):
        keys = begin + own_rows
        allowed = allowed_block(lengths, keys, begin, own_rows)
        query = q_out[begin:keys] * BF16(HEAD_DIM ** (-0.5))
        parts = []
        for head in range(third // HEAD_DIM):
            key = jnp.where(head_mask(third, head), k_out[:keys], BF16(0))
            scores = jnp.where(allowed, dot_nt(key, query), MASKED)
            largest = jnp.max(scores, axis=0, keepdims=True)
            weights = jnp.exp(scores - largest)
            summed = jnp.sum(weights, axis=0, keepdims=True)
            lse[head : head + 1, begin:keys] = largest + jnp.log(summed)
            mixed = dot(
                values_t[head * HEAD_DIM : (head + 1) * HEAD_DIM, :keys], weights.astype(BF16)
            )
            parts.append(mixed / summed)
        o_out[begin:keys] = jnp.concatenate(parts, axis=0).T.astype(BF16)
    for copy in copies:
        copy.wait()


def split_tokens(total_of, keep, send, own_rows, col):
    keep[...] = total_of(half_rows(col, own_rows))
    send[...] = total_of(half_rows(1 - col, own_rows)).astype(BF16)


def branch_kernel(mixed, mixed_other, w_mine, got, got_side, keep, send, w_other):
    w_other[...] = both_sides(got, got_side, 0)
    row, col = lax.axis_index("row"), lax.axis_index("col")
    third = mixed.shape[1]
    own, far = half_rows(row, third), half_rows(1 - row, third)

    def total_of(rows):
        near_rows, far_rows = mixed[rows], mixed_other[rows]
        return jnp.concatenate(
            [dot(near_rows, w[own]) + dot(far_rows, w[far]) for w in (w_mine, w_other)], axis=1
        )

    split_tokens(total_of, keep, send, keep.shape[0], col)


def second_norm_kernel(tokens, tokens_other, keep, got, vec, vec_other, middle, normed, unit_out, inverse_out):
    values = jnp.concatenate([tokens[...], tokens_other[...]], axis=1).astype(F32)
    values = values + (keep[...] + got[...].astype(F32) + wide_vector(vec, vec_other, 2))
    middle[...] = values[:, : middle.shape[1]]
    unit, inverse = normed_parts(values)
    gain, shift = wide_vector(vec, vec_other, 3), wide_vector(vec, vec_other, 4)
    normed[...] = (unit * gain + shift).astype(BF16)
    unit_out[...] = unit
    inverse_out[...] = jnp.broadcast_to(inverse, inverse_out.shape)


def both_sides(got, got_side, axis):
    first = lax.axis_index("dp") % 2 == 0
    low = jnp.where(first, got[...], got_side[...])
    high = jnp.where(first, got_side[...], got[...])
    return jnp.concatenate([low, high], axis=axis)


def up_kernel(own, other, w_up, got, got_side, loc, norm_out, hidden_out, slope_out, w_other_out):
    own_rows, width = own.shape
    half = width // 2
    units = got.shape[1]
    row, col = lax.axis_index("row"), lax.axis_index("col")
    w_mine = w_up[:, pl.ds(pl.multiple_of(row * units, units), units)]
    w_other = both_sides(got, got_side, 0)
    w_other_out[...] = w_other
    for ref, at in ((own, col), (other, 1 - col)):
        where = half_rows(at, own_rows)
        values = ref[...]
        norm_out[where] = values
        u = dot(values[:, :half], w_mine) + dot(values[:, half:], w_other) + loc[1:2, :units]
        squared = u * u
        bent = jnp.tanh(ROOT * (u + CUBIC * (squared * u)))
        raised = 0.5 * (1.0 + bent)
        hidden_out[where] = (u * raised).astype(BF16)
        slope_out[where] = raised + 0.5 * u * (1.0 - bent * bent) * (
            ROOT * (1.0 + (3.0 * CUBIC) * squared)
        )


def split_rows(total, keep, send, bit):
    own = (lax.axis_index("dp") // (1 << bit)) % 2 == 0
    half = keep.shape[-2]
    low, high = total[..., :half, :], total[..., half:, :]
    keep[...] = jnp.where(own, low, high)
    send[...] = jnp.where(own, high, low)


def masked_top(lengths, mine, far, at):
    live = lengths[0, 0] + lengths[0, 1]
    own_rows = mine.shape[0]
    position = at * own_rows + lax.broadcasted_iota(jnp.int32, (own_rows, 1), 0)
    values = jnp.concatenate([mine[...], far[...]], axis=1)
    return jnp.where(position < live, values, BF16(0))


def down_kernel(bit_down, bit_up, lengths, top, top_far, top_col, top_far_col, hidden, slope, normed, w_down, got, got_side,
                w_up, w_up_other, down_keep, down_send, up_keep, up_send, keep, send, sums, w_other_out, top_all, grad_pre):
    own_rows, half = top.shape
    units = hidden.shape[1]
    row, col = lax.axis_index("row"), lax.axis_index("col")
    top_all[half_rows(col, own_rows)] = masked_top(lengths, top, top_far, col)
    top_all[half_rows(1 - col, own_rows)] = masked_top(lengths, top_col, top_far_col, 1 - col)
    top_rows = top_all[...]
    split_rows(dot_tn(hidden[...], top_rows).astype(BF16), down_keep, down_send, bit_down)
    w_other = both_sides(got, got_side, 0)
    w_other_out[...] = w_other
    grad_hidden = dot_nt(top_rows[:, :half], w_down[half_rows(row, units)]) + dot_nt(
        top_rows[:, half:], w_other
    )
    grads = (grad_hidden * slope[...]).astype(BF16)
    grad_pre[...] = grads
    w_mine = w_up[:, pl.ds(pl.multiple_of(row * units, units), units)]

    def total_of(rows):
        values = grad_pre[rows]
        return jnp.concatenate([dot_nt(values, w_mine), dot_nt(values, w_up_other[...])], axis=1)

    split_tokens(total_of, keep, send, own_rows, col)
    total = dot_tn(normed[...], grads).astype(BF16)
    split_rows(total.reshape(2, half, units), up_keep, up_send, bit_up)
    sums[...] = jnp.zeros_like(sums)
    sums[0:1] = jnp.sum(grads.astype(F32), axis=0, keepdims=True)
    sums[1:2, :half] = jnp.sum(top_rows[:, :half].astype(F32), axis=0, keepdims=True)


def output_kernel(hidden, w_down, w_other, keep, send):
    units = hidden.shape[1]
    row, col = lax.axis_index("row"), lax.axis_index("col")
    w_mine = w_down[half_rows(row, units)]

    def total_of(rows):
        values = hidden[rows]
        return jnp.concatenate([dot(values, w_mine), dot(values, w_other[...])], axis=1)

    split_tokens(total_of, keep, send, keep.shape[0], col)


def second_back_kernel(lengths, total, total_far, unit_ref, inverse_ref, vec, vec_other, top, top_far, middle_out, datt, sums):
    half = top.shape[1]
    got = total_far[...].astype(F32)
    grads = total[...].astype(F32) + jnp.concatenate([got[:, half:], got[:, :half]], axis=1)
    unit = unit_ref[...]
    scaled = grads * wide_vector(vec, vec_other, 3)
    mean_plain = jnp.mean(scaled, axis=1, keepdims=True)
    mean_unit = jnp.mean(scaled * unit, axis=1, keepdims=True)
    own = masked_top(lengths, top, top_far, lax.axis_index("col")).astype(F32)
    result = own + inverse_ref[:, :1] * (scaled - mean_plain - unit * mean_unit)
    middle_out[...] = result[:, :half]
    datt[...] = result.astype(BF16)
    sums[...] = jnp.zeros_like(sums)
    sums[0:1] = jnp.sum((grads * unit)[:, :half], axis=0, keepdims=True)
    sums[1:2] = jnp.sum(grads[:, :half], axis=0, keepdims=True)


def backward_kernel(bit_first, bit_second, lengths, own, other, w_mine, w_other, q_hbm, k_hbm, v_hbm, o_ref, lse, normed_hbm, w_kept, got, got_side,
                    first_keep, first_send, second_keep, second_send, keep, send, sums, datt, out, acc_k, acc_v, do_ref,
                    q_ref, k_ref, v_ref, normed, sems):
    copies = start_copies(
        [(q_hbm, q_ref), (k_hbm, k_ref), (v_hbm, v_ref), (normed_hbm, normed)], sems
    )
    own_rows, width = own.shape
    half = width // 2
    third = q_ref.shape[1]
    row, col = lax.axis_index("row"), lax.axis_index("col")
    quarter = half_rows(row, third)
    for ref, at in ((own, col), (other, 1 - col)):
        where = half_rows(at, own_rows)
        values = ref[...]
        datt[where] = values
        do_ref[where] = (
            dot_nt(values[:, :half], w_mine[quarter]) + dot_nt(values[:, half:], w_other[quarter])
        ).astype(BF16)
    for copy in copies:
        copy.wait()
    keys_t = k_ref[...].T
    acc_k[...] = jnp.zeros_like(acc_k)
    acc_v[...] = jnp.zeros_like(acc_v)
    scale = BF16(HEAD_DIM ** (-0.5))
    for begin in (0, own_rows):
        keys = begin + own_rows
        allowed = allowed_block(lengths, keys, begin, own_rows)
        query = q_ref[begin:keys] * scale
        grad_mixed = do_ref[begin:keys]
        parts = []
        for head in range(third // HEAD_DIM):
            mask = head_mask(third, head)
            key = jnp.where(mask, k_ref[:keys], BF16(0))
            scores = jnp.where(allowed, dot_nt(key, query), MASKED)
            probs = jnp.exp(scores - lse[head : head + 1, begin:keys])
            value = jnp.where(mask, v_ref[:keys], BF16(0))
            grad_probs = dot_nt(value, grad_mixed)
            both = probs * grad_probs
            inner = jnp.sum(both, axis=0, keepdims=True)
            grad_raw = (both - probs * inner).astype(BF16) * scale
            acc_v[:keys] += jnp.where(mask, dot(probs.astype(BF16), grad_mixed), 0.0)
            acc_k[:keys] += jnp.where(mask, dot(grad_raw, q_ref[begin:keys]), 0.0)
            parts.append(dot(keys_t[head * HEAD_DIM : (head + 1) * HEAD_DIM, :keys], grad_raw))
        out[begin:keys, :third] = jnp.concatenate(parts, axis=0).T.astype(BF16)
    out[:, third : 2 * third] = acc_k[...].astype(BF16)
    out[:, 2 * third :] = acc_v[...].astype(BF16)
    grads = out[...]
    weights = dot_tn(normed[...], grads).astype(BF16)
    grad_out = dot_tn(datt[...], o_ref[...]).astype(BF16)
    split_rows(weights[:, : 2 * third].reshape(2, half, 2 * third), first_keep, first_send, bit_first)
    last = jnp.concatenate([weights[:, 2 * third :], grad_out], axis=1)
    split_rows(last.reshape(2, half, 2 * third), second_keep, second_send, bit_second)

    w_got = both_sides(got, got_side, 0)

    def total_of(rows):
        values = out[rows]
        return jnp.concatenate([dot_nt(values, w_kept[...]), dot_nt(values, w_got)], axis=1)

    split_tokens(total_of, keep, send, own_rows, col)
    sums[...] = jnp.zeros_like(sums)
    sums[0:1, : 3 * third] = jnp.sum(grads.astype(F32), axis=0, keepdims=True)
    sums[1:2, :half] = jnp.sum(datt[:, :half].astype(F32), axis=0, keepdims=True)


def first_back_kernel(keep, got, unit_ref, vec, vec_other, mine, far, stats):
    half = mine.shape[1]
    grads = keep[...] + got[...].astype(F32)
    mine[...] = grads[:, :half]
    far[...] = grads[:, half:].astype(BF16)
    scaled = grads * wide_vector(vec, vec_other, 0)
    plain = jnp.sum(scaled, axis=1, keepdims=True)
    crossed = jnp.sum(scaled * unit_ref[...], axis=1, keepdims=True)
    lanes = lax.broadcasted_iota(jnp.int32, (1, 128), 1)
    both = jnp.where(lanes == 0, plain, jnp.where(lanes == 1, crossed, 0.0))
    stats[...] = both.T[:8]


def last_kernel(mine, got, stats, stats_far, unit_ref, inverse_ref, vec, middle, result, sums):
    half = mine.shape[1]
    unit = unit_ref[:, :half]
    grads = mine[...] + got[...].astype(F32)
    total = (stats[...] + stats_far[...]) / (2 * half)
    columns = jnp.concatenate([total, jnp.zeros((120, total.shape[1]), F32)], axis=0).T
    grad_in = inverse_ref[:, :1] * (
        grads * vec[0:1] - columns[:, 0:1] - unit * columns[:, 1:2]
    )
    result[...] = (middle[...] + grad_in).astype(BF16)
    sums[...] = jnp.zeros_like(sums)
    sums[0:1] = jnp.sum(grads * unit, axis=0, keepdims=True)
    sums[1:2] = jnp.sum(grads, axis=0, keepdims=True)


def halve_kernel(bit, kept, got, keep, send):
    total = (kept[...].astype(F32) + got[...].astype(F32)).astype(BF16)
    split_rows(total, keep, send, bit)


def turn_kernel(stacked, kept, got, keep, send):
    total = (kept[...].astype(F32) + got[...].astype(F32)).astype(BF16)
    if stacked:
        keep[...], send[...] = total[0], total[1]
    else:
        half = keep.shape[1]
        keep[...], send[...] = total[:, :half], total[:, half:]


def stack_kernel(mine, got, out):
    out[0], out[1] = mine[...], got[...]


def double_kernel(bit, mine, got, out):
    own = (lax.axis_index("dp") // (1 << bit)) % 2 == 0
    half = mine.shape[1]
    out[:, :half] = jnp.where(own, mine[...], got[...])
    out[:, half:] = jnp.where(own, got[...], mine[...])


class Chain:
    def __init__(self, keep, send, bits, stacked):
        self.keep, self.bits, self.stacked = keep, bits, stacked
        self.stage = 0
        self.steps = 2 * len(bits) + 1
        self.got = from_dp(send, bits[0])

    def step(self):
        self.stage += 1
        count, stage = len(self.bits), self.stage
        if stage < count:
            bit = self.bits[stage]
            dims = self.keep.shape[:-2] + (self.keep.shape[-2] // 2, self.keep.shape[-1])
            self.keep, send = call(
                lambda *refs: halve_kernel(bit, *refs), (shape(dims, BF16),) * 2, self.keep, self.got
            )
            self.got = from_dp(send, bit)
        elif stage == count:
            rows, width = self.keep.shape[-2:]
            dims = (rows, width) if self.stacked else (rows, width // 2)
            stacked = self.stacked
            self.keep, send = call(
                lambda *refs: turn_kernel(stacked, *refs),
                (shape(dims, BF16),) * 2,
                self.keep,
                self.got,
            )
            self.got = from_row(send)
        elif stage < self.steps:
            self.gather()
            self.got = from_dp(self.keep, self.bits[2 * count - stage])

    def gather(self):
        count, stage = len(self.bits), self.stage
        if stage == count + 1:
            dims = (2,) + self.keep.shape
            self.keep = call(stack_kernel, shape(dims, BF16), self.keep, self.got)
        else:
            bit = self.bits[2 * count - stage + 1]
            pair, rows, width = self.keep.shape
            self.keep = call(
                lambda *refs: double_kernel(bit, *refs),
                shape((pair, 2 * rows, width), BF16),
                self.keep,
                self.got,
            )

    @property
    def last_bit(self):
        return self.bits[0]


def arrived(chains, *others):
    flat = [(chain.keep, chain.got) for chain in chains]
    flat, others = lax.optimization_barrier((flat, others))
    for chain, (keep, got) in zip(chains, flat):
        chain.keep, chain.got = keep, got
    return others


def advance(chains):
    for chain in chains:
        chain.step()


def ordered_halves(bit, mine, got):
    own = (lax.axis_index("dp") // (1 << bit)) % 2 == 0
    return jnp.concatenate(
        [jnp.where(own, mine, got), jnp.where(own, got, mine)], axis=0
    )


def by_row(mine, far, axis):
    first = lax.axis_index("row") == 0
    return jnp.concatenate(
        [jnp.where(first, mine, far), jnp.where(first, far, mine)], axis=axis
    )


def up_end_kernel(bit, mine, got, out):
    own = (lax.axis_index("dp") // (1 << bit)) % 2
    here = pl.program_id(0) == own
    near = jnp.where(here, mine[0], got[0])
    far = jnp.where(here, mine[1], got[1])
    out[...] = by_row(near, far, 1).astype(F32)


def down_end_kernel(bit, mine, got, out):
    own = (lax.axis_index("dp") // (1 << bit)) % 2
    here = pl.program_id(1) == own
    near = pl.program_id(0) == lax.axis_index("row")
    part = jnp.where(near, jnp.where(here, mine[0], got[0]), jnp.where(here, mine[1], got[1]))
    out[...] = part.astype(F32)


def attention_end_kernel(bit, flip, mine, got, left, right):
    near = ordered_halves(bit, mine[0], got[0])
    far = ordered_halves(bit, mine[1], got[1])
    third = near.shape[1] // 2
    left[...] = by_row(near[:, :third], far[:, :third], 1).astype(F32)
    last = by_row(near[:, third:], far[:, third:], 1).astype(F32)
    right[...] = last.T if flip else last


def end_call(kernel, grid, out_shape, block, index, mine, got):
    whole = pl.BlockSpec(memory_space=pltpu.VMEM)
    return pl.pallas_call(
        kernel,
        grid=grid,
        out_shape=out_shape,
        in_specs=[whole, whole],
        out_specs=pl.BlockSpec(block, index),
        compiler_params=pltpu.CompilerParams(vmem_limit_bytes=16 * MIB),
    )(mine, got)


def body(
    tokens,
    out_grad,
    seq_lengths,
    w_query,
    w_key,
    w_value,
    w_out,
    w_up,
    w_down,
    b_query,
    b_value,
    b_out,
    b_up,
    b_down,
    gain_attn,
    shift_attn,
    gain_mlp,
    shift_mlp,
):
    row = lax.axis_index("row")
    own_rows, half = tokens.shape
    width = 2 * half
    rows = 2 * own_rows
    third = w_query.shape[1] // 2
    units = w_up.shape[1] // 2
    side = lax.axis_index("dp") % 2
    count = lax.axis_size("dp").bit_length() - 1
    bits = list(range(count))
    turned = [1, 0] + bits[2:] if count > 1 else bits
    tall = shape((own_rows, width), F32)
    tall_low = shape((own_rows, width), BF16)
    column = shape((own_rows, 128), F32)
    pair_sums = shape((8, half), F32)

    tokens_far = from_row(tokens)
    operands = (gain_attn, shift_attn, b_out, gain_mlp, shift_mlp, b_query, b_value, b_up, b_down)
    vec, loc = call(
        vector_kernel,
        (shape((8, half), F32), shape((8, units), F32)),
        *operands,
        hbm=range(9),
        vmem=60,
        scratch=[pltpu.VMEM(x.shape, x.dtype) for x in operands] + [pltpu.SemaphoreType.DMA((9,))],
    )
    vec_far = from_row(vec)
    block = pltpu.VMEM((half, 2 * third), BF16)
    w_kept, sent, sent_out, sent_up, sent_down = call(
        pack_kernel,
        (
            shape((half, 3 * third), BF16),
            shape((half // 2, 3 * third), BF16),
            shape((w_out.shape[0] // 2, half), BF16),
            shape((half // 2, units), BF16),
            shape((units // 2, half), BF16),
        ),
        w_query, w_key, w_value, w_out, w_up, w_down, loc,
        hbm=range(6),
        vmem=60,
        scratch=[block, block, block, pltpu.SemaphoreType.DMA((6,))],
    )
    top_col = from_col(out_grad)
    tokens_far, vec_far, sent = hold(tokens_far, vec_far, sent)
    w_got = from_row(sent)
    normed, unit_attn, inverse_attn = call(
        first_norm_kernel, (tall_low, tall, column), tokens, tokens_far, vec, vec_far
    )
    normed, sent_out, sent_up, sent_down = hold(normed, sent_out, sent_up, sent_down)
    normed_col = from_col(normed)
    w_side = from_dp(w_got, 0)
    out_got = from_row(sent_out)
    up_got = from_row(sent_up)
    down_got = from_row(sent_down)
    normed_col, w_got, w_side, out_got = hold(normed_col, w_got, w_side, out_got)
    out_side = from_dp(out_got, 0)

    like = shape((rows, third), BF16)
    normed_all, query, key, value, mixed, lse = call(
        forward_kernel,
        (shape((rows, width), BF16), like, like, like, like, shape((8, rows), F32)),
        seq_lengths,
        normed,
        normed_col,
        w_kept,
        w_got,
        w_side,
        loc,
        smem=(0,),
        hbm_out=range(4),
        scratch=[pltpu.VMEM((rows, width), BF16)]
        + [pltpu.VMEM((rows, third), BF16)] * 3
        + [pltpu.SemaphoreType.DMA((4,))],
    )
    mixed, up_got = hold(mixed, up_got)
    mixed_far = from_row(mixed)
    up_side = from_dp(up_got, 0)
    mixed_far, out_side, up_side, down_got, out_grad_send = hold(
        mixed_far, out_side, up_side, down_got, out_grad
    )

    keep, send, w_out_far = call(
        branch_kernel, (tall, tall_low, shape(w_out.shape, BF16)),
        mixed, mixed_far, w_out, out_got, out_side,
    )
    got = from_col(send)
    top_far = from_row(out_grad_send)
    top_far_col = from_col(top_far)
    down_side = from_dp(down_got, 0)
    (got,) = hold(got)

    middle, normed_mlp, unit_mlp, inverse_mlp = call(
        second_norm_kernel,
        (shape((own_rows, half), F32), tall_low, tall, column),
        tokens, tokens_far, keep, got, vec, vec_far,
    )
    normed_mlp_col = from_col(normed_mlp)
    normed_mlp_col, top_far, down_side = hold(normed_mlp_col, top_far, down_side)

    normed_mlp_all, hidden, slope, w_up_far = call(
        up_kernel,
        (
            shape((rows, width), BF16),
            shape((rows, units), BF16),
            shape((rows, units), F32),
            shape((half, units), BF16),
        ),
        normed_mlp, normed_mlp_col, w_up, up_got, up_side, loc,
    )
    hidden, top_far, top_far_col, down_side = hold(hidden, top_far, top_far_col, down_side)

    split_down = shape((units // 2, width), BF16)
    split_up = shape((2, half // 2, units), BF16)
    down_keep, down_send, up_keep, up_send, keep, send, mlp_sums, w_down_far = call(
        lambda *refs: down_kernel(bits[0], turned[0], *refs),
        (
            split_down, split_down, split_up, split_up, tall, tall_low,
            shape((8, units), F32), shape((units, half), BF16),
        ),
        seq_lengths, out_grad, top_far, top_col, top_far_col, hidden, slope, normed_mlp_all,
        w_down, down_got, down_side, w_up, w_up_far,
        scratch=[pltpu.VMEM((rows, width), BF16), pltpu.VMEM((rows, units), BF16)],
        smem=(0,),
    )
    got = from_col(send)
    down = Chain(down_keep, down_send, bits, False)
    up = Chain(up_keep, up_send, turned, True)
    (got,) = hold(got)

    total = (keep + got.astype(F32)).astype(BF16)
    total_far = from_row(total)
    keep, send = call(
        output_kernel, (tall, tall_low), hidden, w_down, w_down_far,
    )
    got = from_col(send)
    total_far, got = hold(total_far, got)

    grad_middle, datt, mid_sums = call(
        second_back_kernel,
        (shape((own_rows, half), F32), tall_low, pair_sums),
        seq_lengths, total, total_far, unit_mlp, inverse_mlp, vec, vec_far, out_grad, top_far,
        smem=(0,),
    )
    datt_col = from_col(datt)
    raised = keep + got.astype(F32)
    raised_far = from_row(raised[:, half:].astype(BF16))
    (datt_col,) = arrived([down, up], datt_col)
    advance([down, up])

    split_pair = shape((2, half // 2, 2 * third), BF16)
    first_keep, first_send, second_keep, second_send, keep, send, attn_sums = call(
        lambda *refs: backward_kernel(bits[0], turned[0], *refs),
        (split_pair,) * 4 + (tall, tall_low, shape((8, width), F32)),
        seq_lengths, datt, datt_col, w_out, w_out_far, query, key, value, mixed, lse,
        normed_all, w_kept, w_got, w_side,
        scratch=[
            pltpu.VMEM((rows, width), BF16),
            pltpu.VMEM((rows, 3 * third), BF16),
            pltpu.VMEM((rows, third), F32),
            pltpu.VMEM((rows, third), F32),
        ]
        + [pltpu.VMEM((rows, third), BF16)] * 4
        + [pltpu.VMEM((rows, width), BF16), pltpu.SemaphoreType.DMA((4,))],
        smem=(0,),
        hbm=(5, 6, 7, 10),
    )
    keep, send, raised_far = arrived([down, up], keep, send, raised_far)
    got = from_col(send)
    first = Chain(first_keep, first_send, bits, True)
    second = Chain(second_keep, second_send, turned, True)
    advance([down, up])
    output = (middle + raised[:, :half] + raised_far.astype(F32) + loc[2:3, :half]).astype(BF16)
    (got,) = hold(got)

    mine, far, stats = call(
        first_back_kernel,
        (shape((own_rows, half), F32), shape((own_rows, half), BF16), shape((8, own_rows), F32)),
        keep, got, unit_attn, vec, vec_far,
    )
    got = from_row(far)
    stats_far = from_row(stats)
    pair, late = [first, second], [down, up]
    got, stats_far = arrived(pair + late, got, stats_far)
    advance(pair + late)
    input_grad, in_sums = call(
        last_kernel,
        (shape((own_rows, half), BF16), pair_sums),
        mine, got, stats, stats_far, unit_attn, inverse_attn, vec, grad_middle,
    )

    halves = jnp.concatenate([in_sums, mid_sums], axis=1)
    halves_col = from_col(halves)
    (halves_col,) = arrived(pair + late, halves_col)
    small = jnp.concatenate(
        [
            (halves + halves_col)[:2],
            mlp_sums[:2, :width],
            attn_sums[:2],
            jnp.zeros((2, width), F32),
        ]
    )
    waiting = list(bits)
    while pair[0].stage < pair[0].steps - 1:
        moving = [chain for chain in late + pair if chain.stage < chain.steps - 1]
        advance(moving)
        if waiting:
            (small_far,) = arrived(moving, from_dp(small, waiting.pop(0)))
            small = small + small_far
        else:
            arrived(moving)
    for bit in waiting:
        small = small + from_dp(small, bit)

    wide = w_query.shape[1]
    outs = (shape((half, wide), F32),) * 2
    grad_query, grad_key = call(
        lambda *refs: attention_end_kernel(first.last_bit, False, *refs), outs, first.keep, first.got
    )
    grad_value, grad_out = call(
        lambda *refs: attention_end_kernel(second.last_bit, True, *refs), outs, second.keep, second.got
    )
    grad_down = end_call(
        lambda *refs: down_end_kernel(down.last_bit, *refs),
        (2, 2),
        shape((2 * units, half), F32),
        (units // 2, half),
        lambda i, j: (2 * i + j, 0),
        down.keep,
        down.got,
    )
    grad_up = end_call(
        lambda *refs: up_end_kernel(up.last_bit, *refs),
        (2,),
        shape((half, 2 * units), F32),
        (half // 2, 2 * units),
        lambda i: (i, 0),
        up.keep,
        up.got,
    )
    return (
        output,
        input_grad,
        grad_query,
        grad_key,
        grad_value,
        grad_out,
        grad_up,
        grad_down,
        small[4, :third],
        small[4, 2 * third : 3 * third],
        small[5, :half],
        small[2, :units],
        small[3, :half],
        small[0, :half],
        small[1, :half],
        small[0, half:],
        small[1, half:],
    )


def solution(mesh):
    return jax.shard_map(
        body,
        mesh=mesh,
        in_specs=(
            P(("dp", "col"), "row"),
            P(("dp", "col"), "row"),
            P("dp", None),
            P("row", "col"),
            P("row", "col"),
            P("row", "col"),
            P("col", "row"),
            P("row", "col"),
            P("col", "row"),
            P(("col", "row")),
            P(("col", "row")),
            P("row"),
            P(("col", "row")),
            P("row"),
            P("row"),
            P("row"),
            P("row"),
            P("row"),
        ),
        out_specs=(
            P(("dp", "col"), "row"),
            P(("dp", "col"), "row"),
            P("row", "col"),
            P("row", "col"),
            P("row", "col"),
            P("col", "row"),
            P("row", "col"),
            P("col", "row"),
            P(("col", "row")),
            P(("col", "row")),
            P("row"),
            P(("col", "row")),
            P("row"),
            P("row"),
            P("row"),
            P("row"),
            P("row"),
        ),
        check_vma=False,
    )
```

```python
import jax
import jax.numpy as jnp
from jax import lax
from jax.experimental import pallas as pl
from jax.experimental.pallas import tpu as pltpu
from jax.sharding import PartitionSpec as P

HEAD_DIM = 64
EPSILON = 1e-05
MASKED = -1e30
F32 = jnp.float32
BF16 = jnp.bfloat16
SWAP = ((0, 1), (1, 0))
CUBIC = 0.044715
ROOT = 0.7978845608028654
MIB = 1024 * 1024
VMEM_START = 54
EXTRA = 16


def dot(left, right):
    return jnp.dot(left, right, preferred_element_type=F32)


def dot_nt(left, right):
    return lax.dot_general(left, right, (((1,), (1,)), ((), ())), preferred_element_type=F32)


def dot_tn(left, right):
    return lax.dot_general(left, right, (((0,), (0,)), ((), ())), preferred_element_type=F32)


def from_row(values):
    return lax.ppermute(values, "row", SWAP)


def from_col(values):
    return lax.ppermute(values, "col", SWAP)


def dp_pairs(bit):
    count = lax.axis_size("dp")
    return [(i, i ^ (1 << bit)) for i in range(count)]


def from_dp(values, bit):
    return lax.ppermute(values, "dp", dp_pairs(bit))


def hold(*values):
    return lax.optimization_barrier(values)


def shape(dims, kind):
    return jax.ShapeDtypeStruct(tuple(dims), kind)


def call(kernel, out_shape, *operands, scratch=(), smem=(), hbm=(), hbm_out=(), vmem=16):
    spaces = [
        pltpu.SMEM if i in smem else pltpu.HBM if i in hbm else pltpu.VMEM
        for i in range(len(operands))
    ]
    out_specs = jax.tree.map(lambda _: pl.BlockSpec(memory_space=pltpu.VMEM), out_shape)
    if hbm_out:
        out_specs = tuple(
            pl.BlockSpec(memory_space=pltpu.HBM if i in hbm_out else pltpu.VMEM)
            for i in range(len(out_shape))
        )
    return pl.pallas_call(
        kernel,
        out_shape=out_shape,
        in_specs=[pl.BlockSpec(memory_space=space) for space in spaces],
        out_specs=out_specs,
        scratch_shapes=list(scratch),
        compiler_params=pltpu.CompilerParams(vmem_limit_bytes=vmem * MIB),
        cost_estimate=pl.CostEstimate(flops=0, bytes_accessed=0, transcendentals=0),
    )(*operands)


def half_rows(index, size):
    return pl.ds(pl.multiple_of(index * size, size), size)


def start_copies(pairs, sems):
    copies = [
        pltpu.make_async_copy(source, target, sems.at[i]) for i, (source, target) in enumerate(pairs)
    ]
    for copy in copies:
        copy.start()
    return copies


GAIN_A, SHIFT_A, BIAS_O, GAIN_M, SHIFT_M, BIAS_QKV, BIAS_UP, BIAS_DOWN = 0, 1, 2, 3, 4, 5, 6, 8


def start_kernel(*refs):
    vectors, (w_q, w_k, w_v, w_out, w_up, w_down) = refs[:9], refs[9:15]
    kept, sent, out_sent, up_sent, down_sent = refs[15:20]
    held, held_w, extra, sems = refs[20:29], refs[29:32], refs[32], refs[33]
    row, side = lax.axis_index("row"), lax.axis_index("dp") % 2
    other_side = (lax.axis_index("dp") // 2) % 2
    units = up_sent.shape[1]
    copies = start_copies(
        list(zip((w_q, w_k, w_v), held_w))
        + list(zip(vectors, held))
        + [
            (w_out.at[half_rows(side, out_sent.shape[0])], out_sent),
            (w_up.at[half_rows(side, up_sent.shape[0]), half_rows(1 - row, units)], up_sent),
            (w_down.at[half_rows(2 * (1 - row) + other_side, down_sent.shape[0])], down_sent),
        ],
        sems,
    )
    first = row == 0
    half, third = w_q.shape[0], w_q.shape[1] // 2
    keeps, sends = [], []
    for ref, copy in zip(held_w, copies):
        copy.wait()
        low, high = ref[:, :third], ref[:, third:]
        keeps.append(jnp.where(first, low, high))
        sends.append(jnp.where(first, high, low))
    kept[:half] = jnp.concatenate(keeps, axis=1)
    sent[:half] = jnp.concatenate(sends, axis=1)
    for copy in copies[3:]:
        copy.wait()
    extra[...] = jnp.zeros_like(extra)
    lines = [ref[...].astype(F32).reshape(1, -1) for ref in held]
    for i in range(5):
        extra[i : i + 1, :half] = lines[i]
    b_q, b_v, b_u, b_d = lines[5:]
    extra[BIAS_QKV : BIAS_QKV + 1, :third] = b_q
    extra[BIAS_QKV : BIAS_QKV + 1, 2 * third :] = b_v
    for i in range(2):
        extra[BIAS_UP + i : BIAS_UP + i + 1, :half] = b_u[:, i * half : (i + 1) * half]
    extra[BIAS_DOWN : BIAS_DOWN + 1, :half] = b_d
    kept[half:] = extra[...].astype(BF16)
    sent[half:] = extra[...].astype(BF16)


def normed_parts(values):
    mean = jnp.mean(values, axis=1, keepdims=True)
    centered = values - mean
    variance = jnp.mean(centered * centered, axis=1, keepdims=True)
    inverse = lax.rsqrt(variance + EPSILON)
    return centered * inverse, inverse


def both_halves(mine, far):
    return jnp.concatenate([mine[...], far[...]], axis=1).astype(F32)


def vector_of(kept, i):
    half = kept.shape[0] - EXTRA
    return kept[half:].astype(F32)[i : i + 1, :half]


def wide_vector(kept, got, i):
    return jnp.concatenate([vector_of(kept, i), vector_of(got, i)], axis=1)


def head_mask(width, head):
    lanes = lax.broadcasted_iota(jnp.int32, (1, width), 1)
    return lanes // HEAD_DIM == head


def allowed_block(lengths, keys, first_query, count):
    first, second = lengths[0, 0], lengths[0, 0] + lengths[0, 1]
    query = first_query + lax.broadcasted_iota(jnp.int32, (1, count), 1)
    begin = jnp.where(query >= second, second, jnp.where(query >= first, first, 0))
    key = lax.broadcasted_iota(jnp.int32, (keys, count), 0)
    return (key >= begin) & (key <= query)


def forward_kernel(lengths, own, own_far, col_own, col_far, w_kept, w_got, norm_hbm, q_hbm, k_hbm, v_hbm, o_out, lse,
                   norm_out, q_out, k_out, v_out, sems):
    own_rows, half = own.shape
    third = q_out.shape[1]
    col = lax.axis_index("col")
    gain, shift = wide_vector(w_kept, w_got, GAIN_A), wide_vector(w_kept, w_got, SHIFT_A)
    bias = w_kept[half:].astype(F32)[BIAS_QKV : BIAS_QKV + 1]
    for ref, far, at in ((own, own_far, col), (col_own, col_far, 1 - col)):
        where = half_rows(at, own_rows)
        unit, _ = normed_parts(both_halves(ref, far))
        values = (unit * gain + shift).astype(BF16)
        norm_out[where] = values
        total = dot(values[:, :half], w_kept[:half]) + dot(values[:, half:], w_got[:half])
        total = (total + bias).astype(BF16)
        q_out[where] = total[:, :third]
        k_out[where] = total[:, third : 2 * third]
        v_out[where] = total[:, 2 * third :]
    copies = start_copies(
        [(norm_out, norm_hbm), (q_out, q_hbm), (k_out, k_hbm), (v_out, v_hbm)], sems
    )
    lse[...] = jnp.zeros_like(lse)
    values_t = v_out[...].T
    for begin in (0, own_rows):
        keys = begin + own_rows
        allowed = allowed_block(lengths, keys, begin, own_rows)
        query = q_out[begin:keys] * BF16(HEAD_DIM ** (-0.5))
        parts = []
        for head in range(third // HEAD_DIM):
            key = jnp.where(head_mask(third, head), k_out[:keys], BF16(0))
            scores = jnp.where(allowed, dot_nt(key, query), MASKED)
            largest = jnp.max(scores, axis=0, keepdims=True)
            weights = jnp.exp(scores - largest)
            summed = jnp.sum(weights, axis=0, keepdims=True)
            lse[head : head + 1, begin:keys] = largest + jnp.log(summed)
            mixed = dot(
                values_t[head * HEAD_DIM : (head + 1) * HEAD_DIM, :keys], weights.astype(BF16)
            )
            parts.append(mixed / summed)
        o_out[begin:keys] = jnp.concatenate(parts, axis=0).T.astype(BF16)
    for copy in copies:
        copy.wait()


def split_tokens(total_of, keep, send, own_rows, col):
    keep[...] = total_of(half_rows(col, own_rows))
    send[...] = total_of(half_rows(1 - col, own_rows)).astype(BF16)


def branch_kernel(mixed, mixed_other, w_mine, got, got_side, keep, send, w_other):
    w_other[...] = both_sides(got, got_side, 0)
    row = lax.axis_index("row")
    third = mixed.shape[1]
    own, far = half_rows(row, third), half_rows(1 - row, third)

    for i, w in enumerate((w_mine, w_other)):
        lanes = slice(i * w.shape[1], (i + 1) * w.shape[1])
        part = dot(mixed[...], w[own]) + dot(mixed_other[...], w[far])
        keep[:, lanes] = part
        send[:, lanes] = part.astype(BF16)


def second_norm_kernel(own, own_far, col_own, col_far, keep, got, kept, sent, middle, normed, unit_out, inverse_out):
    own_rows = own.shape[0]
    col = lax.axis_index("col")
    bias, gain, shift = [wide_vector(kept, sent, i) for i in (BIAS_O, GAIN_M, SHIFT_M)]
    for ref, far, at in ((own, own_far, col), (col_own, col_far, 1 - col)):
        where = half_rows(at, own_rows)
        values = both_halves(ref, far) + (keep[where] + got[where].astype(F32) + bias)
        unit, inverse = normed_parts(values)
        normed[where] = (unit * gain + shift).astype(BF16)
        if ref is own:
            middle[...] = values[:, : middle.shape[1]]
            unit_out[...] = unit
            inverse_out[...] = jnp.broadcast_to(inverse, inverse_out.shape)


def both_sides(got, got_side, axis, bit=0):
    first = (lax.axis_index("dp") // (1 << bit)) % 2 == 0
    low = jnp.where(first, got[...], got_side[...])
    high = jnp.where(first, got_side[...], got[...])
    return jnp.concatenate([low, high], axis=axis)


def up_kernel(normed, w_up, got, got_side, kept, hidden_out, slope_out, w_other_out):
    rows, width = normed.shape
    half = width // 2
    units = got.shape[1]
    row = lax.axis_index("row")
    w_mine = w_up[:, pl.ds(pl.multiple_of(row * units, units), units)]
    w_other = both_sides(got, got_side, 0)
    w_other_out[...] = w_other
    bias = jnp.concatenate([vector_of(kept, BIAS_UP + i) for i in range(2)], axis=1)
    for begin in (0, rows // 2):
        where = slice(begin, begin + rows // 2)
        values = normed[where]
        u = dot(values[:, :half], w_mine) + dot(values[:, half:], w_other) + bias
        squared = u * u
        bent = jnp.tanh(ROOT * (u + CUBIC * (squared * u)))
        raised = 0.5 * (1.0 + bent)
        hidden_out[where] = (u * raised).astype(BF16)
        slope_out[where] = raised + 0.5 * u * (1.0 - bent * bent) * (
            ROOT * (1.0 + (3.0 * CUBIC) * squared)
        )


def split_rows(total, keep, send, bit):
    own = (lax.axis_index("dp") // (1 << bit)) % 2 == 0
    half = keep.shape[-2]
    low, high = total[..., :half, :], total[..., half:, :]
    keep[...] = jnp.where(own, low, high)
    send[...] = jnp.where(own, high, low)


def masked_top(lengths, mine, far, at):
    live = lengths[0, 0] + lengths[0, 1]
    own_rows = mine.shape[0]
    position = at * own_rows + lax.broadcasted_iota(jnp.int32, (own_rows, 1), 0)
    values = jnp.concatenate([mine[...], far[...]], axis=1)
    return jnp.where(position < live, values, BF16(0))


def down_kernel(bit_down, bit_up, lengths, top, top_far, top_col, top_far_col, hidden, slope, normed, w_down, got, got_side,
                w_up, w_up_other, down_keep, down_send, up_keep, up_send, keep, send, sums, w_other_out, top_all, grad_pre):
    own_rows, half = top.shape
    units = hidden.shape[1]
    row, col = lax.axis_index("row"), lax.axis_index("col")
    top_all[half_rows(col, own_rows)] = masked_top(lengths, top, top_far, col)
    top_all[half_rows(1 - col, own_rows)] = masked_top(lengths, top_col, top_far_col, 1 - col)
    top_rows = top_all[...]
    total = dot_tn(hidden[...], top_rows).astype(BF16)
    split_rows(jnp.stack([total[:, :half], total[:, half:]]), down_keep, down_send, bit_down)
    w_other = both_sides(got, got_side, 0, 1)
    w_other_out[...] = w_other
    grad_hidden = dot_nt(top_rows[:, :half], w_down[half_rows(row, units)]) + dot_nt(
        top_rows[:, half:], w_other
    )
    grads = (grad_hidden * slope[...]).astype(BF16)
    grad_pre[...] = grads
    w_mine = w_up[:, pl.ds(pl.multiple_of(row * units, units), units)]

    def total_of(rows):
        values = grad_pre[rows]
        return jnp.concatenate([dot_nt(values, w_mine), dot_nt(values, w_up_other[...])], axis=1)

    split_tokens(total_of, keep, send, own_rows, col)
    total = dot_tn(normed[...], grads).astype(BF16)
    total = total.reshape(2, half, units)
    total = jnp.concatenate([total[..., : units // 2], total[..., units // 2 :]], axis=1)
    split_rows(total, up_keep, up_send, bit_up)
    sums[...] = jnp.zeros_like(sums)
    sums[0:1] = jnp.sum(grads.astype(F32), axis=0, keepdims=True)
    sums[1:2, :half] = jnp.sum(top_rows[:, :half].astype(F32), axis=0, keepdims=True)


def output_kernel(hidden, w_down, w_other, keep, send):
    units = hidden.shape[1]
    row, col = lax.axis_index("row"), lax.axis_index("col")
    w_mine = w_down[half_rows(row, units)]

    def total_of(rows):
        values = hidden[rows]
        return jnp.concatenate([dot(values, w_mine), dot(values, w_other[...])], axis=1)

    split_tokens(total_of, keep, send, keep.shape[0], col)


def second_back_kernel(lengths, total, total_far, unit_ref, inverse_ref, kept, sent, top, top_far, middle_out, datt, sums):
    half = top.shape[1]
    got = total_far[...].astype(F32)
    grads = total[...].astype(F32) + jnp.concatenate([got[:, half:], got[:, :half]], axis=1)
    unit = unit_ref[...]
    scaled = grads * wide_vector(kept, sent, GAIN_M)
    mean_plain = jnp.mean(scaled, axis=1, keepdims=True)
    mean_unit = jnp.mean(scaled * unit, axis=1, keepdims=True)
    own = masked_top(lengths, top, top_far, lax.axis_index("col")).astype(F32)
    result = own + inverse_ref[:, :1] * (scaled - mean_plain - unit * mean_unit)
    middle_out[...] = result[:, :half]
    datt[...] = result.astype(BF16)
    sums[...] = jnp.zeros_like(sums)
    sums[0:1] = jnp.sum((grads * unit)[:, :half], axis=0, keepdims=True)
    sums[1:2] = jnp.sum(grads[:, :half], axis=0, keepdims=True)


def backward_kernel(bit_first, bit_second, lengths, own, other, w_mine, w_other, q_hbm, k_hbm, v_hbm, o_ref, lse, normed_hbm, w_kept, w_got,
                    first_keep, first_send, second_keep, second_send, keep, send, sums, datt, out, acc_k, acc_v, do_ref,
                    q_ref, k_ref, v_ref, normed, sems):
    copies = start_copies(
        [(q_hbm, q_ref), (k_hbm, k_ref), (v_hbm, v_ref), (normed_hbm, normed)], sems
    )
    own_rows, width = own.shape
    half = width // 2
    third = q_ref.shape[1]
    row, col = lax.axis_index("row"), lax.axis_index("col")
    quarter = half_rows(row, third)
    for ref, at in ((own, col), (other, 1 - col)):
        where = half_rows(at, own_rows)
        values = ref[...]
        datt[where] = values
        do_ref[where] = (
            dot_nt(values[:, :half], w_mine[quarter]) + dot_nt(values[:, half:], w_other[quarter])
        ).astype(BF16)
    for copy in copies:
        copy.wait()
    keys_t = k_ref[...].T
    acc_k[...] = jnp.zeros_like(acc_k)
    acc_v[...] = jnp.zeros_like(acc_v)
    scale = BF16(HEAD_DIM ** (-0.5))
    for begin in (0, own_rows):
        keys = begin + own_rows
        allowed = allowed_block(lengths, keys, begin, own_rows)
        query = q_ref[begin:keys] * scale
        grad_mixed = do_ref[begin:keys]
        parts = []
        for head in range(third // HEAD_DIM):
            mask = head_mask(third, head)
            key = jnp.where(mask, k_ref[:keys], BF16(0))
            scores = jnp.where(allowed, dot_nt(key, query), MASKED)
            probs = jnp.exp(scores - lse[head : head + 1, begin:keys])
            value = jnp.where(mask, v_ref[:keys], BF16(0))
            grad_probs = dot_nt(value, grad_mixed)
            both = probs * grad_probs
            inner = jnp.sum(both, axis=0, keepdims=True)
            grad_raw = (both - probs * inner).astype(BF16) * scale
            acc_v[:keys] += jnp.where(mask, dot(probs.astype(BF16), grad_mixed), 0.0)
            acc_k[:keys] += jnp.where(mask, dot(grad_raw, q_ref[begin:keys]), 0.0)
            parts.append(dot(keys_t[head * HEAD_DIM : (head + 1) * HEAD_DIM, :keys], grad_raw))
        out[begin:keys, :third] = jnp.concatenate(parts, axis=0).T.astype(BF16)
    out[:, third : 2 * third] = acc_k[...].astype(BF16)
    out[:, 2 * third :] = acc_v[...].astype(BF16)
    grads = out[...]
    weights = dot_tn(normed[...], grads).astype(BF16)
    grad_out = dot_tn(datt[...], o_ref[...]).astype(BF16)
    split_rows(weights[:, : 2 * third].reshape(2, half, 2 * third), first_keep, first_send, bit_first)
    last = jnp.concatenate([weights[:, 2 * third :], grad_out], axis=1)
    split_rows(last.reshape(2, half, 2 * third), second_keep, second_send, bit_second)

    def total_of(rows):
        values = out[rows]
        return jnp.concatenate([dot_nt(values, w_kept[:half]), dot_nt(values, w_got[:half])], axis=1)

    split_tokens(total_of, keep, send, own_rows, col)
    sums[...] = jnp.zeros_like(sums)
    sums[0:1, : 3 * third] = jnp.sum(grads.astype(F32), axis=0, keepdims=True)
    sums[1:2, :half] = jnp.sum(datt[:, :half].astype(F32), axis=0, keepdims=True)


def first_back_kernel(keep, got, raised_keep, raised_got, own, own_far, kept, sent, mine, raised, out, stats, unit_out, inverse_out):
    own_rows, half = mine.shape
    unit, inverse = normed_parts(both_halves(own, own_far))
    unit_out[...] = unit[:, :half]
    inverse_out[...] = jnp.broadcast_to(inverse, inverse_out.shape)
    grads = keep[...] + got[...].astype(F32)
    total = raised_keep[...] + raised_got[...].astype(F32)
    mine[...], raised[...] = grads[:, :half], total[:, :half]
    out[:own_rows] = grads[:, half:].astype(BF16)
    out[own_rows : 2 * own_rows] = total[:, half:].astype(BF16)
    scaled = grads * wide_vector(kept, sent, GAIN_A)
    plain = jnp.sum(scaled, axis=1, keepdims=True)
    crossed = jnp.sum(scaled * unit, axis=1, keepdims=True)
    lanes = lax.broadcasted_iota(jnp.int32, (1, 128), 1)
    both = jnp.where(lanes == 0, plain, jnp.where(lanes == 1, crossed, 0.0)).T[:8]
    stats[...] = both
    high = both.astype(BF16)
    low = (both - high.astype(F32)).astype(BF16)
    out[2 * own_rows :] = jnp.zeros((EXTRA, half), BF16)
    out[2 * own_rows :, :own_rows] = jnp.concatenate([high, low], axis=0)


def last_kernel(mine, raised, got, stats, unit_ref, inverse_ref, kept, middle, grad_middle, mid_sums, output, result, sums):
    own_rows, half = mine.shape
    unit = unit_ref[...]
    grads = mine[...] + got[:own_rows].astype(F32)
    pairs = got[2 * own_rows :, :own_rows].astype(F32)
    total = (stats[...] + (pairs[:8] + pairs[8:])) / (2 * half)
    columns = jnp.concatenate([total, jnp.zeros((120, total.shape[1]), F32)], axis=0).T
    grad_in = inverse_ref[:, :1] * (
        grads * vector_of(kept, GAIN_A) - columns[:, 0:1] - unit * columns[:, 1:2]
    )
    result[...] = (grad_middle[...] + grad_in).astype(BF16)
    far = got[own_rows : 2 * own_rows].astype(F32)
    output[...] = (middle[...] + (raised[...] + far) + vector_of(kept, BIAS_DOWN)).astype(BF16)
    sums[...] = jnp.zeros_like(sums)
    sums[0:1] = jnp.sum(grads * unit, axis=0, keepdims=True)
    sums[1:2] = jnp.sum(grads, axis=0, keepdims=True)
    sums[2:4] = mid_sums[0:2]


def bit_clear(bit):
    return (lax.axis_index("dp") // (1 << bit)) % 2 == 0


def total_of_pair(kept, got):
    return (kept[...].astype(F32) + got[...].astype(F32)).astype(BF16)


def halve_kernel(bit_a, bit_b, kept_a, got_a, kept_b, got_b, keep_a, send_a, keep_b, send_b):
    split_rows(total_of_pair(kept_a, got_a), keep_a, send_a, bit_a)
    split_rows(total_of_pair(kept_b, got_b), keep_b, send_b, bit_b)


def cross_kernel(bit, kept_a, got_a, kept_b, got_b, keep, to_dp, to_row, to_both):
    own = bit_clear(bit)
    half = keep.shape[1]
    for i, (kept, got) in enumerate(((kept_a, got_a), (kept_b, got_b))):
        total = total_of_pair(kept, got)
        low, high = total[:, :half], total[:, half:]
        here, there = jnp.where(own, low, high), jnp.where(own, high, low)
        keep[i], to_dp[i], to_row[i], to_both[i] = here[0], there[0], here[1], there[1]


def join_kernel(keep, from_dp_ref, from_row_ref, from_both_ref, out):
    mine = total_of_pair(keep, from_dp_ref)
    other = total_of_pair(from_row_ref, from_both_ref)
    for i in range(2):
        out[i, 0], out[i, 1] = mine[i], other[i]


def join_more_kernel(keep, from_dp_ref, from_row_ref, from_both_ref, halves, halves_col, mlp, attn, out):
    mine = total_of_pair(keep, from_dp_ref)
    other = total_of_pair(from_row_ref, from_both_ref)
    rows, half = mine.shape[1:]
    for i in range(2):
        out[2 * i * rows : (2 * i + 1) * rows] = mine[i]
        out[(2 * i + 1) * rows : (2 * i + 2) * rows] = other[i]
    third = half // 2
    lines = [
        (halves[...] + halves_col[...])[:4],
        jnp.concatenate([attn[0:1, :third], attn[0:1, 2 * third : 3 * third]], axis=1),
        attn[1:2, :half],
        mlp[0:1, :half],
        mlp[0:1, half : 2 * half],
        mlp[1:2, :half],
        jnp.zeros((EXTRA - 9, half), F32),
    ]
    out[4 * rows :] = jnp.concatenate(lines, axis=0).astype(BF16)


def extra_sum(mine, got):
    return mine[-EXTRA:].astype(F32) + got[-EXTRA:].astype(F32)


def ordered_rows(own, mine, got, begin, rows, out, at):
    low, high = mine[begin : begin + rows], got[begin : begin + rows]
    out[at : at + rows] = jnp.where(own, low, high)
    out[at + rows : at + 2 * rows] = jnp.where(own, high, low)


def part_more_kernel(bit, mine, got, out_a, out_b):
    own = bit_clear(bit)
    rows = out_b.shape[0] // 4
    for i, out in enumerate((out_a, out_b)):
        for p in range(2):
            ordered_rows(own, mine, got, (2 * i + p) * rows, rows, out, 2 * p * rows)
    out_a[4 * rows :] = extra_sum(mine, got).astype(BF16)


def double_more_kernel(bit_a, bit_b, mine_a, got_a, mine_b, got_b, out_a, out_b):
    rows = mine_b.shape[0] // 2
    for bit, mine, got, out in ((bit_a, mine_a, got_a, out_a), (bit_b, mine_b, got_b, out_b)):
        own = bit_clear(bit)
        for p in range(2):
            ordered_rows(own, mine, got, p * rows, rows, out, 2 * p * rows)
    out_a[4 * rows :] = extra_sum(mine_a, got_a).astype(BF16)


def doubled(bit, mine, got, out):
    own = bit_clear(bit)
    half = mine.shape[1]
    out[:, :half] = jnp.where(own, mine, got)
    out[:, half:] = jnp.where(own, got, mine)


def part_kernel(bit, mine, got, out_a, out_b):
    doubled(bit, mine[0], got[0], out_a)
    doubled(bit, mine[1], got[1], out_b)


def double_kernel(bit_a, bit_b, mine_a, got_a, mine_b, got_b, out_a, out_b):
    doubled(bit_a, mine_a[...], got_a[...], out_a)
    doubled(bit_b, mine_b[...], got_b[...], out_b)


def double_apart_kernel(bit_a, bit_b, mine_a, got_a, mine_b, got_b, *outs):
    for i in range(2):
        for bit, mine, got, out in ((bit_a, mine_a, got_a, outs[i]), (bit_b, mine_b, got_b, outs[2 + i])):
            own = bit_clear(bit)
            half = mine.shape[1]
            out[:half] = jnp.where(own, mine[i], got[i])
            out[half:] = jnp.where(own, got[i], mine[i])


def from_both(values, bit):
    count = lax.axis_size("dp")
    pairs = [(2 * i + r, 2 * (i ^ (1 << bit)) + 1 - r) for i in range(count) for r in range(2)]
    return lax.ppermute(values, ("dp", "row"), pairs)


class Pair:
    def __init__(self, keep_a, send_a, keep_b, send_b, bits_a, bits_b, apart):
        self.bits_a, self.bits_b = bits_a, bits_b
        self.apart = apart
        self.count = len(bits_a)
        self.stage = 0
        self.steps = 2 * self.count + apart
        self.state = (keep_a, from_dp(send_a, bits_a[0]), keep_b, from_dp(send_b, bits_b[0]))

    @property
    def on_last(self):
        return self.stage == self.steps - 1

    def step(self):
        self.stage += 1
        count, stage = self.count, self.stage
        last = self.bits_a[-1]
        if stage < count:
            rows, lanes = self.state[0].shape[1:]
            if stage < count - 1:
                bit_a, bit_b = self.bits_a[stage], self.bits_b[stage]
                keep_a, send_a, keep_b, send_b = call(
                    lambda *refs: halve_kernel(bit_a, bit_b, *refs),
                    (shape((2, rows // 2, lanes), BF16),) * 4,
                    *self.state,
                )
                self.state = (keep_a, from_dp(send_a, bit_a), keep_b, from_dp(send_b, bit_b))
            else:
                keep, to_dp, to_row, to_both = call(
                    lambda *refs: cross_kernel(last, *refs),
                    (shape((2, rows // 2, lanes), BF16),) * 4,
                    *self.state,
                )
                self.state = (keep, from_dp(to_dp, last), from_row(to_row), from_both(to_both, last))
        elif not self.apart:
            self.gather()
        elif stage == count:
            rows, lanes = self.state[0].shape[1:]
            mine = call(join_kernel, shape((2, 2, rows, lanes), BF16), *self.state)
            self.state = (mine, from_dp(mine, last))
        elif stage == 2 * count:
            mine_a, got_a, mine_b, got_b, next_a, next_b = self.state
            more_a, more_b = from_dp(next_a, self.bits_a[0]), from_dp(next_b, self.bits_b[0])
            self.state = (mine_a, got_a, mine_b, got_b, next_a, more_a, next_b, more_b)
        elif self.apart and stage == 2 * count - 1:
            rows, lanes = self.state[0].shape[-2:]
            before_a, before_b = self.bits_a[1], self.bits_b[1]
            a0, a1, b0, b1 = call(
                lambda *refs: double_apart_kernel(before_a, before_b, *refs),
                (shape((2 * rows, lanes), BF16),) * 4,
                *self.state,
            )
            self.state = (a0, from_dp(a0, self.bits_a[0]), b0, from_dp(b0, self.bits_b[0]), a1, b1)
        else:
            index = 2 * count - 1 - stage
            bit_a, bit_b = self.bits_a[index], self.bits_b[index]
            rows, lanes = self.state[0].shape[-2:]
            outs = (shape((2, 2 * rows, lanes), BF16),) * 2
            if stage == count + 1:
                mine_a, mine_b = call(lambda *refs: part_kernel(last, *refs), outs, *self.state)
            else:
                before_a, before_b = self.bits_a[index + 1], self.bits_b[index + 1]
                mine_a, mine_b = call(
                    lambda *refs: double_kernel(before_a, before_b, *refs), outs, *self.state
                )
            self.state = (mine_a, from_dp(mine_a, bit_a), mine_b, from_dp(mine_b, bit_b))


    def gather(self):
        count, stage = self.count, self.stage
        rows, lanes = self.state[0].shape[-2:]
        last = self.bits_a[-1]
        if stage == count:
            out = shape((4 * rows + EXTRA, lanes), BF16)
            mine = call(join_more_kernel, out, *self.state, *self.vectors)
            self.state = (mine, from_dp(mine, last))
            return
        index = 2 * count - 1 - stage
        if stage == count + 1:
            rows = rows - EXTRA
            kernel = lambda *refs: part_more_kernel(last, *refs)
        else:
            rows = 2 * (rows - EXTRA)
            before_a, before_b = self.bits_a[index + 1], self.bits_b[index + 1]
            kernel = lambda *refs: double_more_kernel(before_a, before_b, *refs)
        outs = (shape((rows + EXTRA, lanes), BF16), shape((rows, lanes), BF16))
        mine_a, mine_b = call(kernel, outs, *self.state)
        got_a, got_b = from_dp(mine_a, self.bits_a[index]), from_dp(mine_b, self.bits_b[index])
        self.state = (mine_a, got_a, mine_b, got_b)


def arrived(pairs, *others):
    states, others = lax.optimization_barrier(([pair.state for pair in pairs], others))
    for pair, state in zip(pairs, states):
        pair.state = state
    return others


def ordered_halves(bit, mine, got):
    own = (lax.axis_index("dp") // (1 << bit)) % 2 == 0
    return jnp.concatenate(
        [jnp.where(own, mine, got), jnp.where(own, got, mine)], axis=0
    )


def by_row(mine, far, axis):
    first = lax.axis_index("row") == 0
    return jnp.concatenate(
        [jnp.where(first, mine, far), jnp.where(first, far, mine)], axis=axis
    )


def feed_end_kernel(bit, mine_0, got_0, mine_1, got_1, out):
    own = (lax.axis_index("dp") // (1 << bit)) % 2
    here = pl.program_id(1) == own
    near = pl.program_id(0) == lax.axis_index("row")
    part = jnp.where(
        near,
        jnp.where(here, mine_0[...], got_0[...]),
        jnp.where(here, mine_1[...], got_1[...]),
    )
    out[...] = part.astype(F32)


def attention_end(bit, flip, mine, got, left, right):
    rows, half = left.shape[0], left.shape[1]
    own = bit_clear(bit)
    part = rows // 2
    sides = []
    for p in range(2):
        low, high = mine[p * part : (p + 1) * part], got[p * part : (p + 1) * part]
        sides.append(jnp.concatenate([jnp.where(own, low, high), jnp.where(own, high, low)], axis=0))
    near, far = sides
    third = half // 2
    left[...] = by_row(near[:, :third], far[:, :third], 1).astype(F32)
    last = by_row(near[:, third:], far[:, third:], 1).astype(F32)
    right[...] = last.T if flip else last


def first_end_kernel(bit, mine, got, left, right, small):
    attention_end(bit, False, mine, got, left, right)
    small[...] = extra_sum(mine, got)


def second_end_kernel(bit, mine, got, left, right):
    attention_end(bit, True, mine, got, left, right)


def end_call(kernel, grid, out_shape, block, index, *operands):
    whole = pl.BlockSpec(memory_space=pltpu.VMEM)
    return pl.pallas_call(
        kernel,
        grid=grid,
        out_shape=out_shape,
        in_specs=[whole] * len(operands),
        out_specs=pl.BlockSpec(block, index),
        compiler_params=pltpu.CompilerParams(vmem_limit_bytes=16 * MIB),
    )(*operands)


def body(
    tokens,
    out_grad,
    seq_lengths,
    w_query,
    w_key,
    w_value,
    w_out,
    w_up,
    w_down,
    b_query,
    b_value,
    b_out,
    b_up,
    b_down,
    gain_attn,
    shift_attn,
    gain_mlp,
    shift_mlp,
):
    row = lax.axis_index("row")
    own_rows, half = tokens.shape
    width = 2 * half
    rows = 2 * own_rows
    third = w_query.shape[1] // 2
    units = w_up.shape[1] // 2
    side = lax.axis_index("dp") % 2
    count = lax.axis_size("dp").bit_length() - 1
    bits = list(range(count))
    turned = [1, 0] + bits[2:] if count > 1 else bits
    tall = shape((own_rows, width), F32)
    tall_low = shape((own_rows, width), BF16)
    column = shape((own_rows, 128), F32)
    pair_sums = shape((8, half), F32)

    tokens_far = from_row(tokens)
    vectors = (gain_attn, shift_attn, b_out, gain_mlp, shift_mlp, b_query, b_value, b_up, b_down)
    block = pltpu.VMEM((half, 2 * third), BF16)
    w_kept, sent, sent_out, sent_up, sent_down = call(
        start_kernel,
        (
            shape((half + EXTRA, 3 * third), BF16),
            shape((half + EXTRA, 3 * third), BF16),
            shape((w_out.shape[0] // 2, half), BF16),
            shape((half // 2, units), BF16),
            shape((units // 2, half), BF16),
        ),
        *vectors, w_query, w_key, w_value, w_out, w_up, w_down,
        hbm=range(15),
        scratch=[pltpu.VMEM(x.shape, x.dtype) for x in vectors]
        + [block, block, block, pltpu.VMEM((EXTRA, 3 * third), F32), pltpu.SemaphoreType.DMA((15,))],
        vmem=VMEM_START,
    )
    tokens_far, sent, sent_out = hold(tokens_far, sent, sent_out)
    w_got = from_row(sent)
    out_got = from_row(sent_out)
    tokens_col = from_col(tokens)
    tokens_far_col = from_col(tokens_far)
    top_col = from_col(out_grad)
    tokens_far, tokens_col, tokens_far_col, w_got, out_got, sent_up, sent_down = hold(
        tokens_far, tokens_col, tokens_far_col, w_got, out_got, sent_up, sent_down
    )
    up_got = from_row(sent_up)
    down_got = from_row(sent_down)
    out_side = from_dp(out_got, 0)
    every_token = (tokens, tokens_far, tokens_col, tokens_far_col)

    like = shape((rows, third), BF16)
    normed_all, query, key, value, mixed, lse = call(
        forward_kernel,
        (shape((rows, width), BF16), like, like, like, like, shape((8, rows), F32)),
        seq_lengths,
        *every_token,
        w_kept,
        w_got,
        smem=(0,),
        hbm_out=range(4),
        scratch=[pltpu.VMEM((rows, width), BF16)]
        + [pltpu.VMEM((rows, third), BF16)] * 3
        + [pltpu.SemaphoreType.DMA((4,))],
    )
    mixed_far = from_row(mixed)
    mixed_gate, up_got = hold(mixed, up_got)
    up_side = from_dp(up_got, 0)
    mixed_far, out_side, up_side, down_got, out_grad_send = hold(
        mixed_far, out_side, up_side, down_got, out_grad
    )

    keep, send, w_out_far = call(
        branch_kernel,
        (shape((rows, width), F32), shape((rows, width), BF16), shape(w_out.shape, BF16)),
        mixed_gate, mixed_far, w_out, out_got, out_side,
    )
    got = from_col(send)
    top_far = from_row(out_grad_send)
    down_side = from_dp(down_got, 1)
    (got,) = hold(got)

    middle, normed_mlp_all, unit_mlp, inverse_mlp = call(
        second_norm_kernel,
        (shape((own_rows, half), F32), shape((rows, width), BF16), tall, column),
        *every_token, keep, got, w_kept, w_got,
    )
    hidden, slope, w_up_far = call(
        up_kernel,
        (shape((rows, units), BF16), shape((rows, units), F32), shape((half, units), BF16)),
        normed_mlp_all, w_up, up_got, up_side, w_kept,
    )
    hidden, top_far = hold(hidden, top_far)
    top_far_col = from_col(top_far)
    top_far_col, down_side = hold(top_far_col, down_side)

    split_down = shape((2, units // 2, half), BF16)
    split_up = shape((2, half, units // 2), BF16)
    down_keep, down_send, up_keep, up_send, keep, send, mlp_sums, w_down_far = call(
        lambda *refs: down_kernel(bits[0], turned[0], *refs),
        (
            split_down, split_down, split_up, split_up, tall, tall_low,
            shape((8, units), F32), shape((units, half), BF16),
        ),
        seq_lengths, out_grad, top_far, top_col, top_far_col, hidden, slope, normed_mlp_all,
        w_down, down_got, down_side, w_up, w_up_far,
        scratch=[pltpu.VMEM((rows, width), BF16), pltpu.VMEM((rows, units), BF16)],
        smem=(0,),
    )
    got = from_col(send)
    feed = Pair(down_keep, down_send, up_keep, up_send, bits, turned, True)
    (got,) = hold(got)

    total = (keep + got.astype(F32)).astype(BF16)
    total_far = from_row(total)
    keep, send = call(
        output_kernel, (tall, tall_low), hidden, w_down, w_down_far,
    )
    got = from_col(send)
    total_far, got = hold(total_far, got)

    grad_middle, datt, mid_sums = call(
        second_back_kernel,
        (shape((own_rows, half), F32), tall_low, pair_sums),
        seq_lengths, total, total_far, unit_mlp, inverse_mlp, w_kept, w_got, out_grad, top_far,
        smem=(0,),
    )
    datt_col = from_col(datt)
    raised_keep, raised_got = keep, got
    (datt_col,) = arrived([feed], datt_col)
    feed.step()

    split_pair = shape((2, half // 2, 2 * third), BF16)
    first_keep, first_send, second_keep, second_send, keep, send, attn_sums = call(
        lambda *refs: backward_kernel(bits[0], turned[0], *refs),
        (split_pair,) * 4 + (tall, tall_low, shape((8, width), F32)),
        seq_lengths, datt, datt_col, w_out, w_out_far, query, key, value, mixed, lse,
        normed_all, w_kept, w_got,
        scratch=[
            pltpu.VMEM((rows, width), BF16),
            pltpu.VMEM((rows, 3 * third), BF16),
            pltpu.VMEM((rows, third), F32),
            pltpu.VMEM((rows, third), F32),
        ]
        + [pltpu.VMEM((rows, third), BF16)] * 4
        + [pltpu.VMEM((rows, width), BF16), pltpu.SemaphoreType.DMA((4,))],
        smem=(0,),
        hbm=(5, 6, 7, 10),
    )
    keep, send = arrived([feed], keep, send)
    got = from_col(send)
    attention = Pair(first_keep, first_send, second_keep, second_send, bits, turned, False)
    pairs = [feed, attention]
    feed.step()
    (got,) = arrived(pairs, got)

    mine, raised, out, stats, unit_attn, inverse_attn = call(
        first_back_kernel,
        (
            shape((own_rows, half), F32),
            shape((own_rows, half), F32),
            shape((rows + EXTRA, half), BF16),
            shape((8, own_rows), F32),
            shape((own_rows, half), F32),
            column,
        ),
        keep, got, raised_keep, raised_got, tokens, tokens_far, w_kept, w_got,
    )
    got = from_row(out)
    feed.step()
    attention.step()
    (got,) = arrived(pairs, got)

    output, input_grad, halves = call(
        last_kernel,
        (shape((own_rows, half), BF16), shape((own_rows, half), BF16), pair_sums),
        mine, raised, got, stats, unit_attn, inverse_attn, w_kept, middle, grad_middle, mid_sums,
    )
    halves_col = from_col(halves)
    feed.step()
    attention.step()
    (halves_col,) = arrived(pairs, halves_col)
    attention.vectors = (halves, halves_col, mlp_sums, attn_sums)
    while not attention.on_last:
        moving = [pair for pair in pairs if not pair.on_last]
        for pair in moving:
            pair.step()
        arrived(moving)

    wide = w_query.shape[1]
    outs = (shape((half, wide), F32),) * 2
    mine_a, got_a, mine_b, got_b = attention.state
    grad_query, grad_key, small = call(
        lambda *refs: first_end_kernel(bits[0], *refs),
        outs + (shape((EXTRA, half), F32),),
        mine_a,
        got_a,
    )
    grad_value, grad_out = call(
        lambda *refs: second_end_kernel(turned[0], *refs), outs, mine_b, got_b
    )
    a_0, got_a_0, b_0, got_b_0, a_1, got_a_1, b_1, got_b_1 = feed.state
    grad_down = end_call(
        lambda *refs: feed_end_kernel(bits[0], *refs),
        (2, 2),
        shape((2 * units, half), F32),
        (units // 2, half),
        lambda i, j: (2 * i + j, 0),
        a_0,
        got_a_0,
        a_1,
        got_a_1,
    )
    grad_up = end_call(
        lambda *refs: feed_end_kernel(turned[0], *refs),
        (2, 2),
        shape((half, 2 * units), F32),
        (half, units // 2),
        lambda i, j: (0, 2 * i + j),
        b_0,
        got_b_0,
        b_1,
        got_b_1,
    )
    return (
        output,
        input_grad,
        grad_query,
        grad_key,
        grad_value,
        grad_out,
        grad_up,
        grad_down,
        small[4, :third],
        small[4, third:],
        small[5],
        small[6:8].reshape(-1),
        small[8],
        small[0],
        small[1],
        small[2],
        small[3],
    )


def solution(mesh):
    return jax.shard_map(
        body,
        mesh=mesh,
        in_specs=(
            P(("dp", "col"), "row"),
            P(("dp", "col"), "row"),
            P("dp", None),
            P("row", "col"),
            P("row", "col"),
            P("row", "col"),
            P("col", "row"),
            P("row", "col"),
            P("col", "row"),
            P(("col", "row")),
            P(("col", "row")),
            P("row"),
            P(("col", "row")),
            P("row"),
            P("row"),
            P("row"),
            P("row"),
            P("row"),
        ),
        out_specs=(
            P(("dp", "col"), "row"),
            P(("dp", "col"), "row"),
            P("row", "col"),
            P("row", "col"),
            P("row", "col"),
            P("col", "row"),
            P("row", "col"),
            P("col", "row"),
            P(("col", "row")),
            P(("col", "row")),
            P("row"),
            P(("col", "row")),
            P("row"),
            P("row"),
            P("row"),
            P("row"),
            P("row"),
        ),
        check_vma=False,
    )
```

```python
import jax
import jax.numpy as jnp
from jax import lax
from jax.experimental import pallas as pl
from jax.experimental.pallas import tpu as pltpu
from jax.sharding import PartitionSpec as P

HEAD_DIM = 64
EPSILON = 1e-05
MASKED = -1e30
F32 = jnp.float32
BF16 = jnp.bfloat16
SWAP = ((0, 1), (1, 0))
CUBIC = 0.044715
ROOT = 0.7978845608028654
MIB = 1024 * 1024
VMEM_START = 54
EXTRA = 16


def dot(left, right):
    return jnp.dot(left, right, preferred_element_type=F32)


def dot_nt(left, right):
    return lax.dot_general(left, right, (((1,), (1,)), ((), ())), preferred_element_type=F32)


def dot_tn(left, right):
    return lax.dot_general(left, right, (((0,), (0,)), ((), ())), preferred_element_type=F32)


def from_row(values):
    return lax.ppermute(values, "row", SWAP)


def from_col(values):
    return lax.ppermute(values, "col", SWAP)


def dp_pairs(bit):
    count = lax.axis_size("dp")
    return [(i, i ^ (1 << bit)) for i in range(count)]


def from_dp(values, bit):
    return lax.ppermute(values, "dp", dp_pairs(bit))


def hold(*values):
    return lax.optimization_barrier(values)


def shape(dims, kind):
    return jax.ShapeDtypeStruct(tuple(dims), kind)


def call(kernel, out_shape, *operands, scratch=(), smem=(), hbm=(), hbm_out=(), vmem=16):
    spaces = [
        pltpu.SMEM if i in smem else pltpu.HBM if i in hbm else pltpu.VMEM
        for i in range(len(operands))
    ]
    out_specs = jax.tree.map(lambda _: pl.BlockSpec(memory_space=pltpu.VMEM), out_shape)
    if hbm_out:
        out_specs = tuple(
            pl.BlockSpec(memory_space=pltpu.HBM if i in hbm_out else pltpu.VMEM)
            for i in range(len(out_shape))
        )
    return pl.pallas_call(
        kernel,
        out_shape=out_shape,
        in_specs=[pl.BlockSpec(memory_space=space) for space in spaces],
        out_specs=out_specs,
        scratch_shapes=list(scratch),
        compiler_params=pltpu.CompilerParams(vmem_limit_bytes=vmem * MIB),
        cost_estimate=pl.CostEstimate(flops=0, bytes_accessed=0, transcendentals=0),
    )(*operands)


def half_rows(index, size):
    return pl.ds(pl.multiple_of(index * size, size), size)


def start_copies(pairs, sems):
    copies = [
        pltpu.make_async_copy(source, target, sems.at[i]) for i, (source, target) in enumerate(pairs)
    ]
    for copy in copies:
        copy.start()
    return copies


GAIN_A, SHIFT_A, BIAS_O, GAIN_M, SHIFT_M, BIAS_QKV, BIAS_UP, BIAS_DOWN = 0, 1, 2, 3, 4, 5, 6, 8


def start_kernel(*refs):
    vectors, (w_q, w_k, w_v, w_out, w_up, w_down) = refs[:9], refs[9:15]
    kept, sent, out_sent, up_sent, down_sent = refs[15:20]
    held, held_w, extra, sems = refs[20:29], refs[29:32], refs[32], refs[33]
    row, side = lax.axis_index("row"), lax.axis_index("dp") % 2
    other_side = (lax.axis_index("dp") // 2) % 2
    units = up_sent.shape[1]
    copies = start_copies(
        list(zip((w_q, w_k, w_v), held_w))
        + list(zip(vectors, held))
        + [
            (w_out.at[half_rows(side, out_sent.shape[0])], out_sent),
            (w_up.at[half_rows(side, up_sent.shape[0]), half_rows(1 - row, units)], up_sent),
            (w_down.at[half_rows(2 * (1 - row) + other_side, down_sent.shape[0])], down_sent),
        ],
        sems,
    )
    first = row == 0
    half, third = w_q.shape[0], w_q.shape[1] // 2
    part = half // 2
    keeps, sends = [], []
    for ref, copy in zip(held_w, copies):
        copy.wait()
        low, high = ref[:, :third], ref[:, third:]
        keeps.append(jnp.where(first, low, high))
        away = jnp.where(first, high, low)
        sends.append(jnp.where(side == 0, away[:part], away[part:]))
    kept[:half] = jnp.concatenate(keeps, axis=1)
    sent[:part] = jnp.concatenate(sends, axis=1)
    for copy in copies[3:]:
        copy.wait()
    extra[...] = jnp.zeros_like(extra)
    lines = [ref[...].astype(F32).reshape(1, -1) for ref in held]
    for i in range(5):
        extra[i : i + 1, :half] = lines[i]
    b_q, b_v, b_u, b_d = lines[5:]
    extra[BIAS_QKV : BIAS_QKV + 1, :third] = b_q
    extra[BIAS_QKV : BIAS_QKV + 1, 2 * third :] = b_v
    for i in range(2):
        extra[BIAS_UP + i : BIAS_UP + i + 1, :half] = b_u[:, i * half : (i + 1) * half]
    extra[BIAS_DOWN : BIAS_DOWN + 1, :half] = b_d
    kept[half:] = extra[...].astype(BF16)
    sent[part:] = extra[...].astype(BF16)


def normed_parts(values):
    mean = jnp.mean(values, axis=1, keepdims=True)
    centered = values - mean
    variance = jnp.mean(centered * centered, axis=1, keepdims=True)
    inverse = lax.rsqrt(variance + EPSILON)
    return centered * inverse, inverse


def both_halves(mine, far):
    return jnp.concatenate([mine[...], far[...]], axis=1).astype(F32)


def vector_of(kept, i):
    return kept[kept.shape[0] - EXTRA :].astype(F32)[i : i + 1, : 2 * kept.shape[1] // 3]


def wide_vector(kept, got, i):
    return jnp.concatenate([vector_of(kept, i), vector_of(got, i)], axis=1)


def head_mask(width, head):
    lanes = lax.broadcasted_iota(jnp.int32, (1, width), 1)
    return lanes // HEAD_DIM == head


def allowed_block(lengths, keys, first_query, count):
    first, second = lengths[0, 0], lengths[0, 0] + lengths[0, 1]
    query = first_query + lax.broadcasted_iota(jnp.int32, (1, count), 1)
    begin = jnp.where(query >= second, second, jnp.where(query >= first, first, 0))
    key = lax.broadcasted_iota(jnp.int32, (keys, count), 0)
    return (key >= begin) & (key <= query)


def weights_got(got, got_side):
    part = got.shape[0] - EXTRA
    first = lax.axis_index("dp") % 2 == 0
    here, there = got[:part], got_side[:part]
    return jnp.concatenate([jnp.where(first, here, there), jnp.where(first, there, here)], axis=0)


def forward_kernel(lengths, own, own_far, col_own, col_far, w_kept, got, got_side, norm_hbm, q_hbm, k_hbm, v_hbm, o_out, lse,
                   norm_out, q_out, k_out, v_out, sems):
    own_rows, half = own.shape
    w_got = weights_got(got, got_side)
    third = q_out.shape[1]
    col = lax.axis_index("col")
    gain, shift = wide_vector(w_kept, got, GAIN_A), wide_vector(w_kept, got, SHIFT_A)
    bias = w_kept[half:].astype(F32)[BIAS_QKV : BIAS_QKV + 1]
    for ref, far, at in ((own, own_far, col), (col_own, col_far, 1 - col)):
        where = half_rows(at, own_rows)
        unit, _ = normed_parts(both_halves(ref, far))
        values = (unit * gain + shift).astype(BF16)
        norm_out[where] = values
        total = dot(values[:, :half], w_kept[:half]) + dot(values[:, half:], w_got)
        total = (total + bias).astype(BF16)
        q_out[where] = total[:, :third]
        k_out[where] = total[:, third : 2 * third]
        v_out[where] = total[:, 2 * third :]
    copies = start_copies(
        [(norm_out, norm_hbm), (q_out, q_hbm), (k_out, k_hbm), (v_out, v_hbm)], sems
    )
    lse[...] = jnp.zeros_like(lse)
    values_t = v_out[...].T
    for begin in (0, own_rows):
        keys = begin + own_rows
        allowed = allowed_block(lengths, keys, begin, own_rows)
        query = q_out[begin:keys] * BF16(HEAD_DIM ** (-0.5))
        parts = []
        for head in range(third // HEAD_DIM):
            key = jnp.where(head_mask(third, head), k_out[:keys], BF16(0))
            scores = jnp.where(allowed, dot_nt(key, query), MASKED)
            largest = jnp.max(scores, axis=0, keepdims=True)
            weights = jnp.exp(scores - largest)
            summed = jnp.sum(weights, axis=0, keepdims=True)
            lse[head : head + 1, begin:keys] = largest + jnp.log(summed)
            mixed = dot(
                values_t[head * HEAD_DIM : (head + 1) * HEAD_DIM, :keys], weights.astype(BF16)
            )
            parts.append(mixed / summed)
        o_out[begin:keys] = jnp.concatenate(parts, axis=0).T.astype(BF16)
    for copy in copies:
        copy.wait()


def split_tokens(total_of, keep, send, own_rows, col):
    keep[...] = total_of(half_rows(col, own_rows))
    send[...] = total_of(half_rows(1 - col, own_rows)).astype(BF16)


def branch_kernel(mixed, mixed_other, w_mine, got, got_side, keep, send, w_other):
    w_other[...] = both_sides(got, got_side, 0)
    row = lax.axis_index("row")
    third = mixed.shape[1]
    own, far = half_rows(row, third), half_rows(1 - row, third)

    for i, w in enumerate((w_mine, w_other)):
        lanes = slice(i * w.shape[1], (i + 1) * w.shape[1])
        part = dot(mixed[...], w[own]) + dot(mixed_other[...], w[far])
        keep[:, lanes] = part
        send[:, lanes] = part.astype(BF16)


def second_norm_kernel(own, own_far, col_own, col_far, keep, got, kept, sent, middle, normed, unit_out, inverse_out):
    own_rows = own.shape[0]
    col = lax.axis_index("col")
    bias, gain, shift = [wide_vector(kept, sent, i) for i in (BIAS_O, GAIN_M, SHIFT_M)]
    for ref, far, at in ((own, own_far, col), (col_own, col_far, 1 - col)):
        where = half_rows(at, own_rows)
        values = both_halves(ref, far) + (keep[where] + got[where].astype(F32) + bias)
        unit, inverse = normed_parts(values)
        normed[where] = (unit * gain + shift).astype(BF16)
        if ref is own:
            middle[...] = values[:, : middle.shape[1]]
            unit_out[...] = unit
            inverse_out[...] = jnp.broadcast_to(inverse, inverse_out.shape)


def both_sides(got, got_side, axis, bit=0):
    first = (lax.axis_index("dp") // (1 << bit)) % 2 == 0
    low = jnp.where(first, got[...], got_side[...])
    high = jnp.where(first, got_side[...], got[...])
    return jnp.concatenate([low, high], axis=axis)


def up_kernel(normed, w_up, got, got_side, kept, hidden_out, slope_out, w_other_out):
    rows, width = normed.shape
    half = width // 2
    units = got.shape[1]
    row = lax.axis_index("row")
    w_mine = w_up[:, pl.ds(pl.multiple_of(row * units, units), units)]
    w_other = both_sides(got, got_side, 0)
    w_other_out[...] = w_other
    bias = jnp.concatenate([vector_of(kept, BIAS_UP + i) for i in range(2)], axis=1)
    for begin in (0, rows // 2):
        where = slice(begin, begin + rows // 2)
        values = normed[where]
        u = dot(values[:, :half], w_mine) + dot(values[:, half:], w_other) + bias
        squared = u * u
        bent = jnp.tanh(ROOT * (u + CUBIC * (squared * u)))
        raised = 0.5 * (1.0 + bent)
        hidden_out[where] = (u * raised).astype(BF16)
        slope_out[where] = raised + 0.5 * u * (1.0 - bent * bent) * (
            ROOT * (1.0 + (3.0 * CUBIC) * squared)
        )


def split_rows(total, keep, send, bit):
    own = (lax.axis_index("dp") // (1 << bit)) % 2 == 0
    half = keep.shape[-2]
    low, high = total[..., :half, :], total[..., half:, :]
    keep[...] = jnp.where(own, low, high)
    send[...] = jnp.where(own, high, low)


def masked_top(lengths, mine, far, at):
    live = lengths[0, 0] + lengths[0, 1]
    own_rows = mine.shape[0]
    position = at * own_rows + lax.broadcasted_iota(jnp.int32, (own_rows, 1), 0)
    values = jnp.concatenate([mine[...], far[...]], axis=1)
    return jnp.where(position < live, values, BF16(0))


def down_kernel(bit_down, bit_up, lengths, top, top_far, top_col, top_far_col, hidden, slope, normed, w_down, got, got_side,
                w_up, w_up_other, down_keep, down_send, up_keep, up_send, keep, send, sums, w_other_out, top_all, grad_pre):
    own_rows, half = top.shape
    units = hidden.shape[1]
    row, col = lax.axis_index("row"), lax.axis_index("col")
    top_all[half_rows(col, own_rows)] = masked_top(lengths, top, top_far, col)
    top_all[half_rows(1 - col, own_rows)] = masked_top(lengths, top_col, top_far_col, 1 - col)
    top_rows = top_all[...]
    total = dot_tn(hidden[...], top_rows).astype(BF16)
    split_rows(jnp.stack([total[:, :half], total[:, half:]]), down_keep, down_send, bit_down)
    w_other = both_sides(got, got_side, 0, 1)
    w_other_out[...] = w_other
    grad_hidden = dot_nt(top_rows[:, :half], w_down[half_rows(row, units)]) + dot_nt(
        top_rows[:, half:], w_other
    )
    grads = (grad_hidden * slope[...]).astype(BF16)
    grad_pre[...] = grads
    w_mine = w_up[:, pl.ds(pl.multiple_of(row * units, units), units)]

    def total_of(rows):
        values = grad_pre[rows]
        return jnp.concatenate([dot_nt(values, w_mine), dot_nt(values, w_up_other[...])], axis=1)

    split_tokens(total_of, keep, send, own_rows, col)
    total = dot_tn(normed[...], grads).astype(BF16)
    total = total.reshape(2, half, units)
    total = jnp.concatenate([total[..., : units // 2], total[..., units // 2 :]], axis=1)
    split_rows(total, up_keep, up_send, bit_up)
    sums[...] = jnp.zeros_like(sums)
    sums[0:1] = jnp.sum(grads.astype(F32), axis=0, keepdims=True)
    sums[1:2, :half] = jnp.sum(top_rows[:, :half].astype(F32), axis=0, keepdims=True)


def output_kernel(hidden, w_down, w_other, keep, send):
    units = hidden.shape[1]
    row, col = lax.axis_index("row"), lax.axis_index("col")
    w_mine = w_down[half_rows(row, units)]

    def total_of(rows):
        values = hidden[rows]
        return jnp.concatenate([dot(values, w_mine), dot(values, w_other[...])], axis=1)

    split_tokens(total_of, keep, send, keep.shape[0], col)


def second_back_kernel(lengths, total, total_far, unit_ref, inverse_ref, kept, sent, top, top_far, middle_out, datt, sums):
    half = top.shape[1]
    got = total_far[...].astype(F32)
    grads = total[...].astype(F32) + jnp.concatenate([got[:, half:], got[:, :half]], axis=1)
    unit = unit_ref[...]
    scaled = grads * wide_vector(kept, sent, GAIN_M)
    mean_plain = jnp.mean(scaled, axis=1, keepdims=True)
    mean_unit = jnp.mean(scaled * unit, axis=1, keepdims=True)
    own = masked_top(lengths, top, top_far, lax.axis_index("col")).astype(F32)
    result = own + inverse_ref[:, :1] * (scaled - mean_plain - unit * mean_unit)
    middle_out[...] = result[:, :half]
    datt[...] = result.astype(BF16)
    sums[...] = jnp.zeros_like(sums)
    sums[0:1] = jnp.sum((grads * unit)[:, :half], axis=0, keepdims=True)
    sums[1:2] = jnp.sum(grads[:, :half], axis=0, keepdims=True)


def backward_kernel(bit_first, bit_second, lengths, own, other, w_mine, w_other, q_hbm, k_hbm, v_hbm, o_ref, lse, normed_hbm, w_kept, got, got_side,
                    first_keep, first_send, second_keep, second_send, keep, send, sums, datt, out, acc_k, acc_v, do_ref,
                    q_ref, k_ref, v_ref, normed, sems):
    copies = start_copies(
        [(q_hbm, q_ref), (k_hbm, k_ref), (v_hbm, v_ref), (normed_hbm, normed)], sems
    )
    own_rows, width = own.shape
    half = width // 2
    third = q_ref.shape[1]
    row, col = lax.axis_index("row"), lax.axis_index("col")
    quarter = half_rows(row, third)
    for ref, at in ((own, col), (other, 1 - col)):
        where = half_rows(at, own_rows)
        values = ref[...]
        datt[where] = values
        do_ref[where] = (
            dot_nt(values[:, :half], w_mine[quarter]) + dot_nt(values[:, half:], w_other[quarter])
        ).astype(BF16)
    for copy in copies:
        copy.wait()
    keys_t = k_ref[...].T
    acc_k[...] = jnp.zeros_like(acc_k)
    acc_v[...] = jnp.zeros_like(acc_v)
    scale = BF16(HEAD_DIM ** (-0.5))
    for begin in (0, own_rows):
        keys = begin + own_rows
        allowed = allowed_block(lengths, keys, begin, own_rows)
        query = q_ref[begin:keys] * scale
        grad_mixed = do_ref[begin:keys]
        parts = []
        for head in range(third // HEAD_DIM):
            mask = head_mask(third, head)
            key = jnp.where(mask, k_ref[:keys], BF16(0))
            scores = jnp.where(allowed, dot_nt(key, query), MASKED)
            probs = jnp.exp(scores - lse[head : head + 1, begin:keys])
            value = jnp.where(mask, v_ref[:keys], BF16(0))
            grad_probs = dot_nt(value, grad_mixed)
            both = probs * grad_probs
            inner = jnp.sum(both, axis=0, keepdims=True)
            grad_raw = (both - probs * inner).astype(BF16) * scale
            acc_v[:keys] += jnp.where(mask, dot(probs.astype(BF16), grad_mixed), 0.0)
            acc_k[:keys] += jnp.where(mask, dot(grad_raw, q_ref[begin:keys]), 0.0)
            parts.append(dot(keys_t[head * HEAD_DIM : (head + 1) * HEAD_DIM, :keys], grad_raw))
        out[begin:keys, :third] = jnp.concatenate(parts, axis=0).T.astype(BF16)
    out[:, third : 2 * third] = acc_k[...].astype(BF16)
    out[:, 2 * third :] = acc_v[...].astype(BF16)
    grads = out[...]
    weights = dot_tn(normed[...], grads).astype(BF16)
    grad_out = dot_tn(datt[...], o_ref[...]).astype(BF16)
    split_rows(weights[:, : 2 * third].reshape(2, half, 2 * third), first_keep, first_send, bit_first)
    last = jnp.concatenate([weights[:, 2 * third :], grad_out], axis=1)
    split_rows(last.reshape(2, half, 2 * third), second_keep, second_send, bit_second)

    w_got = weights_got(got, got_side)

    def total_of(rows):
        values = out[rows]
        return jnp.concatenate([dot_nt(values, w_kept[:half]), dot_nt(values, w_got)], axis=1)

    split_tokens(total_of, keep, send, own_rows, col)
    sums[...] = jnp.zeros_like(sums)
    sums[0:1, : 3 * third] = jnp.sum(grads.astype(F32), axis=0, keepdims=True)
    sums[1:2, :half] = jnp.sum(datt[:, :half].astype(F32), axis=0, keepdims=True)


def first_back_kernel(keep, got, raised_keep, raised_got, own, own_far, kept, sent, mine, raised, out, stats, unit_out, inverse_out):
    own_rows, half = mine.shape
    unit, inverse = normed_parts(both_halves(own, own_far))
    unit_out[...] = unit[:, :half]
    inverse_out[...] = jnp.broadcast_to(inverse, inverse_out.shape)
    grads = keep[...] + got[...].astype(F32)
    total = raised_keep[...] + raised_got[...].astype(F32)
    mine[...], raised[...] = grads[:, :half], total[:, :half]
    out[:own_rows] = grads[:, half:].astype(BF16)
    out[own_rows : 2 * own_rows] = total[:, half:].astype(BF16)
    scaled = grads * wide_vector(kept, sent, GAIN_A)
    plain = jnp.sum(scaled, axis=1, keepdims=True)
    crossed = jnp.sum(scaled * unit, axis=1, keepdims=True)
    lanes = lax.broadcasted_iota(jnp.int32, (1, 128), 1)
    both = jnp.where(lanes == 0, plain, jnp.where(lanes == 1, crossed, 0.0)).T[:8]
    stats[...] = both
    high = both.astype(BF16)
    low = (both - high.astype(F32)).astype(BF16)
    out[2 * own_rows :] = jnp.zeros((EXTRA, half), BF16)
    out[2 * own_rows :, :own_rows] = jnp.concatenate([high, low], axis=0)


def last_kernel(mine, raised, got, stats, unit_ref, inverse_ref, kept, middle, grad_middle, mid_sums, output, result, sums):
    own_rows, half = mine.shape
    unit = unit_ref[...]
    grads = mine[...] + got[:own_rows].astype(F32)
    pairs = got[2 * own_rows :, :own_rows].astype(F32)
    total = (stats[...] + (pairs[:8] + pairs[8:])) / (2 * half)
    columns = jnp.concatenate([total, jnp.zeros((120, total.shape[1]), F32)], axis=0).T
    grad_in = inverse_ref[:, :1] * (
        grads * vector_of(kept, GAIN_A) - columns[:, 0:1] - unit * columns[:, 1:2]
    )
    result[...] = (grad_middle[...] + grad_in).astype(BF16)
    far = got[own_rows : 2 * own_rows].astype(F32)
    output[...] = (middle[...] + (raised[...] + far) + vector_of(kept, BIAS_DOWN)).astype(BF16)
    sums[...] = jnp.zeros_like(sums)
    sums[0:1] = jnp.sum(grads * unit, axis=0, keepdims=True)
    sums[1:2] = jnp.sum(grads, axis=0, keepdims=True)
    sums[2:4] = mid_sums[0:2]


def bit_clear(bit):
    return (lax.axis_index("dp") // (1 << bit)) % 2 == 0


def total_of_pair(kept, got):
    return (kept[...].astype(F32) + got[...].astype(F32)).astype(BF16)


def halve_kernel(bit_a, bit_b, kept_a, got_a, kept_b, got_b, keep_a, send_a, keep_b, send_b):
    split_rows(total_of_pair(kept_a, got_a), keep_a, send_a, bit_a)
    split_rows(total_of_pair(kept_b, got_b), keep_b, send_b, bit_b)


def cross_kernel(bit, kept_a, got_a, kept_b, got_b, keep, to_dp, to_row, to_both):
    own = bit_clear(bit)
    half = keep.shape[1]
    for i, (kept, got) in enumerate(((kept_a, got_a), (kept_b, got_b))):
        total = total_of_pair(kept, got)
        low, high = total[:, :half], total[:, half:]
        here, there = jnp.where(own, low, high), jnp.where(own, high, low)
        keep[i], to_dp[i], to_row[i], to_both[i] = here[0], there[0], here[1], there[1]


def join_kernel(keep, from_dp_ref, from_row_ref, from_both_ref, out):
    mine = total_of_pair(keep, from_dp_ref)
    other = total_of_pair(from_row_ref, from_both_ref)
    for i in range(2):
        out[i, 0], out[i, 1] = mine[i], other[i]


def join_more_kernel(keep, from_dp_ref, from_row_ref, from_both_ref, halves, halves_col, mlp, attn, out):
    mine = total_of_pair(keep, from_dp_ref)
    other = total_of_pair(from_row_ref, from_both_ref)
    rows, half = mine.shape[1:]
    for i in range(2):
        out[2 * i * rows : (2 * i + 1) * rows] = mine[i]
        out[(2 * i + 1) * rows : (2 * i + 2) * rows] = other[i]
    third = half // 2
    lines = [
        (halves[...] + halves_col[...])[:4],
        jnp.concatenate([attn[0:1, :third], attn[0:1, 2 * third : 3 * third]], axis=1),
        attn[1:2, :half],
        mlp[0:1, :half],
        mlp[0:1, half : 2 * half],
        mlp[1:2, :half],
        jnp.zeros((EXTRA - 9, half), F32),
    ]
    out[4 * rows :] = jnp.concatenate(lines, axis=0).astype(BF16)


def extra_sum(mine, got):
    return mine[-EXTRA:].astype(F32) + got[-EXTRA:].astype(F32)


def ordered_rows(own, mine, got, begin, rows, out, at):
    low, high = mine[begin : begin + rows], got[begin : begin + rows]
    out[at : at + rows] = jnp.where(own, low, high)
    out[at + rows : at + 2 * rows] = jnp.where(own, high, low)


def part_more_kernel(bit, mine, got, out_a, out_b):
    own = bit_clear(bit)
    rows = out_b.shape[0] // 4
    for i, out in enumerate((out_a, out_b)):
        for p in range(2):
            ordered_rows(own, mine, got, (2 * i + p) * rows, rows, out, 2 * p * rows)
    out_a[4 * rows :] = extra_sum(mine, got).astype(BF16)


def double_more_kernel(bit_a, bit_b, mine_a, got_a, mine_b, got_b, out_a, out_b):
    rows = mine_b.shape[0] // 2
    for bit, mine, got, out in ((bit_a, mine_a, got_a, out_a), (bit_b, mine_b, got_b, out_b)):
        own = bit_clear(bit)
        for p in range(2):
            ordered_rows(own, mine, got, p * rows, rows, out, 2 * p * rows)
    out_a[4 * rows :] = extra_sum(mine_a, got_a).astype(BF16)


def doubled(bit, mine, got, out):
    own = bit_clear(bit)
    half = mine.shape[1]
    out[:, :half] = jnp.where(own, mine, got)
    out[:, half:] = jnp.where(own, got, mine)


def part_kernel(bit, mine, got, out_a, out_b):
    doubled(bit, mine[0], got[0], out_a)
    doubled(bit, mine[1], got[1], out_b)


def double_kernel(bit_a, bit_b, mine_a, got_a, mine_b, got_b, out_a, out_b):
    doubled(bit_a, mine_a[...], got_a[...], out_a)
    doubled(bit_b, mine_b[...], got_b[...], out_b)


def double_apart_kernel(bit_a, bit_b, mine_a, got_a, mine_b, got_b, *outs):
    for i in range(2):
        for bit, mine, got, out in ((bit_a, mine_a, got_a, outs[i]), (bit_b, mine_b, got_b, outs[2 + i])):
            own = bit_clear(bit)
            half = mine.shape[1]
            out[:half] = jnp.where(own, mine[i], got[i])
            out[half:] = jnp.where(own, got[i], mine[i])


def from_both(values, bit):
    count = lax.axis_size("dp")
    pairs = [(2 * i + r, 2 * (i ^ (1 << bit)) + 1 - r) for i in range(count) for r in range(2)]
    return lax.ppermute(values, ("dp", "row"), pairs)


class Pair:
    def __init__(self, keep_a, send_a, keep_b, send_b, bits_a, bits_b, apart):
        self.bits_a, self.bits_b = bits_a, bits_b
        self.apart = apart
        self.count = len(bits_a)
        self.stage = 0
        self.steps = 2 * self.count + apart
        self.state = (keep_a, from_dp(send_a, bits_a[0]), keep_b, from_dp(send_b, bits_b[0]))

    @property
    def on_last(self):
        return self.stage == self.steps - 1

    def step(self):
        self.stage += 1
        count, stage = self.count, self.stage
        last = self.bits_a[-1]
        if stage < count:
            rows, lanes = self.state[0].shape[1:]
            if stage < count - 1:
                bit_a, bit_b = self.bits_a[stage], self.bits_b[stage]
                keep_a, send_a, keep_b, send_b = call(
                    lambda *refs: halve_kernel(bit_a, bit_b, *refs),
                    (shape((2, rows // 2, lanes), BF16),) * 4,
                    *self.state,
                )
                self.state = (keep_a, from_dp(send_a, bit_a), keep_b, from_dp(send_b, bit_b))
            else:
                keep, to_dp, to_row, to_both = call(
                    lambda *refs: cross_kernel(last, *refs),
                    (shape((2, rows // 2, lanes), BF16),) * 4,
                    *self.state,
                )
                self.state = (keep, from_dp(to_dp, last), from_row(to_row), from_both(to_both, last))
        elif not self.apart:
            self.gather()
        elif stage == count:
            rows, lanes = self.state[0].shape[1:]
            mine = call(join_kernel, shape((2, 2, rows, lanes), BF16), *self.state)
            self.state = (mine, from_dp(mine, last))
        elif stage == 2 * count:
            mine_a, got_a, mine_b, got_b, next_a, next_b = self.state
            more_a, more_b = from_dp(next_a, self.bits_a[0]), from_dp(next_b, self.bits_b[0])
            self.state = (mine_a, got_a, mine_b, got_b, next_a, more_a, next_b, more_b)
        elif self.apart and stage == 2 * count - 1:
            rows, lanes = self.state[0].shape[-2:]
            before_a, before_b = self.bits_a[1], self.bits_b[1]
            a0, a1, b0, b1 = call(
                lambda *refs: double_apart_kernel(before_a, before_b, *refs),
                (shape((2 * rows, lanes), BF16),) * 4,
                *self.state,
            )
            self.state = (a0, from_dp(a0, self.bits_a[0]), b0, from_dp(b0, self.bits_b[0]), a1, b1)
        else:
            index = 2 * count - 1 - stage
            bit_a, bit_b = self.bits_a[index], self.bits_b[index]
            rows, lanes = self.state[0].shape[-2:]
            outs = (shape((2, 2 * rows, lanes), BF16),) * 2
            if stage == count + 1:
                mine_a, mine_b = call(lambda *refs: part_kernel(last, *refs), outs, *self.state)
            else:
                before_a, before_b = self.bits_a[index + 1], self.bits_b[index + 1]
                mine_a, mine_b = call(
                    lambda *refs: double_kernel(before_a, before_b, *refs), outs, *self.state
                )
            self.state = (mine_a, from_dp(mine_a, bit_a), mine_b, from_dp(mine_b, bit_b))


    def gather(self):
        count, stage = self.count, self.stage
        rows, lanes = self.state[0].shape[-2:]
        last = self.bits_a[-1]
        if stage == count:
            out = shape((4 * rows + EXTRA, lanes), BF16)
            mine = call(join_more_kernel, out, *self.state, *self.vectors)
            self.state = (mine, from_dp(mine, last))
            return
        index = 2 * count - 1 - stage
        if stage == count + 1:
            rows = rows - EXTRA
            kernel = lambda *refs: part_more_kernel(last, *refs)
        else:
            rows = 2 * (rows - EXTRA)
            before_a, before_b = self.bits_a[index + 1], self.bits_b[index + 1]
            kernel = lambda *refs: double_more_kernel(before_a, before_b, *refs)
        outs = (shape((rows + EXTRA, lanes), BF16), shape((rows, lanes), BF16))
        mine_a, mine_b = call(kernel, outs, *self.state)
        got_a, got_b = from_dp(mine_a, self.bits_a[index]), from_dp(mine_b, self.bits_b[index])
        self.state = (mine_a, got_a, mine_b, got_b)


def arrived(pairs, *others):
    states, others = lax.optimization_barrier(([pair.state for pair in pairs], others))
    for pair, state in zip(pairs, states):
        pair.state = state
    return others


def ordered_halves(bit, mine, got):
    own = (lax.axis_index("dp") // (1 << bit)) % 2 == 0
    return jnp.concatenate(
        [jnp.where(own, mine, got), jnp.where(own, got, mine)], axis=0
    )


def by_row(mine, far, axis):
    first = lax.axis_index("row") == 0
    return jnp.concatenate(
        [jnp.where(first, mine, far), jnp.where(first, far, mine)], axis=axis
    )


def feed_end_kernel(bit, mine_0, got_0, mine_1, got_1, out):
    own = (lax.axis_index("dp") // (1 << bit)) % 2
    here = pl.program_id(1) == own
    near = pl.program_id(0) == lax.axis_index("row")
    part = jnp.where(
        near,
        jnp.where(here, mine_0[...], got_0[...]),
        jnp.where(here, mine_1[...], got_1[...]),
    )
    out[...] = part.astype(F32)


def attention_end(bit, flip, mine, got, left, right):
    rows, half = left.shape[0], left.shape[1]
    own = bit_clear(bit)
    part = rows // 2
    sides = []
    for p in range(2):
        low, high = mine[p * part : (p + 1) * part], got[p * part : (p + 1) * part]
        sides.append(jnp.concatenate([jnp.where(own, low, high), jnp.where(own, high, low)], axis=0))
    near, far = sides
    third = half // 2
    left[...] = by_row(near[:, :third], far[:, :third], 1).astype(F32)
    last = by_row(near[:, third:], far[:, third:], 1).astype(F32)
    right[...] = last.T if flip else last


def first_end_kernel(bit, mine, got, left, right, *refs):
    outs, held, sems = refs[:9], refs[9:18], refs[18]
    small = extra_sum(mine, got)
    half = small.shape[1]
    third = half // 2
    lines = [
        small[4:5, :third],
        small[4:5, third:],
        small[5:6],
        jnp.concatenate([small[6:7], small[7:8]], axis=1),
        small[8:9],
    ] + [small[i : i + 1] for i in range(4)]
    for ref, line in zip(held, lines):
        ref[...] = line.reshape(line.shape[1])
    copies = start_copies(list(zip(held, outs)), sems)
    attention_end(bit, False, mine, got, left, right)
    for copy in copies:
        copy.wait()


def second_end_kernel(bit, mine, got, left, right):
    attention_end(bit, True, mine, got, left, right)


def end_call(kernel, grid, out_shape, block, index, *operands):
    whole = pl.BlockSpec(memory_space=pltpu.VMEM)
    return pl.pallas_call(
        kernel,
        grid=grid,
        out_shape=out_shape,
        in_specs=[whole] * len(operands),
        out_specs=pl.BlockSpec(block, index),
        compiler_params=pltpu.CompilerParams(vmem_limit_bytes=16 * MIB),
    )(*operands)


def body(
    tokens,
    out_grad,
    seq_lengths,
    w_query,
    w_key,
    w_value,
    w_out,
    w_up,
    w_down,
    b_query,
    b_value,
    b_out,
    b_up,
    b_down,
    gain_attn,
    shift_attn,
    gain_mlp,
    shift_mlp,
):
    row = lax.axis_index("row")
    own_rows, half = tokens.shape
    width = 2 * half
    rows = 2 * own_rows
    third = w_query.shape[1] // 2
    units = w_up.shape[1] // 2
    side = lax.axis_index("dp") % 2
    count = lax.axis_size("dp").bit_length() - 1
    bits = list(range(count))
    turned = [1, 0] + bits[2:] if count > 1 else bits
    tall = shape((own_rows, width), F32)
    tall_low = shape((own_rows, width), BF16)
    column = shape((own_rows, 128), F32)
    pair_sums = shape((8, half), F32)

    tokens_far = from_row(tokens)
    vectors = (gain_attn, shift_attn, b_out, gain_mlp, shift_mlp, b_query, b_value, b_up, b_down)
    block = pltpu.VMEM((half, 2 * third), BF16)
    w_kept, sent, sent_out, sent_up, sent_down = call(
        start_kernel,
        (
            shape((half + EXTRA, 3 * third), BF16),
            shape((half // 2 + EXTRA, 3 * third), BF16),
            shape((w_out.shape[0] // 2, half), BF16),
            shape((half // 2, units), BF16),
            shape((units // 2, half), BF16),
        ),
        *vectors, w_query, w_key, w_value, w_out, w_up, w_down,
        hbm=range(15),
        scratch=[pltpu.VMEM(x.shape, x.dtype) for x in vectors]
        + [block, block, block, pltpu.VMEM((EXTRA, 3 * third), F32), pltpu.SemaphoreType.DMA((15,))],
        vmem=VMEM_START,
    )
    tokens_col = from_col(tokens)
    tokens_far, tokens_col, sent, sent_out, sent_up = hold(
        tokens_far, tokens_col, sent, sent_out, sent_up
    )
    w_got = from_row(sent)
    w_side = from_dp(w_got, 0)
    out_got = from_row(sent_out)
    up_got = from_row(sent_up)
    tokens_far_col = from_col(tokens_far)
    tokens_far, tokens_far_col, w_got, w_side, out_got, up_got, sent_down, out_grad_col = hold(
        tokens_far, tokens_far_col, w_got, w_side, out_got, up_got, sent_down, out_grad
    )
    top_col = from_col(out_grad_col)
    down_got = from_row(sent_down)
    out_side = from_dp(out_got, 0)
    up_side = from_dp(up_got, 0)
    every_token = (tokens, tokens_far, tokens_col, tokens_far_col)

    like = shape((rows, third), BF16)
    normed_all, query, key, value, mixed, lse = call(
        forward_kernel,
        (shape((rows, width), BF16), like, like, like, like, shape((8, rows), F32)),
        seq_lengths,
        *every_token,
        w_kept,
        w_got,
        w_side,
        smem=(0,),
        hbm_out=range(4),
        scratch=[pltpu.VMEM((rows, width), BF16)]
        + [pltpu.VMEM((rows, third), BF16)] * 3
        + [pltpu.SemaphoreType.DMA((4,))],
    )
    mixed_far = from_row(mixed)
    mixed_gate = mixed
    mixed_far, out_side, up_side, down_got, out_grad_send = hold(
        mixed_far, out_side, up_side, down_got, out_grad
    )

    keep, send, w_out_far = call(
        branch_kernel,
        (shape((rows, width), F32), shape((rows, width), BF16), shape(w_out.shape, BF16)),
        mixed_gate, mixed_far, w_out, out_got, out_side,
    )
    got = from_col(send)
    top_far = from_row(out_grad_send)
    down_side = from_dp(down_got, 1)
    (got,) = hold(got)

    middle, normed_mlp_all, unit_mlp, inverse_mlp = call(
        second_norm_kernel,
        (shape((own_rows, half), F32), shape((rows, width), BF16), tall, column),
        *every_token, keep, got, w_kept, w_got,
    )
    hidden, slope, w_up_far = call(
        up_kernel,
        (shape((rows, units), BF16), shape((rows, units), F32), shape((half, units), BF16)),
        normed_mlp_all, w_up, up_got, up_side, w_kept,
    )
    hidden, top_far = hold(hidden, top_far)
    top_far_col = from_col(top_far)
    top_far_col, down_side = hold(top_far_col, down_side)

    split_down = shape((2, units // 2, half), BF16)
    split_up = shape((2, half, units // 2), BF16)
    down_keep, down_send, up_keep, up_send, keep, send, mlp_sums, w_down_far = call(
        lambda *refs: down_kernel(bits[0], turned[0], *refs),
        (
            split_down, split_down, split_up, split_up, tall, tall_low,
            shape((8, units), F32), shape((units, half), BF16),
        ),
        seq_lengths, out_grad, top_far, top_col, top_far_col, hidden, slope, normed_mlp_all,
        w_down, down_got, down_side, w_up, w_up_far,
        scratch=[pltpu.VMEM((rows, width), BF16), pltpu.VMEM((rows, units), BF16)],
        smem=(0,),
    )
    got = from_col(send)
    feed = Pair(down_keep, down_send, up_keep, up_send, bits, turned, True)
    (got,) = hold(got)

    total = (keep + got.astype(F32)).astype(BF16)
    total_far = from_row(total)
    keep, send = call(
        output_kernel, (tall, tall_low), hidden, w_down, w_down_far,
    )
    got = from_col(send)
    total_far, got = hold(total_far, got)

    grad_middle, datt, mid_sums = call(
        second_back_kernel,
        (shape((own_rows, half), F32), tall_low, pair_sums),
        seq_lengths, total, total_far, unit_mlp, inverse_mlp, w_kept, w_got, out_grad, top_far,
        smem=(0,),
    )
    datt_col = from_col(datt)
    raised_keep, raised_got = keep, got
    (datt_col,) = arrived([feed], datt_col)
    feed.step()

    split_pair = shape((2, half // 2, 2 * third), BF16)
    first_keep, first_send, second_keep, second_send, keep, send, attn_sums = call(
        lambda *refs: backward_kernel(bits[0], turned[0], *refs),
        (split_pair,) * 4 + (tall, tall_low, shape((8, width), F32)),
        seq_lengths, datt, datt_col, w_out, w_out_far, query, key, value, mixed, lse,
        normed_all, w_kept, w_got, w_side,
        scratch=[
            pltpu.VMEM((rows, width), BF16),
            pltpu.VMEM((rows, 3 * third), BF16),
            pltpu.VMEM((rows, third), F32),
            pltpu.VMEM((rows, third), F32),
        ]
        + [pltpu.VMEM((rows, third), BF16)] * 4
        + [pltpu.VMEM((rows, width), BF16), pltpu.SemaphoreType.DMA((4,))],
        smem=(0,),
        hbm=(5, 6, 7, 10),
    )
    keep, send = arrived([feed], keep, send)
    got = from_col(send)
    attention = Pair(first_keep, first_send, second_keep, second_send, bits, turned, False)
    pairs = [feed, attention]
    feed.step()
    mine, raised, out, stats, unit_attn, inverse_attn = call(
        first_back_kernel,
        (
            shape((own_rows, half), F32),
            shape((own_rows, half), F32),
            shape((rows + EXTRA, half), BF16),
            shape((8, own_rows), F32),
            shape((own_rows, half), F32),
            column,
        ),
        keep, got, raised_keep, raised_got, tokens, tokens_far, w_kept, w_got,
    )
    (out,) = arrived(pairs, out)
    got = from_row(out)
    feed.step()
    attention.step()

    output, input_grad, halves = call(
        last_kernel,
        (shape((own_rows, half), BF16), shape((own_rows, half), BF16), pair_sums),
        mine, raised, got, stats, unit_attn, inverse_attn, w_kept, middle, grad_middle, mid_sums,
    )
    (halves,) = arrived(pairs, halves)
    halves_col = from_col(halves)
    feed.step()
    attention.step()
    (halves_col,) = arrived(pairs, halves_col)
    attention.vectors = (halves, halves_col, mlp_sums, attn_sums)
    while not attention.on_last:
        moving = [pair for pair in pairs if not pair.on_last]
        for pair in moving:
            pair.step()
        arrived(moving)

    wide = w_query.shape[1]
    outs = (shape((half, wide), F32),) * 2
    mine_a, got_a, mine_b, got_b = attention.state
    sizes = (third, third, half, 2 * half, half, half, half, half, half)
    grad_query, grad_key, *vector_grads = call(
        lambda *refs: first_end_kernel(bits[0], *refs),
        outs + tuple(shape((size,), F32) for size in sizes),
        mine_a,
        got_a,
        hbm_out=range(2, 11),
        scratch=[pltpu.VMEM((size,), F32) for size in sizes] + [pltpu.SemaphoreType.DMA((9,))],
    )
    grad_value, grad_out = call(
        lambda *refs: second_end_kernel(turned[0], *refs), outs, mine_b, got_b
    )
    a_0, got_a_0, b_0, got_b_0, a_1, got_a_1, b_1, got_b_1 = feed.state
    grad_down = end_call(
        lambda *refs: feed_end_kernel(bits[0], *refs),
        (2, 2),
        shape((2 * units, half), F32),
        (units // 2, half),
        lambda i, j: (2 * i + j, 0),
        a_0,
        got_a_0,
        a_1,
        got_a_1,
    )
    grad_up = end_call(
        lambda *refs: feed_end_kernel(turned[0], *refs),
        (2, 2),
        shape((half, 2 * units), F32),
        (half, units // 2),
        lambda i, j: (0, 2 * i + j),
        b_0,
        got_b_0,
        b_1,
        got_b_1,
    )
    return (
        output,
        input_grad,
        grad_query,
        grad_key,
        grad_value,
        grad_out,
        grad_up,
        grad_down,
        *vector_grads,
    )


def solution(mesh):
    return jax.shard_map(
        body,
        mesh=mesh,
        in_specs=(
            P(("dp", "col"), "row"),
            P(("dp", "col"), "row"),
            P("dp", None),
            P("row", "col"),
            P("row", "col"),
            P("row", "col"),
            P("col", "row"),
            P("row", "col"),
            P("col", "row"),
            P(("col", "row")),
            P(("col", "row")),
            P("row"),
            P(("col", "row")),
            P("row"),
            P("row"),
            P("row"),
            P("row"),
            P("row"),
        ),
        out_specs=(
            P(("dp", "col"), "row"),
            P(("dp", "col"), "row"),
            P("row", "col"),
            P("row", "col"),
            P("row", "col"),
            P("col", "row"),
            P("row", "col"),
            P("col", "row"),
            P(("col", "row")),
            P(("col", "row")),
            P("row"),
            P(("col", "row")),
            P("row"),
            P("row"),
            P("row"),
            P("row"),
            P("row"),
        ),
        check_vma=False,
    )
```

```python
import jax
import jax.numpy as jnp
from jax import lax
from jax.experimental import pallas as pl
from jax.experimental.pallas import tpu as pltpu
from jax.sharding import PartitionSpec as P

HEAD_DIM = 64
EPSILON = 1e-05
MASKED = -1e30
F32 = jnp.float32
BF16 = jnp.bfloat16
SWAP = ((0, 1), (1, 0))
CUBIC = 0.044715
ROOT = 0.7978845608028654
MIB = 1024 * 1024
VMEM_START = 54
EXTRA = 16


def dot(left, right):
    return jnp.dot(left, right, preferred_element_type=F32)


def dot_nt(left, right):
    return lax.dot_general(left, right, (((1,), (1,)), ((), ())), preferred_element_type=F32)


def dot_tn(left, right):
    return lax.dot_general(left, right, (((0,), (0,)), ((), ())), preferred_element_type=F32)


def from_row(values):
    return lax.ppermute(values, "row", SWAP)


def from_col(values):
    return lax.ppermute(values, "col", SWAP)


def dp_pairs(bit):
    count = lax.axis_size("dp")
    return [(i, i ^ (1 << bit)) for i in range(count)]


def from_dp(values, bit):
    return lax.ppermute(values, "dp", dp_pairs(bit))


def hold(*values):
    return lax.optimization_barrier(values)


def shape(dims, kind):
    return jax.ShapeDtypeStruct(tuple(dims), kind)


def call(kernel, out_shape, *operands, scratch=(), smem=(), hbm=(), hbm_out=(), vmem=16):
    spaces = [
        pltpu.SMEM if i in smem else pltpu.HBM if i in hbm else pltpu.VMEM
        for i in range(len(operands))
    ]
    out_specs = jax.tree.map(lambda _: pl.BlockSpec(memory_space=pltpu.VMEM), out_shape)
    if hbm_out:
        out_specs = tuple(
            pl.BlockSpec(memory_space=pltpu.HBM if i in hbm_out else pltpu.VMEM)
            for i in range(len(out_shape))
        )
    return pl.pallas_call(
        kernel,
        out_shape=out_shape,
        in_specs=[pl.BlockSpec(memory_space=space) for space in spaces],
        out_specs=out_specs,
        scratch_shapes=list(scratch),
        compiler_params=pltpu.CompilerParams(vmem_limit_bytes=vmem * MIB),
        cost_estimate=pl.CostEstimate(flops=0, bytes_accessed=0, transcendentals=0),
    )(*operands)


def half_rows(index, size):
    return pl.ds(pl.multiple_of(index * size, size), size)


def start_copies(pairs, sems):
    copies = [
        pltpu.make_async_copy(source, target, sems.at[i]) for i, (source, target) in enumerate(pairs)
    ]
    for copy in copies:
        copy.start()
    return copies


GAIN_A, SHIFT_A, BIAS_O, GAIN_M, SHIFT_M, BIAS_QKV, BIAS_UP, BIAS_DOWN = 0, 1, 2, 3, 4, 5, 6, 8


def start_kernel(*refs):
    vectors, (w_q, w_k, w_v, w_out, w_up, w_down) = refs[:9], refs[9:15]
    kept, sent, out_sent, up_sent, down_sent = refs[15:20]
    held, held_w, extra, sems = refs[20:29], refs[29:32], refs[32], refs[33]
    row, side = lax.axis_index("row"), lax.axis_index("dp") % 2
    other_side = (lax.axis_index("dp") // 2) % 2
    units = up_sent.shape[1]
    copies = start_copies(
        list(zip((w_q, w_k, w_v), held_w))
        + list(zip(vectors, held))
        + [
            (w_out.at[half_rows(side, out_sent.shape[0])], out_sent),
            (w_up.at[half_rows(side, up_sent.shape[0]), half_rows(1 - row, units)], up_sent),
            (w_down.at[half_rows(2 * (1 - row) + other_side, down_sent.shape[0])], down_sent),
        ],
        sems,
    )
    first = row == 0
    half, third = w_q.shape[0], w_q.shape[1] // 2
    part = half // 2
    keeps, sends = [], []
    for ref, copy in zip(held_w, copies):
        copy.wait()
        low, high = ref[:, :third], ref[:, third:]
        keeps.append(jnp.where(first, low, high))
        away = jnp.where(first, high, low)
        sends.append(jnp.where(side == 0, away[:part], away[part:]))
    kept[:half] = jnp.concatenate(keeps, axis=1)
    sent[:part] = jnp.concatenate(sends, axis=1)
    for copy in copies[3:]:
        copy.wait()
    extra[...] = jnp.zeros_like(extra)
    lines = [ref[...].astype(F32).reshape(1, -1) for ref in held]
    for i in range(5):
        extra[i : i + 1, :half] = lines[i]
    b_q, b_v, b_u, b_d = lines[5:]
    extra[BIAS_QKV : BIAS_QKV + 1, :third] = b_q
    extra[BIAS_QKV : BIAS_QKV + 1, 2 * third :] = b_v
    for i in range(2):
        extra[BIAS_UP + i : BIAS_UP + i + 1, :half] = b_u[:, i * half : (i + 1) * half]
    extra[BIAS_DOWN : BIAS_DOWN + 1, :half] = b_d
    kept[half:] = extra[...].astype(BF16)
    sent[part:] = extra[...].astype(BF16)


def normed_parts(values):
    mean = jnp.mean(values, axis=1, keepdims=True)
    centered = values - mean
    variance = jnp.mean(centered * centered, axis=1, keepdims=True)
    inverse = lax.rsqrt(variance + EPSILON)
    return centered * inverse, inverse


def both_halves(mine, far):
    return jnp.concatenate([mine[...], far[...]], axis=1).astype(F32)


def vector_of(kept, i):
    return kept[kept.shape[0] - EXTRA :].astype(F32)[i : i + 1, : 2 * kept.shape[1] // 3]


def wide_vector(kept, got, i):
    return jnp.concatenate([vector_of(kept, i), vector_of(got, i)], axis=1)


def head_mask(width, head):
    lanes = lax.broadcasted_iota(jnp.int32, (1, width), 1)
    return lanes // HEAD_DIM == head


def allowed_block(lengths, keys, first_query, count):
    first, second = lengths[0, 0], lengths[0, 0] + lengths[0, 1]
    query = first_query + lax.broadcasted_iota(jnp.int32, (1, count), 1)
    begin = jnp.where(query >= second, second, jnp.where(query >= first, first, 0))
    key = lax.broadcasted_iota(jnp.int32, (keys, count), 0)
    return (key >= begin) & (key <= query)


def weights_got(got, got_side):
    part = got.shape[0] - EXTRA
    first = lax.axis_index("dp") % 2 == 0
    here, there = got[:part], got_side[:part]
    return jnp.concatenate([jnp.where(first, here, there), jnp.where(first, there, here)], axis=0)


def forward_kernel(lengths, own, own_far, col_own, col_far, w_kept, got, got_side, norm_hbm, q_hbm, k_hbm, v_hbm, o_out, lse,
                   norm_out, q_out, k_out, v_out, sems):
    own_rows, half = own.shape
    w_got = weights_got(got, got_side)
    third = q_out.shape[1]
    col = lax.axis_index("col")
    gain, shift = wide_vector(w_kept, got, GAIN_A), wide_vector(w_kept, got, SHIFT_A)
    bias = w_kept[half:].astype(F32)[BIAS_QKV : BIAS_QKV + 1]
    for ref, far, at in ((own, own_far, col), (col_own, col_far, 1 - col)):
        where = half_rows(at, own_rows)
        unit, _ = normed_parts(both_halves(ref, far))
        values = (unit * gain + shift).astype(BF16)
        norm_out[where] = values
        total = dot(values[:, :half], w_kept[:half]) + dot(values[:, half:], w_got)
        total = (total + bias).astype(BF16)
        q_out[where] = total[:, :third]
        k_out[where] = total[:, third : 2 * third]
        v_out[where] = total[:, 2 * third :]
    copies = start_copies(
        [(norm_out, norm_hbm), (q_out, q_hbm), (k_out, k_hbm), (v_out, v_hbm)], sems
    )
    lse[...] = jnp.zeros_like(lse)
    values_t = v_out[...].T
    for begin in (0, own_rows):
        keys = begin + own_rows
        allowed = allowed_block(lengths, keys, begin, own_rows)
        query = q_out[begin:keys] * BF16(HEAD_DIM ** (-0.5))
        parts = []
        for head in range(third // HEAD_DIM):
            key = jnp.where(head_mask(third, head), k_out[:keys], BF16(0))
            scores = jnp.where(allowed, dot_nt(key, query), MASKED)
            largest = jnp.max(scores, axis=0, keepdims=True)
            weights = jnp.exp(scores - largest)
            summed = jnp.sum(weights, axis=0, keepdims=True)
            lse[head : head + 1, begin:keys] = largest + jnp.log(summed)
            mixed = dot(
                values_t[head * HEAD_DIM : (head + 1) * HEAD_DIM, :keys], weights.astype(BF16)
            )
            parts.append(mixed / summed)
        o_out[begin:keys] = jnp.concatenate(parts, axis=0).T.astype(BF16)
    for copy in copies:
        copy.wait()


def split_tokens(total_of, keep, send, own_rows, col):
    keep[...] = total_of(half_rows(col, own_rows))
    send[...] = total_of(half_rows(1 - col, own_rows)).astype(BF16)


def branch_kernel(mixed, mixed_other, w_mine, got, got_side, keep, send, w_other):
    w_other[...] = both_sides(got, got_side, 0)
    row = lax.axis_index("row")
    third = mixed.shape[1]
    own, far = half_rows(row, third), half_rows(1 - row, third)

    for i, w in enumerate((w_mine, w_other)):
        lanes = slice(i * w.shape[1], (i + 1) * w.shape[1])
        part = dot(mixed[...], w[own]) + dot(mixed_other[...], w[far])
        keep[:, lanes] = part
        send[:, lanes] = part.astype(BF16)


def second_norm_kernel(own, own_far, col_own, col_far, keep, got, kept, sent, middle, normed, unit_out, inverse_out):
    own_rows = own.shape[0]
    col = lax.axis_index("col")
    bias, gain, shift = [wide_vector(kept, sent, i) for i in (BIAS_O, GAIN_M, SHIFT_M)]
    for ref, far, at in ((own, own_far, col), (col_own, col_far, 1 - col)):
        where = half_rows(at, own_rows)
        values = both_halves(ref, far) + (keep[where] + got[where].astype(F32) + bias)
        unit, inverse = normed_parts(values)
        normed[where] = (unit * gain + shift).astype(BF16)
        if ref is own:
            middle[...] = values[:, : middle.shape[1]]
            unit_out[...] = unit
            inverse_out[...] = jnp.broadcast_to(inverse, inverse_out.shape)


def both_sides(got, got_side, axis, bit=0):
    first = (lax.axis_index("dp") // (1 << bit)) % 2 == 0
    low = jnp.where(first, got[...], got_side[...])
    high = jnp.where(first, got_side[...], got[...])
    return jnp.concatenate([low, high], axis=axis)


def up_kernel(normed, w_up, got, got_side, kept, hidden_out, slope_out, w_other_out):
    rows, width = normed.shape
    half = width // 2
    units = got.shape[1]
    row = lax.axis_index("row")
    w_mine = w_up[:, pl.ds(pl.multiple_of(row * units, units), units)]
    w_other = both_sides(got, got_side, 0)
    w_other_out[...] = w_other
    bias = jnp.concatenate([vector_of(kept, BIAS_UP + i) for i in range(2)], axis=1)
    for begin in (0, rows // 2):
        where = slice(begin, begin + rows // 2)
        values = normed[where]
        u = dot(values[:, :half], w_mine) + dot(values[:, half:], w_other) + bias
        squared = u * u
        bent = jnp.tanh(ROOT * (u + CUBIC * (squared * u)))
        raised = 0.5 * (1.0 + bent)
        hidden_out[where] = (u * raised).astype(BF16)
        slope_out[where] = raised + 0.5 * u * (1.0 - bent * bent) * (
            ROOT * (1.0 + (3.0 * CUBIC) * squared)
        )


def split_rows(total, keep, send, bit):
    own = (lax.axis_index("dp") // (1 << bit)) % 2 == 0
    half = keep.shape[-2]
    low, high = total[..., :half, :], total[..., half:, :]
    keep[...] = jnp.where(own, low, high)
    send[...] = jnp.where(own, high, low)


def masked_top(lengths, mine, far, at):
    live = lengths[0, 0] + lengths[0, 1]
    own_rows = mine.shape[0]
    position = at * own_rows + lax.broadcasted_iota(jnp.int32, (own_rows, 1), 0)
    values = jnp.concatenate([mine[...], far[...]], axis=1)
    return jnp.where(position < live, values, BF16(0))


def down_kernel(bit_down, bit_up, lengths, top, top_far, top_col, top_far_col, hidden, slope, normed, w_down, got, got_side,
                w_up, w_up_other, down_keep, down_send, up_keep, up_send, keep, send, sums, w_other_out, top_all, grad_pre):
    own_rows, half = top.shape
    units = hidden.shape[1]
    row, col = lax.axis_index("row"), lax.axis_index("col")
    top_all[half_rows(col, own_rows)] = masked_top(lengths, top, top_far, col)
    top_all[half_rows(1 - col, own_rows)] = masked_top(lengths, top_col, top_far_col, 1 - col)
    top_rows = top_all[...]
    total = dot_tn(hidden[...], top_rows).astype(BF16)
    split_rows(jnp.stack([total[:, :half], total[:, half:]]), down_keep, down_send, bit_down)
    w_other = both_sides(got, got_side, 0, 1)
    w_other_out[...] = w_other
    grad_hidden = dot_nt(top_rows[:, :half], w_down[half_rows(row, units)]) + dot_nt(
        top_rows[:, half:], w_other
    )
    grads = (grad_hidden * slope[...]).astype(BF16)
    grad_pre[...] = grads
    w_mine = w_up[:, pl.ds(pl.multiple_of(row * units, units), units)]

    def total_of(rows):
        values = grad_pre[rows]
        return jnp.concatenate([dot_nt(values, w_mine), dot_nt(values, w_up_other[...])], axis=1)

    split_tokens(total_of, keep, send, own_rows, col)
    total = dot_tn(normed[...], grads).astype(BF16)
    total = total.reshape(2, half, units)
    total = jnp.concatenate([total[..., : units // 2], total[..., units // 2 :]], axis=1)
    split_rows(total, up_keep, up_send, bit_up)
    sums[...] = jnp.zeros_like(sums)
    sums[0:1] = jnp.sum(grads.astype(F32), axis=0, keepdims=True)
    sums[1:2, :half] = jnp.sum(top_rows[:, :half].astype(F32), axis=0, keepdims=True)


def output_kernel(hidden, w_down, w_other, keep, send):
    units = hidden.shape[1]
    row, col = lax.axis_index("row"), lax.axis_index("col")
    w_mine = w_down[half_rows(row, units)]

    def total_of(rows):
        values = hidden[rows]
        return jnp.concatenate([dot(values, w_mine), dot(values, w_other[...])], axis=1)

    split_tokens(total_of, keep, send, keep.shape[0], col)


def second_back_kernel(lengths, total, total_far, unit_ref, inverse_ref, kept, sent, top, top_far, middle_out, datt, sums):
    half = top.shape[1]
    got = total_far[...].astype(F32)
    grads = total[...].astype(F32) + jnp.concatenate([got[:, half:], got[:, :half]], axis=1)
    unit = unit_ref[...]
    scaled = grads * wide_vector(kept, sent, GAIN_M)
    mean_plain = jnp.mean(scaled, axis=1, keepdims=True)
    mean_unit = jnp.mean(scaled * unit, axis=1, keepdims=True)
    own = masked_top(lengths, top, top_far, lax.axis_index("col")).astype(F32)
    result = own + inverse_ref[:, :1] * (scaled - mean_plain - unit * mean_unit)
    middle_out[...] = result[:, :half]
    datt[...] = result.astype(BF16)
    sums[...] = jnp.zeros_like(sums)
    sums[0:1] = jnp.sum((grads * unit)[:, :half], axis=0, keepdims=True)
    sums[1:2] = jnp.sum(grads[:, :half], axis=0, keepdims=True)


def backward_kernel(bit_first, bit_second, lengths, own, other, w_mine, w_other, q_hbm, k_hbm, v_hbm, o_ref, lse, normed_hbm, w_kept, got, got_side,
                    first_keep, first_send, second_keep, second_send, keep, send, sums, datt, out, acc_k, acc_v, do_ref,
                    q_ref, k_ref, v_ref, normed, sems):
    copies = start_copies(
        [(q_hbm, q_ref), (k_hbm, k_ref), (v_hbm, v_ref), (normed_hbm, normed)], sems
    )
    own_rows, width = own.shape
    half = width // 2
    third = q_ref.shape[1]
    row, col = lax.axis_index("row"), lax.axis_index("col")
    quarter = half_rows(row, third)
    for ref, at in ((own, col), (other, 1 - col)):
        where = half_rows(at, own_rows)
        values = ref[...]
        datt[where] = values
        do_ref[where] = (
            dot_nt(values[:, :half], w_mine[quarter]) + dot_nt(values[:, half:], w_other[quarter])
        ).astype(BF16)
    for copy in copies:
        copy.wait()
    keys_t = k_ref[...].T
    acc_k[...] = jnp.zeros_like(acc_k)
    acc_v[...] = jnp.zeros_like(acc_v)
    scale = BF16(HEAD_DIM ** (-0.5))
    for begin in (0, own_rows):
        keys = begin + own_rows
        allowed = allowed_block(lengths, keys, begin, own_rows)
        query = q_ref[begin:keys] * scale
        grad_mixed = do_ref[begin:keys]
        parts = []
        for head in range(third // HEAD_DIM):
            mask = head_mask(third, head)
            key = jnp.where(mask, k_ref[:keys], BF16(0))
            scores = jnp.where(allowed, dot_nt(key, query), MASKED)
            probs = jnp.exp(scores - lse[head : head + 1, begin:keys])
            value = jnp.where(mask, v_ref[:keys], BF16(0))
            grad_probs = dot_nt(value, grad_mixed)
            both = probs * grad_probs
            inner = jnp.sum(both, axis=0, keepdims=True)
            grad_raw = (both - probs * inner).astype(BF16) * scale
            acc_v[:keys] += jnp.where(mask, dot(probs.astype(BF16), grad_mixed), 0.0)
            acc_k[:keys] += jnp.where(mask, dot(grad_raw, q_ref[begin:keys]), 0.0)
            parts.append(dot(keys_t[head * HEAD_DIM : (head + 1) * HEAD_DIM, :keys], grad_raw))
        out[begin:keys, :third] = jnp.concatenate(parts, axis=0).T.astype(BF16)
    out[:, third : 2 * third] = acc_k[...].astype(BF16)
    out[:, 2 * third :] = acc_v[...].astype(BF16)
    grads = out[...]
    weights = dot_tn(normed[...], grads).astype(BF16)
    grad_out = dot_tn(datt[...], o_ref[...]).astype(BF16)
    split_rows(weights[:, : 2 * third].reshape(2, half, 2 * third), first_keep, first_send, bit_first)
    last = jnp.concatenate([weights[:, 2 * third :], grad_out], axis=1)
    split_rows(last.reshape(2, half, 2 * third), second_keep, second_send, bit_second)

    w_got = weights_got(got, got_side)

    def total_of(rows):
        values = out[rows]
        return jnp.concatenate([dot_nt(values, w_kept[:half]), dot_nt(values, w_got)], axis=1)

    split_tokens(total_of, keep, send, own_rows, col)
    sums[...] = jnp.zeros_like(sums)
    sums[0:1, : 3 * third] = jnp.sum(grads.astype(F32), axis=0, keepdims=True)
    sums[1:2, :half] = jnp.sum(datt[:, :half].astype(F32), axis=0, keepdims=True)


def first_back_kernel(keep, got, raised_keep, raised_got, own, own_far, kept, sent, mine, raised, out, stats, unit_out, inverse_out):
    own_rows, half = mine.shape
    unit, inverse = normed_parts(both_halves(own, own_far))
    unit_out[...] = unit[:, :half]
    inverse_out[...] = jnp.broadcast_to(inverse, inverse_out.shape)
    grads = keep[...] + got[...].astype(F32)
    total = raised_keep[...] + raised_got[...].astype(F32)
    mine[...], raised[...] = grads[:, :half], total[:, :half]
    out[:own_rows] = grads[:, half:].astype(BF16)
    out[own_rows : 2 * own_rows] = total[:, half:].astype(BF16)
    scaled = grads * wide_vector(kept, sent, GAIN_A)
    plain = jnp.sum(scaled, axis=1, keepdims=True)
    crossed = jnp.sum(scaled * unit, axis=1, keepdims=True)
    lanes = lax.broadcasted_iota(jnp.int32, (1, 128), 1)
    both = jnp.where(lanes == 0, plain, jnp.where(lanes == 1, crossed, 0.0)).T[:8]
    stats[...] = both
    high = both.astype(BF16)
    low = (both - high.astype(F32)).astype(BF16)
    out[2 * own_rows :] = jnp.zeros((EXTRA, half), BF16)
    out[2 * own_rows :, :own_rows] = jnp.concatenate([high, low], axis=0)


def last_kernel(mine, raised, got, stats, unit_ref, inverse_ref, kept, middle, grad_middle, mid_sums, output, result, sums):
    own_rows, half = mine.shape
    unit = unit_ref[...]
    grads = mine[...] + got[:own_rows].astype(F32)
    pairs = got[2 * own_rows :, :own_rows].astype(F32)
    total = (stats[...] + (pairs[:8] + pairs[8:])) / (2 * half)
    columns = jnp.concatenate([total, jnp.zeros((120, total.shape[1]), F32)], axis=0).T
    grad_in = inverse_ref[:, :1] * (
        grads * vector_of(kept, GAIN_A) - columns[:, 0:1] - unit * columns[:, 1:2]
    )
    result[...] = (grad_middle[...] + grad_in).astype(BF16)
    far = got[own_rows : 2 * own_rows].astype(F32)
    output[...] = (middle[...] + (raised[...] + far) + vector_of(kept, BIAS_DOWN)).astype(BF16)
    sums[...] = jnp.zeros_like(sums)
    sums[0:1] = jnp.sum(grads * unit, axis=0, keepdims=True)
    sums[1:2] = jnp.sum(grads, axis=0, keepdims=True)
    sums[2:4] = mid_sums[0:2]


def bit_clear(bit):
    return (lax.axis_index("dp") // (1 << bit)) % 2 == 0


def total_of_pair(kept, got):
    return (kept[...].astype(F32) + got[...].astype(F32)).astype(BF16)


def halve_kernel(bit_a, bit_b, kept_a, got_a, kept_b, got_b, keep_a, send_a, keep_b, send_b):
    split_rows(total_of_pair(kept_a, got_a), keep_a, send_a, bit_a)
    split_rows(total_of_pair(kept_b, got_b), keep_b, send_b, bit_b)


def cross_kernel(bit, kept_a, got_a, kept_b, got_b, keep, to_dp, to_row, to_both):
    own = bit_clear(bit)
    half = keep.shape[1]
    for i, (kept, got) in enumerate(((kept_a, got_a), (kept_b, got_b))):
        total = total_of_pair(kept, got)
        low, high = total[:, :half], total[:, half:]
        here, there = jnp.where(own, low, high), jnp.where(own, high, low)
        keep[i], to_dp[i], to_row[i], to_both[i] = here[0], there[0], here[1], there[1]


def join_kernel(keep, from_dp_ref, from_row_ref, from_both_ref, out):
    mine = total_of_pair(keep, from_dp_ref)
    other = total_of_pair(from_row_ref, from_both_ref)
    for i in range(2):
        out[i, 0], out[i, 1] = mine[i], other[i]


def join_more_kernel(keep, from_dp_ref, from_row_ref, from_both_ref, halves, halves_col, mlp, attn, out):
    mine = total_of_pair(keep, from_dp_ref)
    other = total_of_pair(from_row_ref, from_both_ref)
    rows, half = mine.shape[1:]
    for i in range(2):
        out[2 * i * rows : (2 * i + 1) * rows] = mine[i]
        out[(2 * i + 1) * rows : (2 * i + 2) * rows] = other[i]
    third = half // 2
    lines = [
        (halves[...] + halves_col[...])[:4],
        jnp.concatenate([attn[0:1, :third], attn[0:1, 2 * third : 3 * third]], axis=1),
        attn[1:2, :half],
        mlp[0:1, :half],
        mlp[0:1, half : 2 * half],
        mlp[1:2, :half],
        jnp.zeros((EXTRA - 9, half), F32),
    ]
    out[4 * rows :] = jnp.concatenate(lines, axis=0).astype(BF16)


def extra_sum(mine, got):
    return mine[-EXTRA:].astype(F32) + got[-EXTRA:].astype(F32)


def ordered_rows(own, mine, got, begin, rows, out, at):
    low, high = mine[begin : begin + rows], got[begin : begin + rows]
    out[at : at + rows] = jnp.where(own, low, high)
    out[at + rows : at + 2 * rows] = jnp.where(own, high, low)


def part_more_kernel(bit, mine, got, out_a, out_b):
    own = bit_clear(bit)
    rows = out_b.shape[0] // 4
    for i, out in enumerate((out_a, out_b)):
        for p in range(2):
            ordered_rows(own, mine, got, (2 * i + p) * rows, rows, out, 2 * p * rows)
    out_a[4 * rows :] = extra_sum(mine, got).astype(BF16)


def double_more_kernel(bit_a, bit_b, mine_a, got_a, mine_b, got_b, out_a, out_b):
    rows = mine_b.shape[0] // 2
    for bit, mine, got, out in ((bit_a, mine_a, got_a, out_a), (bit_b, mine_b, got_b, out_b)):
        own = bit_clear(bit)
        for p in range(2):
            ordered_rows(own, mine, got, p * rows, rows, out, 2 * p * rows)
    out_a[4 * rows :] = extra_sum(mine_a, got_a).astype(BF16)


def doubled(bit, mine, got, out):
    own = bit_clear(bit)
    half = mine.shape[1]
    out[:, :half] = jnp.where(own, mine, got)
    out[:, half:] = jnp.where(own, got, mine)


def part_kernel(bit, mine, got, out_a, out_b):
    doubled(bit, mine[0], got[0], out_a)
    doubled(bit, mine[1], got[1], out_b)


def double_kernel(bit_a, bit_b, mine_a, got_a, mine_b, got_b, out_a, out_b):
    doubled(bit_a, mine_a[...], got_a[...], out_a)
    doubled(bit_b, mine_b[...], got_b[...], out_b)


def double_apart_kernel(bit_a, bit_b, mine_a, got_a, mine_b, got_b, *outs):
    for i in range(2):
        for bit, mine, got, out in ((bit_a, mine_a, got_a, outs[i]), (bit_b, mine_b, got_b, outs[2 + i])):
            own = bit_clear(bit)
            half = mine.shape[1]
            out[:half] = jnp.where(own, mine[i], got[i])
            out[half:] = jnp.where(own, got[i], mine[i])


def from_both(values, bit):
    count = lax.axis_size("dp")
    pairs = [(2 * i + r, 2 * (i ^ (1 << bit)) + 1 - r) for i in range(count) for r in range(2)]
    return lax.ppermute(values, ("dp", "row"), pairs)


class Pair:
    def __init__(self, keep_a, send_a, keep_b, send_b, bits_a, bits_b, apart):
        self.bits_a, self.bits_b = bits_a, bits_b
        self.apart = apart
        self.count = len(bits_a)
        self.stage = 0
        self.steps = 2 * self.count + apart
        self.state = (keep_a, from_dp(send_a, bits_a[0]), keep_b, from_dp(send_b, bits_b[0]))

    @property
    def on_last(self):
        return self.stage == self.steps - 1

    def step(self):
        self.stage += 1
        count, stage = self.count, self.stage
        last = self.bits_a[-1]
        if stage < count:
            rows, lanes = self.state[0].shape[1:]
            if stage < count - 1:
                bit_a, bit_b = self.bits_a[stage], self.bits_b[stage]
                keep_a, send_a, keep_b, send_b = call(
                    lambda *refs: halve_kernel(bit_a, bit_b, *refs),
                    (shape((2, rows // 2, lanes), BF16),) * 4,
                    *self.state,
                )
                self.state = (keep_a, from_dp(send_a, bit_a), keep_b, from_dp(send_b, bit_b))
            else:
                keep, to_dp, to_row, to_both = call(
                    lambda *refs: cross_kernel(last, *refs),
                    (shape((2, rows // 2, lanes), BF16),) * 4,
                    *self.state,
                )
                self.state = (keep, from_dp(to_dp, last), from_row(to_row), from_both(to_both, last))
        elif not self.apart:
            self.gather()
        elif stage == count:
            rows, lanes = self.state[0].shape[1:]
            mine = call(join_kernel, shape((2, 2, rows, lanes), BF16), *self.state)
            self.state = (mine, from_dp(mine, last))
        elif stage == 2 * count:
            mine_a, got_a, mine_b, got_b, next_a, next_b = self.state
            more_a, more_b = from_dp(next_a, self.bits_a[0]), from_dp(next_b, self.bits_b[0])
            self.state = (mine_a, got_a, mine_b, got_b, next_a, more_a, next_b, more_b)
        elif self.apart and stage == 2 * count - 1:
            rows, lanes = self.state[0].shape[-2:]
            before_a, before_b = self.bits_a[1], self.bits_b[1]
            a0, a1, b0, b1 = call(
                lambda *refs: double_apart_kernel(before_a, before_b, *refs),
                (shape((2 * rows, lanes), BF16),) * 4,
                *self.state,
            )
            self.state = (a0, from_dp(a0, self.bits_a[0]), b0, from_dp(b0, self.bits_b[0]), a1, b1)
        else:
            index = 2 * count - 1 - stage
            bit_a, bit_b = self.bits_a[index], self.bits_b[index]
            rows, lanes = self.state[0].shape[-2:]
            outs = (shape((2, 2 * rows, lanes), BF16),) * 2
            if stage == count + 1:
                mine_a, mine_b = call(lambda *refs: part_kernel(last, *refs), outs, *self.state)
            else:
                before_a, before_b = self.bits_a[index + 1], self.bits_b[index + 1]
                mine_a, mine_b = call(
                    lambda *refs: double_kernel(before_a, before_b, *refs), outs, *self.state
                )
            self.state = (mine_a, from_dp(mine_a, bit_a), mine_b, from_dp(mine_b, bit_b))


    def gather(self):
        count, stage = self.count, self.stage
        rows, lanes = self.state[0].shape[-2:]
        last = self.bits_a[-1]
        if stage == count:
            out = shape((4 * rows + EXTRA, lanes), BF16)
            mine = call(join_more_kernel, out, *self.state, *self.vectors)
            self.state = (mine, from_dp(mine, last))
            return
        index = 2 * count - 1 - stage
        if stage == count + 1:
            rows = rows - EXTRA
            kernel = lambda *refs: part_more_kernel(last, *refs)
        else:
            rows = 2 * (rows - EXTRA)
            before_a, before_b = self.bits_a[index + 1], self.bits_b[index + 1]
            kernel = lambda *refs: double_more_kernel(before_a, before_b, *refs)
        outs = (shape((rows + EXTRA, lanes), BF16), shape((rows, lanes), BF16))
        mine_a, mine_b = call(kernel, outs, *self.state)
        got_a, got_b = from_dp(mine_a, self.bits_a[index]), from_dp(mine_b, self.bits_b[index])
        self.state = (mine_a, got_a, mine_b, got_b)


def arrived(pairs, *others):
    states, others = lax.optimization_barrier(([pair.state for pair in pairs], others))
    for pair, state in zip(pairs, states):
        pair.state = state
    return others


def ordered_halves(bit, mine, got):
    own = (lax.axis_index("dp") // (1 << bit)) % 2 == 0
    return jnp.concatenate(
        [jnp.where(own, mine, got), jnp.where(own, got, mine)], axis=0
    )


def by_row(mine, far, axis):
    first = lax.axis_index("row") == 0
    return jnp.concatenate(
        [jnp.where(first, mine, far), jnp.where(first, far, mine)], axis=axis
    )


def feed_end_kernel(bit, mine_0, got_0, mine_1, got_1, out):
    own = (lax.axis_index("dp") // (1 << bit)) % 2
    here = pl.program_id(1) == own
    near = pl.program_id(0) == lax.axis_index("row")
    part = jnp.where(
        near,
        jnp.where(here, mine_0[...], got_0[...]),
        jnp.where(here, mine_1[...], got_1[...]),
    )
    out[...] = part.astype(F32)


def attention_end(bit, flip, mine, got, left, right):
    rows, half = left.shape[0], left.shape[1]
    own = bit_clear(bit)
    part = rows // 2
    sides = []
    for p in range(2):
        low, high = mine[p * part : (p + 1) * part], got[p * part : (p + 1) * part]
        sides.append(jnp.concatenate([jnp.where(own, low, high), jnp.where(own, high, low)], axis=0))
    near, far = sides
    third = half // 2
    left[...] = by_row(near[:, :third], far[:, :third], 1).astype(F32)
    last = by_row(near[:, third:], far[:, third:], 1).astype(F32)
    right[...] = last.T if flip else last


def first_end_kernel(bit, mine, got, left, right, *refs):
    outs, held, sems = refs[:9], refs[9:18], refs[18]
    small = extra_sum(mine, got)
    half = small.shape[1]
    third = half // 2
    lines = [
        small[4:5, :third],
        small[4:5, third:],
        small[5:6],
        jnp.concatenate([small[6:7], small[7:8]], axis=1),
        small[8:9],
    ] + [small[i : i + 1] for i in range(4)]
    for ref, line in zip(held, lines):
        ref[...] = line.reshape(line.shape[1])
    copies = start_copies(list(zip(held, outs)), sems)
    attention_end(bit, False, mine, got, left, right)
    for copy in copies:
        copy.wait()


def second_end_kernel(bit, mine, got, left, right):
    attention_end(bit, True, mine, got, left, right)


def end_call(kernel, grid, out_shape, block, index, *operands):
    whole = pl.BlockSpec(memory_space=pltpu.VMEM)
    return pl.pallas_call(
        kernel,
        grid=grid,
        out_shape=out_shape,
        in_specs=[whole] * len(operands),
        out_specs=pl.BlockSpec(block, index),
        compiler_params=pltpu.CompilerParams(vmem_limit_bytes=16 * MIB),
    )(*operands)


def body(
    tokens,
    out_grad,
    seq_lengths,
    w_query,
    w_key,
    w_value,
    w_out,
    w_up,
    w_down,
    b_query,
    b_value,
    b_out,
    b_up,
    b_down,
    gain_attn,
    shift_attn,
    gain_mlp,
    shift_mlp,
):
    row = lax.axis_index("row")
    own_rows, half = tokens.shape
    width = 2 * half
    rows = 2 * own_rows
    third = w_query.shape[1] // 2
    units = w_up.shape[1] // 2
    side = lax.axis_index("dp") % 2
    count = lax.axis_size("dp").bit_length() - 1
    bits = list(range(count))
    turned = [1, 0] + bits[2:] if count > 1 else bits
    tall = shape((own_rows, width), F32)
    tall_low = shape((own_rows, width), BF16)
    column = shape((own_rows, 128), F32)
    pair_sums = shape((8, half), F32)

    tokens_far = from_row(tokens)
    vectors = (gain_attn, shift_attn, b_out, gain_mlp, shift_mlp, b_query, b_value, b_up, b_down)
    block = pltpu.VMEM((half, 2 * third), BF16)
    w_kept, sent, sent_out, sent_up, sent_down = call(
        start_kernel,
        (
            shape((half + EXTRA, 3 * third), BF16),
            shape((half // 2 + EXTRA, 3 * third), BF16),
            shape((w_out.shape[0] // 2, half), BF16),
            shape((half // 2, units), BF16),
            shape((units // 2, half), BF16),
        ),
        *vectors, w_query, w_key, w_value, w_out, w_up, w_down,
        hbm=range(15),
        scratch=[pltpu.VMEM(x.shape, x.dtype) for x in vectors]
        + [block, block, block, pltpu.VMEM((EXTRA, 3 * third), F32), pltpu.SemaphoreType.DMA((15,))],
        vmem=VMEM_START,
    )
    tokens_col = from_col(tokens)
    w_got = from_row(sent)
    w_side = from_dp(w_got, 0)
    up_got = from_row(sent_up)
    tokens_far_col = from_col(tokens_far)
    (
        tokens_far, tokens_col, tokens_far_col, w_got, w_side, up_got, sent_out, sent_down, out_grad_col
    ) = hold(
        tokens_far, tokens_col, tokens_far_col, w_got, w_side, up_got, sent_out, sent_down, out_grad
    )
    top_col = from_col(out_grad_col)
    out_got = from_row(sent_out)
    down_got = from_row(sent_down)
    out_side = from_dp(out_got, 0)
    up_side = from_dp(up_got, 0)
    every_token = (tokens, tokens_far, tokens_col, tokens_far_col)

    like = shape((rows, third), BF16)
    normed_all, query, key, value, mixed, lse = call(
        forward_kernel,
        (shape((rows, width), BF16), like, like, like, like, shape((8, rows), F32)),
        seq_lengths,
        *every_token,
        w_kept,
        w_got,
        w_side,
        smem=(0,),
        hbm_out=range(4),
        scratch=[pltpu.VMEM((rows, width), BF16)]
        + [pltpu.VMEM((rows, third), BF16)] * 3
        + [pltpu.SemaphoreType.DMA((4,))],
    )
    mixed_far = from_row(mixed)
    mixed_gate = mixed
    mixed_far, out_side, up_side, down_got, out_grad_send = hold(
        mixed_far, out_side, up_side, down_got, out_grad
    )

    keep, send, w_out_far = call(
        branch_kernel,
        (shape((rows, width), F32), shape((rows, width), BF16), shape(w_out.shape, BF16)),
        mixed_gate, mixed_far, w_out, out_got, out_side,
    )
    got = from_col(send)
    top_far = from_row(out_grad_send)
    down_side = from_dp(down_got, 1)
    (got,) = hold(got)

    middle, normed_mlp_all, unit_mlp, inverse_mlp = call(
        second_norm_kernel,
        (shape((own_rows, half), F32), shape((rows, width), BF16), tall, column),
        *every_token, keep, got, w_kept, w_got,
    )
    hidden, slope, w_up_far = call(
        up_kernel,
        (shape((rows, units), BF16), shape((rows, units), F32), shape((half, units), BF16)),
        normed_mlp_all, w_up, up_got, up_side, w_kept,
    )
    hidden, top_far = hold(hidden, top_far)
    top_far_col = from_col(top_far)
    top_far_col, down_side = hold(top_far_col, down_side)

    split_down = shape((2, units // 2, half), BF16)
    split_up = shape((2, half, units // 2), BF16)
    down_keep, down_send, up_keep, up_send, keep, send, mlp_sums, w_down_far = call(
        lambda *refs: down_kernel(bits[0], turned[0], *refs),
        (
            split_down, split_down, split_up, split_up, tall, tall_low,
            shape((8, units), F32), shape((units, half), BF16),
        ),
        seq_lengths, out_grad, top_far, top_col, top_far_col, hidden, slope, normed_mlp_all,
        w_down, down_got, down_side, w_up, w_up_far,
        scratch=[pltpu.VMEM((rows, width), BF16), pltpu.VMEM((rows, units), BF16)],
        smem=(0,),
    )
    got = from_col(send)
    feed = Pair(down_keep, down_send, up_keep, up_send, bits, turned, True)
    (got,) = hold(got)

    total = (keep + got.astype(F32)).astype(BF16)
    total_far = from_row(total)
    keep, send = call(
        output_kernel, (tall, tall_low), hidden, w_down, w_down_far,
    )
    got = from_col(send)
    total_far, got = hold(total_far, got)

    grad_middle, datt, mid_sums = call(
        second_back_kernel,
        (shape((own_rows, half), F32), tall_low, pair_sums),
        seq_lengths, total, total_far, unit_mlp, inverse_mlp, w_kept, w_got, out_grad, top_far,
        smem=(0,),
    )
    datt_col = from_col(datt)
    raised_keep, raised_got = keep, got
    (datt_col,) = arrived([feed], datt_col)
    feed.step()

    split_pair = shape((2, half // 2, 2 * third), BF16)
    first_keep, first_send, second_keep, second_send, keep, send, attn_sums = call(
        lambda *refs: backward_kernel(bits[0], turned[0], *refs),
        (split_pair,) * 4 + (tall, tall_low, shape((8, width), F32)),
        seq_lengths, datt, datt_col, w_out, w_out_far, query, key, value, mixed, lse,
        normed_all, w_kept, w_got, w_side,
        scratch=[
            pltpu.VMEM((rows, width), BF16),
            pltpu.VMEM((rows, 3 * third), BF16),
            pltpu.VMEM((rows, third), F32),
            pltpu.VMEM((rows, third), F32),
        ]
        + [pltpu.VMEM((rows, third), BF16)] * 4
        + [pltpu.VMEM((rows, width), BF16), pltpu.SemaphoreType.DMA((4,))],
        smem=(0,),
        hbm=(5, 6, 7, 10),
    )
    keep, send = arrived([feed], keep, send)
    got = from_col(send)
    attention = Pair(first_keep, first_send, second_keep, second_send, bits, turned, False)
    pairs = [feed, attention]
    feed.step()
    mine, raised, out, stats, unit_attn, inverse_attn = call(
        first_back_kernel,
        (
            shape((own_rows, half), F32),
            shape((own_rows, half), F32),
            shape((rows + EXTRA, half), BF16),
            shape((8, own_rows), F32),
            shape((own_rows, half), F32),
            column,
        ),
        keep, got, raised_keep, raised_got, tokens, tokens_far, w_kept, w_got,
    )
    (out,) = arrived([attention], out)
    got = from_row(out)
    feed.step()
    attention.step()

    output, input_grad, halves = call(
        last_kernel,
        (shape((own_rows, half), BF16), shape((own_rows, half), BF16), pair_sums),
        mine, raised, got, stats, unit_attn, inverse_attn, w_kept, middle, grad_middle, mid_sums,
    )
    (halves,) = arrived(pairs, halves)
    halves_col = from_col(halves)
    feed.step()
    attention.step()
    (halves_col,) = arrived(pairs, halves_col)
    attention.vectors = (halves, halves_col, mlp_sums, attn_sums)
    while not attention.on_last:
        moving = [pair for pair in pairs if not pair.on_last]
        for pair in moving:
            pair.step()
        arrived(moving)

    wide = w_query.shape[1]
    outs = (shape((half, wide), F32),) * 2
    mine_a, got_a, mine_b, got_b = attention.state
    sizes = (third, third, half, 2 * half, half, half, half, half, half)
    grad_query, grad_key, *vector_grads = call(
        lambda *refs: first_end_kernel(bits[0], *refs),
        outs + tuple(shape((size,), F32) for size in sizes),
        mine_a,
        got_a,
        hbm_out=range(2, 11),
        scratch=[pltpu.VMEM((size,), F32) for size in sizes] + [pltpu.SemaphoreType.DMA((9,))],
    )
    grad_value, grad_out = call(
        lambda *refs: second_end_kernel(turned[0], *refs), outs, mine_b, got_b
    )
    a_0, got_a_0, b_0, got_b_0, a_1, got_a_1, b_1, got_b_1 = feed.state
    grad_down = end_call(
        lambda *refs: feed_end_kernel(bits[0], *refs),
        (2, 2),
        shape((2 * units, half), F32),
        (units // 2, half),
        lambda i, j: (2 * i + j, 0),
        a_0,
        got_a_0,
        a_1,
        got_a_1,
    )
    grad_up = end_call(
        lambda *refs: feed_end_kernel(turned[0], *refs),
        (2, 2),
        shape((half, 2 * units), F32),
        (half, units // 2),
        lambda i, j: (0, 2 * i + j),
        b_0,
        got_b_0,
        b_1,
        got_b_1,
    )
    return (
        output,
        input_grad,
        grad_query,
        grad_key,
        grad_value,
        grad_out,
        grad_up,
        grad_down,
        *vector_grads,
    )


def solution(mesh):
    return jax.shard_map(
        body,
        mesh=mesh,
        in_specs=(
            P(("dp", "col"), "row"),
            P(("dp", "col"), "row"),
            P("dp", None),
            P("row", "col"),
            P("row", "col"),
            P("row", "col"),
            P("col", "row"),
            P("row", "col"),
            P("col", "row"),
            P(("col", "row")),
            P(("col", "row")),
            P("row"),
            P(("col", "row")),
            P("row"),
            P("row"),
            P("row"),
            P("row"),
            P("row"),
        ),
        out_specs=(
            P(("dp", "col"), "row"),
            P(("dp", "col"), "row"),
            P("row", "col"),
            P("row", "col"),
            P("row", "col"),
            P("col", "row"),
            P("row", "col"),
            P("col", "row"),
            P(("col", "row")),
            P(("col", "row")),
            P("row"),
            P(("col", "row")),
            P("row"),
            P("row"),
            P("row"),
            P("row"),
            P("row"),
        ),
        check_vma=False,
    )
```

```python
import jax
import jax.numpy as jnp
from jax import lax
from jax.experimental import pallas as pl
from jax.experimental.pallas import tpu as pltpu
from jax.sharding import PartitionSpec as P

HEAD_DIM = 64
EPSILON = 1e-05
MASKED = -1e30
F32 = jnp.float32
BF16 = jnp.bfloat16
SWAP = ((0, 1), (1, 0))
CUBIC = 0.044715
ROOT = 0.7978845608028654
MIB = 1024 * 1024
VMEM_START = 54
EXTRA = 16


def dot(left, right):
    return jnp.dot(left, right, preferred_element_type=F32)


def dot_nt(left, right):
    return lax.dot_general(left, right, (((1,), (1,)), ((), ())), preferred_element_type=F32)


def dot_tn(left, right):
    return lax.dot_general(left, right, (((0,), (0,)), ((), ())), preferred_element_type=F32)


def from_row(values):
    return lax.ppermute(values, "row", SWAP)


def from_col(values):
    return lax.ppermute(values, "col", SWAP)


def dp_pairs(bit):
    count = lax.axis_size("dp")
    return [(i, i ^ (1 << bit)) for i in range(count)]


def from_dp(values, bit):
    return lax.ppermute(values, "dp", dp_pairs(bit))


def hold(*values):
    return lax.optimization_barrier(values)


def shape(dims, kind):
    return jax.ShapeDtypeStruct(tuple(dims), kind)


def call(kernel, out_shape, *operands, scratch=(), smem=(), hbm=(), hbm_out=(), vmem=16):
    spaces = [
        pltpu.SMEM if i in smem else pltpu.HBM if i in hbm else pltpu.VMEM
        for i in range(len(operands))
    ]
    out_specs = jax.tree.map(lambda _: pl.BlockSpec(memory_space=pltpu.VMEM), out_shape)
    if hbm_out:
        out_specs = tuple(
            pl.BlockSpec(memory_space=pltpu.HBM if i in hbm_out else pltpu.VMEM)
            for i in range(len(out_shape))
        )
    return pl.pallas_call(
        kernel,
        out_shape=out_shape,
        in_specs=[pl.BlockSpec(memory_space=space) for space in spaces],
        out_specs=out_specs,
        scratch_shapes=list(scratch),
        compiler_params=pltpu.CompilerParams(vmem_limit_bytes=vmem * MIB),
        cost_estimate=pl.CostEstimate(flops=0, bytes_accessed=0, transcendentals=0),
    )(*operands)


def half_rows(index, size):
    return pl.ds(pl.multiple_of(index * size, size), size)


def start_copies(pairs, sems):
    copies = [
        pltpu.make_async_copy(source, target, sems.at[i]) for i, (source, target) in enumerate(pairs)
    ]
    for copy in copies:
        copy.start()
    return copies


GAIN_A, SHIFT_A, BIAS_O, GAIN_M, SHIFT_M, BIAS_QKV, BIAS_UP, BIAS_DOWN = 0, 1, 2, 3, 4, 5, 6, 8


def start_kernel(*refs):
    vectors, (w_q, w_k, w_v, w_out, w_up, w_down) = refs[:9], refs[9:15]
    kept, sent, out_sent, up_sent, down_sent = refs[15:20]
    held, held_w, extra, sems = refs[20:29], refs[29:32], refs[32], refs[33]
    row, side = lax.axis_index("row"), lax.axis_index("dp") % 2
    other_side = (lax.axis_index("dp") // 2) % 2
    units = up_sent.shape[1]
    copies = start_copies(
        list(zip((w_q, w_k, w_v), held_w))
        + list(zip(vectors, held))
        + [
            (w_out.at[half_rows(side, out_sent.shape[0])], out_sent),
            (w_up.at[half_rows(side, up_sent.shape[0]), half_rows(1 - row, units)], up_sent),
            (w_down.at[half_rows(2 * (1 - row) + other_side, down_sent.shape[0])], down_sent),
        ],
        sems,
    )
    first = row == 0
    half, third = w_q.shape[0], w_q.shape[1] // 2
    part = half // 2
    keeps, sends = [], []
    for ref, copy in zip(held_w, copies):
        copy.wait()
        low, high = ref[:, :third], ref[:, third:]
        keeps.append(jnp.where(first, low, high))
        away = jnp.where(first, high, low)
        sends.append(jnp.where(side == 0, away[:part], away[part:]))
    kept[:half] = jnp.concatenate(keeps, axis=1)
    sent[:part] = jnp.concatenate(sends, axis=1)
    for copy in copies[3:]:
        copy.wait()
    extra[...] = jnp.zeros_like(extra)
    lines = [ref[...].astype(F32).reshape(1, -1) for ref in held]
    for i in range(5):
        extra[i : i + 1, :half] = lines[i]
    b_q, b_v, b_u, b_d = lines[5:]
    extra[BIAS_QKV : BIAS_QKV + 1, :third] = b_q
    extra[BIAS_QKV : BIAS_QKV + 1, 2 * third :] = b_v
    for i in range(2):
        extra[BIAS_UP + i : BIAS_UP + i + 1, :half] = b_u[:, i * half : (i + 1) * half]
    extra[BIAS_DOWN : BIAS_DOWN + 1, :half] = b_d
    kept[half:] = extra[...].astype(BF16)
    sent[part:] = extra[...].astype(BF16)


def normed_parts(values):
    mean = jnp.mean(values, axis=1, keepdims=True)
    centered = values - mean
    variance = jnp.mean(centered * centered, axis=1, keepdims=True)
    inverse = lax.rsqrt(variance + EPSILON)
    return centered * inverse, inverse


def both_halves(mine, far):
    return jnp.concatenate([mine[...], far[...]], axis=1).astype(F32)


def vector_of(kept, i):
    return kept[kept.shape[0] - EXTRA :].astype(F32)[i : i + 1, : 2 * kept.shape[1] // 3]


def wide_vector(kept, got, i):
    return jnp.concatenate([vector_of(kept, i), vector_of(got, i)], axis=1)


def head_mask(width, head):
    lanes = lax.broadcasted_iota(jnp.int32, (1, width), 1)
    return lanes // HEAD_DIM == head


def allowed_block(lengths, keys, first_query, count):
    first, second = lengths[0, 0], lengths[0, 0] + lengths[0, 1]
    query = first_query + lax.broadcasted_iota(jnp.int32, (1, count), 1)
    begin = jnp.where(query >= second, second, jnp.where(query >= first, first, 0))
    key = lax.broadcasted_iota(jnp.int32, (keys, count), 0)
    return (key >= begin) & (key <= query)


def weights_got(got, got_side):
    part = got.shape[0] - EXTRA
    first = lax.axis_index("dp") % 2 == 0
    here, there = got[:part], got_side[:part]
    return jnp.concatenate([jnp.where(first, here, there), jnp.where(first, there, here)], axis=0)


def forward_kernel(lengths, own, own_far, col_own, col_far, w_kept, got, got_side, norm_hbm, q_hbm, k_hbm, v_hbm, o_out, lse,
                   norm_out, q_out, k_out, v_out, sems):
    own_rows, half = own.shape
    w_got = weights_got(got, got_side)
    third = q_out.shape[1]
    col = lax.axis_index("col")
    gain, shift = wide_vector(w_kept, got, GAIN_A), wide_vector(w_kept, got, SHIFT_A)
    bias = w_kept[half:].astype(F32)[BIAS_QKV : BIAS_QKV + 1]
    for ref, far, at in ((own, own_far, col), (col_own, col_far, 1 - col)):
        where = half_rows(at, own_rows)
        unit, _ = normed_parts(both_halves(ref, far))
        values = (unit * gain + shift).astype(BF16)
        norm_out[where] = values
        total = dot(values[:, :half], w_kept[:half]) + dot(values[:, half:], w_got)
        total = (total + bias).astype(BF16)
        q_out[where] = total[:, :third]
        k_out[where] = total[:, third : 2 * third]
        v_out[where] = total[:, 2 * third :]
    copies = start_copies(
        [(norm_out, norm_hbm), (q_out, q_hbm), (k_out, k_hbm), (v_out, v_hbm)], sems
    )
    lse[...] = jnp.zeros_like(lse)
    values_t = v_out[...].T
    for begin in (0, own_rows):
        keys = begin + own_rows
        allowed = allowed_block(lengths, keys, begin, own_rows)
        query = q_out[begin:keys] * BF16(HEAD_DIM ** (-0.5))
        parts = []
        for head in range(third // HEAD_DIM):
            key = jnp.where(head_mask(third, head), k_out[:keys], BF16(0))
            scores = jnp.where(allowed, dot_nt(key, query), MASKED)
            largest = jnp.max(scores, axis=0, keepdims=True)
            weights = jnp.exp(scores - largest)
            summed = jnp.sum(weights, axis=0, keepdims=True)
            lse[head : head + 1, begin:keys] = largest + jnp.log(summed)
            mixed = dot(
                values_t[head * HEAD_DIM : (head + 1) * HEAD_DIM, :keys], weights.astype(BF16)
            )
            parts.append(mixed / summed)
        o_out[begin:keys] = jnp.concatenate(parts, axis=0).T.astype(BF16)
    for copy in copies:
        copy.wait()


def split_tokens(total_of, keep, send, own_rows, col):
    keep[...] = total_of(half_rows(col, own_rows))
    send[...] = total_of(half_rows(1 - col, own_rows)).astype(BF16)


def branch_kernel(mixed, mixed_other, w_mine, got, got_side, keep, send, w_other):
    w_other[...] = both_sides(got, got_side, 0)
    row = lax.axis_index("row")
    third = mixed.shape[1]
    own, far = half_rows(row, third), half_rows(1 - row, third)

    for i, w in enumerate((w_mine, w_other)):
        lanes = slice(i * w.shape[1], (i + 1) * w.shape[1])
        part = dot(mixed[...], w[own]) + dot(mixed_other[...], w[far])
        keep[:, lanes] = part
        send[:, lanes] = part.astype(BF16)


def second_norm_kernel(own, own_far, col_own, col_far, keep, got, kept, sent, middle, normed, unit_out, inverse_out):
    own_rows = own.shape[0]
    col = lax.axis_index("col")
    bias, gain, shift = [wide_vector(kept, sent, i) for i in (BIAS_O, GAIN_M, SHIFT_M)]
    for ref, far, at in ((own, own_far, col), (col_own, col_far, 1 - col)):
        where = half_rows(at, own_rows)
        values = both_halves(ref, far) + (keep[where] + got[where].astype(F32) + bias)
        unit, inverse = normed_parts(values)
        normed[where] = (unit * gain + shift).astype(BF16)
        if ref is own:
            middle[...] = values[:, : middle.shape[1]]
            unit_out[...] = unit
            inverse_out[...] = jnp.broadcast_to(inverse, inverse_out.shape)


def both_sides(got, got_side, axis, bit=0):
    first = (lax.axis_index("dp") // (1 << bit)) % 2 == 0
    low = jnp.where(first, got[...], got_side[...])
    high = jnp.where(first, got_side[...], got[...])
    return jnp.concatenate([low, high], axis=axis)


def up_kernel(normed, w_up, got, got_side, kept, hidden_out, slope_out, w_other_out):
    rows, width = normed.shape
    half = width // 2
    units = got.shape[1]
    row = lax.axis_index("row")
    w_mine = w_up[:, pl.ds(pl.multiple_of(row * units, units), units)]
    w_other = both_sides(got, got_side, 0)
    w_other_out[...] = w_other
    bias = jnp.concatenate([vector_of(kept, BIAS_UP + i) for i in range(2)], axis=1)
    for begin in (0, rows // 2):
        where = slice(begin, begin + rows // 2)
        values = normed[where]
        u = dot(values[:, :half], w_mine) + dot(values[:, half:], w_other) + bias
        squared = u * u
        bent = jnp.tanh(ROOT * (u + CUBIC * (squared * u)))
        raised = 0.5 * (1.0 + bent)
        hidden_out[where] = (u * raised).astype(BF16)
        slope_out[where] = raised + 0.5 * u * (1.0 - bent * bent) * (
            ROOT * (1.0 + (3.0 * CUBIC) * squared)
        )


def split_rows(total, keep, send, bit):
    own = (lax.axis_index("dp") // (1 << bit)) % 2 == 0
    half = keep.shape[-2]
    low, high = total[..., :half, :], total[..., half:, :]
    keep[...] = jnp.where(own, low, high)
    send[...] = jnp.where(own, high, low)


def masked_top(lengths, mine, far, at):
    live = lengths[0, 0] + lengths[0, 1]
    own_rows = mine.shape[0]
    position = at * own_rows + lax.broadcasted_iota(jnp.int32, (own_rows, 1), 0)
    values = jnp.concatenate([mine[...], far[...]], axis=1)
    return jnp.where(position < live, values, BF16(0))


def down_kernel(bit_down, bit_up, lengths, top, top_far, top_col, top_far_col, hidden, slope, normed, w_down, got, got_side,
                w_up, w_up_other, down_keep, down_send, up_keep, up_send, keep, send, sums, w_other_out, top_all, grad_pre):
    own_rows, half = top.shape
    units = hidden.shape[1]
    row, col = lax.axis_index("row"), lax.axis_index("col")
    top_all[half_rows(col, own_rows)] = masked_top(lengths, top, top_far, col)
    top_all[half_rows(1 - col, own_rows)] = masked_top(lengths, top_col, top_far_col, 1 - col)
    top_rows = top_all[...]
    total = dot_tn(hidden[...], top_rows).astype(BF16)
    split_rows(jnp.stack([total[:, :half], total[:, half:]]), down_keep, down_send, bit_down)
    w_other = both_sides(got, got_side, 0, 1)
    w_other_out[...] = w_other
    grad_hidden = dot_nt(top_rows[:, :half], w_down[half_rows(row, units)]) + dot_nt(
        top_rows[:, half:], w_other
    )
    grads = (grad_hidden * slope[...]).astype(BF16)
    grad_pre[...] = grads
    w_mine = w_up[:, pl.ds(pl.multiple_of(row * units, units), units)]

    def total_of(rows):
        values = grad_pre[rows]
        return jnp.concatenate([dot_nt(values, w_mine), dot_nt(values, w_up_other[...])], axis=1)

    split_tokens(total_of, keep, send, own_rows, col)
    total = dot_tn(normed[...], grads).astype(BF16)
    total = total.reshape(2, half, units)
    total = jnp.concatenate([total[..., : units // 2], total[..., units // 2 :]], axis=1)
    split_rows(total, up_keep, up_send, bit_up)
    sums[...] = jnp.zeros_like(sums)
    sums[0:1] = jnp.sum(grads.astype(F32), axis=0, keepdims=True)
    sums[1:2, :half] = jnp.sum(top_rows[:, :half].astype(F32), axis=0, keepdims=True)


def output_kernel(hidden, w_down, w_other, keep, send):
    units = hidden.shape[1]
    row, col = lax.axis_index("row"), lax.axis_index("col")
    w_mine = w_down[half_rows(row, units)]

    def total_of(rows):
        values = hidden[rows]
        return jnp.concatenate([dot(values, w_mine), dot(values, w_other[...])], axis=1)

    split_tokens(total_of, keep, send, keep.shape[0], col)


def second_back_kernel(lengths, total, total_far, unit_ref, inverse_ref, kept, sent, top, top_far, middle_out, datt, sums):
    half = top.shape[1]
    got = total_far[...].astype(F32)
    grads = total[...].astype(F32) + jnp.concatenate([got[:, half:], got[:, :half]], axis=1)
    unit = unit_ref[...]
    scaled = grads * wide_vector(kept, sent, GAIN_M)
    mean_plain = jnp.mean(scaled, axis=1, keepdims=True)
    mean_unit = jnp.mean(scaled * unit, axis=1, keepdims=True)
    own = masked_top(lengths, top, top_far, lax.axis_index("col")).astype(F32)
    result = own + inverse_ref[:, :1] * (scaled - mean_plain - unit * mean_unit)
    middle_out[...] = result[:, :half]
    datt[...] = result.astype(BF16)
    sums[...] = jnp.zeros_like(sums)
    sums[0:1] = jnp.sum((grads * unit)[:, :half], axis=0, keepdims=True)
    sums[1:2] = jnp.sum(grads[:, :half], axis=0, keepdims=True)


def backward_kernel(bit_first, bit_second, lengths, own, other, w_mine, w_other, q_hbm, k_hbm, v_hbm, o_ref, lse, normed_hbm, w_kept, got, got_side,
                    first_keep, first_send, second_keep, second_send, keep, send, sums, datt, out, acc_k, acc_v, do_ref,
                    q_ref, k_ref, v_ref, normed, sems):
    copies = start_copies(
        [(q_hbm, q_ref), (k_hbm, k_ref), (v_hbm, v_ref), (normed_hbm, normed)], sems
    )
    own_rows, width = own.shape
    half = width // 2
    third = q_ref.shape[1]
    row, col = lax.axis_index("row"), lax.axis_index("col")
    quarter = half_rows(row, third)
    for ref, at in ((own, col), (other, 1 - col)):
        where = half_rows(at, own_rows)
        values = ref[...]
        datt[where] = values
        do_ref[where] = (
            dot_nt(values[:, :half], w_mine[quarter]) + dot_nt(values[:, half:], w_other[quarter])
        ).astype(BF16)
    for copy in copies:
        copy.wait()
    keys_t = k_ref[...].T
    acc_k[...] = jnp.zeros_like(acc_k)
    acc_v[...] = jnp.zeros_like(acc_v)
    scale = BF16(HEAD_DIM ** (-0.5))
    for begin in (0, own_rows):
        keys = begin + own_rows
        allowed = allowed_block(lengths, keys, begin, own_rows)
        query = q_ref[begin:keys] * scale
        grad_mixed = do_ref[begin:keys]
        parts = []
        for head in range(third // HEAD_DIM):
            mask = head_mask(third, head)
            key = jnp.where(mask, k_ref[:keys], BF16(0))
            scores = jnp.where(allowed, dot_nt(key, query), MASKED)
            probs = jnp.exp(scores - lse[head : head + 1, begin:keys])
            value = jnp.where(mask, v_ref[:keys], BF16(0))
            grad_probs = dot_nt(value, grad_mixed)
            both = probs * grad_probs
            inner = jnp.sum(both, axis=0, keepdims=True)
            grad_raw = (both - probs * inner).astype(BF16) * scale
            acc_v[:keys] += jnp.where(mask, dot(probs.astype(BF16), grad_mixed), 0.0)
            acc_k[:keys] += jnp.where(mask, dot(grad_raw, q_ref[begin:keys]), 0.0)
            parts.append(dot(keys_t[head * HEAD_DIM : (head + 1) * HEAD_DIM, :keys], grad_raw))
        out[begin:keys, :third] = jnp.concatenate(parts, axis=0).T.astype(BF16)
    out[:, third : 2 * third] = acc_k[...].astype(BF16)
    out[:, 2 * third :] = acc_v[...].astype(BF16)
    grads = out[...]
    weights = dot_tn(normed[...], grads).astype(BF16)
    grad_out = dot_tn(datt[...], o_ref[...]).astype(BF16)
    split_rows(weights[:, : 2 * third].reshape(2, half, 2 * third), first_keep, first_send, bit_first)
    last = jnp.concatenate([weights[:, 2 * third :], grad_out], axis=1)
    split_rows(last.reshape(2, half, 2 * third), second_keep, second_send, bit_second)

    w_got = weights_got(got, got_side)

    def total_of(rows):
        values = out[rows]
        return jnp.concatenate([dot_nt(values, w_kept[:half]), dot_nt(values, w_got)], axis=1)

    split_tokens(total_of, keep, send, own_rows, col)
    sums[...] = jnp.zeros_like(sums)
    sums[0:1, : 3 * third] = jnp.sum(grads.astype(F32), axis=0, keepdims=True)
    sums[1:2, :half] = jnp.sum(datt[:, :half].astype(F32), axis=0, keepdims=True)


def first_back_kernel(keep, got, raised_keep, raised_got, own, own_far, kept, sent, mine, raised, out, stats, unit_out, inverse_out):
    own_rows, half = mine.shape
    unit, inverse = normed_parts(both_halves(own, own_far))
    unit_out[...] = unit[:, :half]
    inverse_out[...] = jnp.broadcast_to(inverse, inverse_out.shape)
    grads = keep[...] + got[...].astype(F32)
    total = raised_keep[...] + raised_got[...].astype(F32)
    mine[...], raised[...] = grads[:, :half], total[:, :half]
    out[:own_rows] = grads[:, half:].astype(BF16)
    out[own_rows : 2 * own_rows] = total[:, half:].astype(BF16)
    scaled = grads * wide_vector(kept, sent, GAIN_A)
    plain = jnp.sum(scaled, axis=1, keepdims=True)
    crossed = jnp.sum(scaled * unit, axis=1, keepdims=True)
    lanes = lax.broadcasted_iota(jnp.int32, (1, 128), 1)
    both = jnp.where(lanes == 0, plain, jnp.where(lanes == 1, crossed, 0.0)).T[:8]
    stats[...] = both
    high = both.astype(BF16)
    low = (both - high.astype(F32)).astype(BF16)
    out[2 * own_rows :] = jnp.zeros((EXTRA, half), BF16)
    out[2 * own_rows :, :own_rows] = jnp.concatenate([high, low], axis=0)


def last_kernel(mine, raised, got, stats, unit_ref, inverse_ref, kept, middle, grad_middle, mid_sums, output, result, sums):
    own_rows, half = mine.shape
    unit = unit_ref[...]
    grads = mine[...] + got[:own_rows].astype(F32)
    pairs = got[2 * own_rows :, :own_rows].astype(F32)
    total = (stats[...] + (pairs[:8] + pairs[8:])) / (2 * half)
    columns = jnp.concatenate([total, jnp.zeros((120, total.shape[1]), F32)], axis=0).T
    grad_in = inverse_ref[:, :1] * (
        grads * vector_of(kept, GAIN_A) - columns[:, 0:1] - unit * columns[:, 1:2]
    )
    result[...] = (grad_middle[...] + grad_in).astype(BF16)
    far = got[own_rows : 2 * own_rows].astype(F32)
    output[...] = (middle[...] + (raised[...] + far) + vector_of(kept, BIAS_DOWN)).astype(BF16)
    sums[...] = jnp.zeros_like(sums)
    sums[0:1] = jnp.sum(grads * unit, axis=0, keepdims=True)
    sums[1:2] = jnp.sum(grads, axis=0, keepdims=True)
    sums[2:4] = mid_sums[0:2]


def bit_clear(bit):
    return (lax.axis_index("dp") // (1 << bit)) % 2 == 0


def total_of_pair(kept, got):
    return (kept[...].astype(F32) + got[...].astype(F32)).astype(BF16)


def halve_kernel(bit_a, bit_b, kept_a, got_a, kept_b, got_b, keep_a, send_a, keep_b, send_b):
    split_rows(total_of_pair(kept_a, got_a), keep_a, send_a, bit_a)
    split_rows(total_of_pair(kept_b, got_b), keep_b, send_b, bit_b)


def cross_kernel(bit, kept_a, got_a, kept_b, got_b, keep, to_dp, to_row, to_both):
    own = bit_clear(bit)
    half = keep.shape[1]
    for i, (kept, got) in enumerate(((kept_a, got_a), (kept_b, got_b))):
        total = total_of_pair(kept, got)
        low, high = total[:, :half], total[:, half:]
        here, there = jnp.where(own, low, high), jnp.where(own, high, low)
        keep[i], to_dp[i], to_row[i], to_both[i] = here[0], there[0], here[1], there[1]


def join_kernel(keep, from_dp_ref, from_row_ref, from_both_ref, out):
    mine = total_of_pair(keep, from_dp_ref)
    other = total_of_pair(from_row_ref, from_both_ref)
    for i in range(2):
        out[i, 0], out[i, 1] = mine[i], other[i]


def join_more_kernel(keep, from_dp_ref, from_row_ref, from_both_ref, halves, halves_col, mlp, attn, out):
    mine = total_of_pair(keep, from_dp_ref)
    other = total_of_pair(from_row_ref, from_both_ref)
    rows, half = mine.shape[1:]
    for i in range(2):
        out[2 * i * rows : (2 * i + 1) * rows] = mine[i]
        out[(2 * i + 1) * rows : (2 * i + 2) * rows] = other[i]
    third = half // 2
    lines = [
        (halves[...] + halves_col[...])[:4],
        jnp.concatenate([attn[0:1, :third], attn[0:1, 2 * third : 3 * third]], axis=1),
        attn[1:2, :half],
        mlp[0:1, :half],
        mlp[0:1, half : 2 * half],
        mlp[1:2, :half],
        jnp.zeros((EXTRA - 9, half), F32),
    ]
    out[4 * rows :] = jnp.concatenate(lines, axis=0).astype(BF16)


def extra_sum(mine, got):
    return mine[-EXTRA:].astype(F32) + got[-EXTRA:].astype(F32)


def ordered_rows(own, mine, got, begin, rows, out, at):
    low, high = mine[begin : begin + rows], got[begin : begin + rows]
    out[at : at + rows] = jnp.where(own, low, high)
    out[at + rows : at + 2 * rows] = jnp.where(own, high, low)


def part_more_kernel(bit, mine, got, out_a, out_b):
    own = bit_clear(bit)
    rows = out_b.shape[0] // 4
    for i, out in enumerate((out_a, out_b)):
        for p in range(2):
            ordered_rows(own, mine, got, (2 * i + p) * rows, rows, out, 2 * p * rows)
    out_a[4 * rows :] = extra_sum(mine, got).astype(BF16)


def double_more_kernel(bit_a, bit_b, mine_a, got_a, mine_b, got_b, out_a, out_b):
    rows = mine_b.shape[0] // 2
    for bit, mine, got, out in ((bit_a, mine_a, got_a, out_a), (bit_b, mine_b, got_b, out_b)):
        own = bit_clear(bit)
        for p in range(2):
            ordered_rows(own, mine, got, p * rows, rows, out, 2 * p * rows)
    out_a[4 * rows :] = extra_sum(mine_a, got_a).astype(BF16)


def doubled(bit, mine, got, out):
    own = bit_clear(bit)
    half = mine.shape[1]
    out[:, :half] = jnp.where(own, mine, got)
    out[:, half:] = jnp.where(own, got, mine)


def part_kernel(bit, mine, got, out_a, out_b):
    doubled(bit, mine[0], got[0], out_a)
    doubled(bit, mine[1], got[1], out_b)


def double_kernel(bit_a, bit_b, mine_a, got_a, mine_b, got_b, out_a, out_b):
    doubled(bit_a, mine_a[...], got_a[...], out_a)
    doubled(bit_b, mine_b[...], got_b[...], out_b)


def double_apart_kernel(bit_a, bit_b, mine_a, got_a, mine_b, got_b, *outs):
    for i in range(2):
        for bit, mine, got, out in ((bit_a, mine_a, got_a, outs[i]), (bit_b, mine_b, got_b, outs[2 + i])):
            own = bit_clear(bit)
            half = mine.shape[1]
            out[:half] = jnp.where(own, mine[i], got[i])
            out[half:] = jnp.where(own, got[i], mine[i])


def from_both(values, bit):
    count = lax.axis_size("dp")
    pairs = [(2 * i + r, 2 * (i ^ (1 << bit)) + 1 - r) for i in range(count) for r in range(2)]
    return lax.ppermute(values, ("dp", "row"), pairs)


class Pair:
    def __init__(self, keep_a, send_a, keep_b, send_b, bits_a, bits_b, apart):
        self.bits_a, self.bits_b = bits_a, bits_b
        self.apart = apart
        self.count = len(bits_a)
        self.stage = 0
        self.steps = 2 * self.count + apart
        self.state = (keep_a, from_dp(send_a, bits_a[0]), keep_b, from_dp(send_b, bits_b[0]))

    @property
    def on_last(self):
        return self.stage == self.steps - 1

    def step(self):
        self.stage += 1
        count, stage = self.count, self.stage
        last = self.bits_a[-1]
        if stage < count:
            rows, lanes = self.state[0].shape[1:]
            if stage < count - 1:
                bit_a, bit_b = self.bits_a[stage], self.bits_b[stage]
                keep_a, send_a, keep_b, send_b = call(
                    lambda *refs: halve_kernel(bit_a, bit_b, *refs),
                    (shape((2, rows // 2, lanes), BF16),) * 4,
                    *self.state,
                )
                self.state = (keep_a, from_dp(send_a, bit_a), keep_b, from_dp(send_b, bit_b))
            else:
                keep, to_dp, to_row, to_both = call(
                    lambda *refs: cross_kernel(last, *refs),
                    (shape((2, rows // 2, lanes), BF16),) * 4,
                    *self.state,
                )
                self.state = (keep, from_dp(to_dp, last), from_row(to_row), from_both(to_both, last))
        elif not self.apart:
            self.gather()
        elif stage == count:
            rows, lanes = self.state[0].shape[1:]
            mine = call(join_kernel, shape((2, 2, rows, lanes), BF16), *self.state)
            self.state = (mine, from_dp(mine, last))
        elif stage == 2 * count:
            mine_a, got_a, mine_b, got_b, next_a, next_b = self.state
            more_a, more_b = from_dp(next_a, self.bits_a[0]), from_dp(next_b, self.bits_b[0])
            self.state = (mine_a, got_a, mine_b, got_b, next_a, more_a, next_b, more_b)
        elif self.apart and stage == 2 * count - 1:
            rows, lanes = self.state[0].shape[-2:]
            before_a, before_b = self.bits_a[1], self.bits_b[1]
            a0, a1, b0, b1 = call(
                lambda *refs: double_apart_kernel(before_a, before_b, *refs),
                (shape((2 * rows, lanes), BF16),) * 4,
                *self.state,
            )
            self.state = (a0, from_dp(a0, self.bits_a[0]), b0, from_dp(b0, self.bits_b[0]), a1, b1)
        else:
            index = 2 * count - 1 - stage
            bit_a, bit_b = self.bits_a[index], self.bits_b[index]
            rows, lanes = self.state[0].shape[-2:]
            outs = (shape((2, 2 * rows, lanes), BF16),) * 2
            if stage == count + 1:
                mine_a, mine_b = call(lambda *refs: part_kernel(last, *refs), outs, *self.state)
            else:
                before_a, before_b = self.bits_a[index + 1], self.bits_b[index + 1]
                mine_a, mine_b = call(
                    lambda *refs: double_kernel(before_a, before_b, *refs), outs, *self.state
                )
            self.state = (mine_a, from_dp(mine_a, bit_a), mine_b, from_dp(mine_b, bit_b))


    def gather(self):
        count, stage = self.count, self.stage
        rows, lanes = self.state[0].shape[-2:]
        last = self.bits_a[-1]
        if stage == count:
            out = shape((4 * rows + EXTRA, lanes), BF16)
            mine = call(join_more_kernel, out, *self.state, *self.vectors)
            self.state = (mine, from_dp(mine, last))
            return
        index = 2 * count - 1 - stage
        if stage == count + 1:
            rows = rows - EXTRA
            kernel = lambda *refs: part_more_kernel(last, *refs)
        else:
            rows = 2 * (rows - EXTRA)
            before_a, before_b = self.bits_a[index + 1], self.bits_b[index + 1]
            kernel = lambda *refs: double_more_kernel(before_a, before_b, *refs)
        outs = (shape((rows + EXTRA, lanes), BF16), shape((rows, lanes), BF16))
        mine_a, mine_b = call(kernel, outs, *self.state)
        got_a, got_b = from_dp(mine_a, self.bits_a[index]), from_dp(mine_b, self.bits_b[index])
        self.state = (mine_a, got_a, mine_b, got_b)


def arrived(pairs, *others):
    states, others = lax.optimization_barrier(([pair.state for pair in pairs], others))
    for pair, state in zip(pairs, states):
        pair.state = state
    return others


def ordered_halves(bit, mine, got):
    own = (lax.axis_index("dp") // (1 << bit)) % 2 == 0
    return jnp.concatenate(
        [jnp.where(own, mine, got), jnp.where(own, got, mine)], axis=0
    )


def by_row(mine, far, axis):
    first = lax.axis_index("row") == 0
    return jnp.concatenate(
        [jnp.where(first, mine, far), jnp.where(first, far, mine)], axis=axis
    )


def feed_end_kernel(bit, mine_0, got_0, mine_1, got_1, out):
    own = (lax.axis_index("dp") // (1 << bit)) % 2
    here = pl.program_id(1) == own
    near = pl.program_id(0) == lax.axis_index("row")
    part = jnp.where(
        near,
        jnp.where(here, mine_0[...], got_0[...]),
        jnp.where(here, mine_1[...], got_1[...]),
    )
    out[...] = part.astype(F32)


def attention_end(bit, flip, mine, got, left, right):
    rows, half = left.shape[0], left.shape[1]
    own = bit_clear(bit)
    part = rows // 2
    sides = []
    for p in range(2):
        low, high = mine[p * part : (p + 1) * part], got[p * part : (p + 1) * part]
        sides.append(jnp.concatenate([jnp.where(own, low, high), jnp.where(own, high, low)], axis=0))
    near, far = sides
    third = half // 2
    left[...] = by_row(near[:, :third], far[:, :third], 1).astype(F32)
    last = by_row(near[:, third:], far[:, third:], 1).astype(F32)
    right[...] = last.T if flip else last


def end_kernel(bit_a, bit_b, mine, got, mine_b, got_b, left, right, left_b, right_b, *refs):
    outs, held, sems = refs[:9], refs[9:18], refs[18]
    small = extra_sum(mine, got)
    half = small.shape[1]
    third = half // 2
    lines = [
        small[4:5, :third],
        small[4:5, third:],
        small[5:6],
        jnp.concatenate([small[6:7], small[7:8]], axis=1),
        small[8:9],
    ] + [small[i : i + 1] for i in range(4)]
    for ref, line in zip(held, lines):
        ref[...] = line.reshape(line.shape[1])
    copies = start_copies(list(zip(held, outs)), sems)
    attention_end(bit_a, False, mine, got, left, right)
    attention_end(bit_b, True, mine_b, got_b, left_b, right_b)
    for copy in copies:
        copy.wait()


def end_call(kernel, grid, out_shape, block, index, *operands):
    whole = pl.BlockSpec(memory_space=pltpu.VMEM)
    return pl.pallas_call(
        kernel,
        grid=grid,
        out_shape=out_shape,
        in_specs=[whole] * len(operands),
        out_specs=pl.BlockSpec(block, index),
        compiler_params=pltpu.CompilerParams(vmem_limit_bytes=16 * MIB),
    )(*operands)


def body(
    tokens,
    out_grad,
    seq_lengths,
    w_query,
    w_key,
    w_value,
    w_out,
    w_up,
    w_down,
    b_query,
    b_value,
    b_out,
    b_up,
    b_down,
    gain_attn,
    shift_attn,
    gain_mlp,
    shift_mlp,
):
    row = lax.axis_index("row")
    own_rows, half = tokens.shape
    width = 2 * half
    rows = 2 * own_rows
    third = w_query.shape[1] // 2
    units = w_up.shape[1] // 2
    side = lax.axis_index("dp") % 2
    count = lax.axis_size("dp").bit_length() - 1
    bits = list(range(count))
    turned = [1, 0] + bits[2:] if count > 1 else bits
    tall = shape((own_rows, width), F32)
    tall_low = shape((own_rows, width), BF16)
    column = shape((own_rows, 128), F32)
    pair_sums = shape((8, half), F32)

    tokens_far = from_row(tokens)
    vectors = (gain_attn, shift_attn, b_out, gain_mlp, shift_mlp, b_query, b_value, b_up, b_down)
    block = pltpu.VMEM((half, 2 * third), BF16)
    w_kept, sent, sent_out, sent_up, sent_down = call(
        start_kernel,
        (
            shape((half + EXTRA, 3 * third), BF16),
            shape((half // 2 + EXTRA, 3 * third), BF16),
            shape((w_out.shape[0] // 2, half), BF16),
            shape((half // 2, units), BF16),
            shape((units // 2, half), BF16),
        ),
        *vectors, w_query, w_key, w_value, w_out, w_up, w_down,
        hbm=range(15),
        scratch=[pltpu.VMEM(x.shape, x.dtype) for x in vectors]
        + [block, block, block, pltpu.VMEM((EXTRA, 3 * third), F32), pltpu.SemaphoreType.DMA((15,))],
        vmem=VMEM_START,
    )
    tokens_col = from_col(tokens)
    w_got = from_row(sent)
    w_side = from_dp(w_got, 0)
    up_got = from_row(sent_up)
    tokens_far_col = from_col(tokens_far)
    (
        tokens_far, tokens_col, tokens_far_col, w_got, w_side, up_got, sent_out, sent_down, out_grad_col
    ) = hold(
        tokens_far, tokens_col, tokens_far_col, w_got, w_side, up_got, sent_out, sent_down, out_grad
    )
    top_col = from_col(out_grad_col)
    out_got = from_row(sent_out)
    down_got = from_row(sent_down)
    out_side = from_dp(out_got, 0)
    up_side = from_dp(up_got, 0)
    every_token = (tokens, tokens_far, tokens_col, tokens_far_col)

    like = shape((rows, third), BF16)
    normed_all, query, key, value, mixed, lse = call(
        forward_kernel,
        (shape((rows, width), BF16), like, like, like, like, shape((8, rows), F32)),
        seq_lengths,
        *every_token,
        w_kept,
        w_got,
        w_side,
        smem=(0,),
        hbm_out=range(4),
        scratch=[pltpu.VMEM((rows, width), BF16)]
        + [pltpu.VMEM((rows, third), BF16)] * 3
        + [pltpu.SemaphoreType.DMA((4,))],
    )
    mixed_far = from_row(mixed)
    mixed_gate = mixed
    mixed_far, out_side, up_side, down_got, out_grad_send = hold(
        mixed_far, out_side, up_side, down_got, out_grad
    )

    keep, send, w_out_far = call(
        branch_kernel,
        (shape((rows, width), F32), shape((rows, width), BF16), shape(w_out.shape, BF16)),
        mixed_gate, mixed_far, w_out, out_got, out_side,
    )
    got = from_col(send)
    top_far = from_row(out_grad_send)
    down_side = from_dp(down_got, 1)
    (got,) = hold(got)

    middle, normed_mlp_all, unit_mlp, inverse_mlp = call(
        second_norm_kernel,
        (shape((own_rows, half), F32), shape((rows, width), BF16), tall, column),
        *every_token, keep, got, w_kept, w_got,
    )
    hidden, slope, w_up_far = call(
        up_kernel,
        (shape((rows, units), BF16), shape((rows, units), F32), shape((half, units), BF16)),
        normed_mlp_all, w_up, up_got, up_side, w_kept,
    )
    hidden, top_far = hold(hidden, top_far)
    top_far_col = from_col(top_far)
    top_far_col, down_side = hold(top_far_col, down_side)

    split_down = shape((2, units // 2, half), BF16)
    split_up = shape((2, half, units // 2), BF16)
    down_keep, down_send, up_keep, up_send, keep, send, mlp_sums, w_down_far = call(
        lambda *refs: down_kernel(bits[0], turned[0], *refs),
        (
            split_down, split_down, split_up, split_up, tall, tall_low,
            shape((8, units), F32), shape((units, half), BF16),
        ),
        seq_lengths, out_grad, top_far, top_col, top_far_col, hidden, slope, normed_mlp_all,
        w_down, down_got, down_side, w_up, w_up_far,
        scratch=[pltpu.VMEM((rows, width), BF16), pltpu.VMEM((rows, units), BF16)],
        smem=(0,),
    )
    got = from_col(send)
    feed = Pair(down_keep, down_send, up_keep, up_send, bits, turned, True)
    (got,) = hold(got)

    total = (keep + got.astype(F32)).astype(BF16)
    total_far = from_row(total)
    keep, send = call(
        output_kernel, (tall, tall_low), hidden, w_down, w_down_far,
    )
    got = from_col(send)
    total_far, got = hold(total_far, got)

    grad_middle, datt, mid_sums = call(
        second_back_kernel,
        (shape((own_rows, half), F32), tall_low, pair_sums),
        seq_lengths, total, total_far, unit_mlp, inverse_mlp, w_kept, w_got, out_grad, top_far,
        smem=(0,),
    )
    datt_col = from_col(datt)
    raised_keep, raised_got = keep, got
    (datt_col,) = arrived([feed], datt_col)
    feed.step()

    split_pair = shape((2, half // 2, 2 * third), BF16)
    first_keep, first_send, second_keep, second_send, keep, send, attn_sums = call(
        lambda *refs: backward_kernel(bits[0], turned[0], *refs),
        (split_pair,) * 4 + (tall, tall_low, shape((8, width), F32)),
        seq_lengths, datt, datt_col, w_out, w_out_far, query, key, value, mixed, lse,
        normed_all, w_kept, w_got, w_side,
        scratch=[
            pltpu.VMEM((rows, width), BF16),
            pltpu.VMEM((rows, 3 * third), BF16),
            pltpu.VMEM((rows, third), F32),
            pltpu.VMEM((rows, third), F32),
        ]
        + [pltpu.VMEM((rows, third), BF16)] * 4
        + [pltpu.VMEM((rows, width), BF16), pltpu.SemaphoreType.DMA((4,))],
        smem=(0,),
        hbm=(5, 6, 7, 10),
    )
    keep, send = arrived([feed], keep, send)
    got = from_col(send)
    attention = Pair(first_keep, first_send, second_keep, second_send, bits, turned, False)
    pairs = [feed, attention]
    feed.step()
    mine, raised, out, stats, unit_attn, inverse_attn = call(
        first_back_kernel,
        (
            shape((own_rows, half), F32),
            shape((own_rows, half), F32),
            shape((rows + EXTRA, half), BF16),
            shape((8, own_rows), F32),
            shape((own_rows, half), F32),
            column,
        ),
        keep, got, raised_keep, raised_got, tokens, tokens_far, w_kept, w_got,
    )
    (out,) = arrived([attention], out)
    got = from_row(out)
    feed.step()
    attention.step()

    output, input_grad, halves = call(
        last_kernel,
        (shape((own_rows, half), BF16), shape((own_rows, half), BF16), pair_sums),
        mine, raised, got, stats, unit_attn, inverse_attn, w_kept, middle, grad_middle, mid_sums,
    )
    (halves,) = arrived(pairs, halves)
    halves_col = from_col(halves)
    feed.step()
    attention.step()
    (halves_col,) = arrived(pairs, halves_col)
    attention.vectors = (halves, halves_col, mlp_sums, attn_sums)
    while not attention.on_last:
        moving = [pair for pair in pairs if not pair.on_last]
        for pair in moving:
            pair.step()
        arrived(moving)

    wide = w_query.shape[1]
    outs = (shape((half, wide), F32),) * 2
    mine_a, got_a, mine_b, got_b = attention.state
    sizes = (third, third, half, 2 * half, half, half, half, half, half)
    grad_query, grad_key, grad_value, grad_out, *vector_grads = call(
        lambda *refs: end_kernel(bits[0], turned[0], *refs),
        outs + outs + tuple(shape((size,), F32) for size in sizes),
        mine_a,
        got_a,
        mine_b,
        got_b,
        hbm_out=range(4, 13),
        scratch=[pltpu.VMEM((size,), F32) for size in sizes] + [pltpu.SemaphoreType.DMA((9,))],
    )
    a_0, got_a_0, b_0, got_b_0, a_1, got_a_1, b_1, got_b_1 = feed.state
    grad_down = end_call(
        lambda *refs: feed_end_kernel(bits[0], *refs),
        (2, 2),
        shape((2 * units, half), F32),
        (units // 2, half),
        lambda i, j: (2 * i + j, 0),
        a_0,
        got_a_0,
        a_1,
        got_a_1,
    )
    grad_up = end_call(
        lambda *refs: feed_end_kernel(turned[0], *refs),
        (2, 2),
        shape((half, 2 * units), F32),
        (half, units // 2),
        lambda i, j: (0, 2 * i + j),
        b_0,
        got_b_0,
        b_1,
        got_b_1,
    )
    return (
        output,
        input_grad,
        grad_query,
        grad_key,
        grad_value,
        grad_out,
        grad_up,
        grad_down,
        *vector_grads,
    )


def solution(mesh):
    return jax.shard_map(
        body,
        mesh=mesh,
        in_specs=(
            P(("dp", "col"), "row"),
            P(("dp", "col"), "row"),
            P("dp", None),
            P("row", "col"),
            P("row", "col"),
            P("row", "col"),
            P("col", "row"),
            P("row", "col"),
            P("col", "row"),
            P(("col", "row")),
            P(("col", "row")),
            P("row"),
            P(("col", "row")),
            P("row"),
            P("row"),
            P("row"),
            P("row"),
            P("row"),
        ),
        out_specs=(
            P(("dp", "col"), "row"),
            P(("dp", "col"), "row"),
            P("row", "col"),
            P("row", "col"),
            P("row", "col"),
            P("col", "row"),
            P("row", "col"),
            P("col", "row"),
            P(("col", "row")),
            P(("col", "row")),
            P("row"),
            P(("col", "row")),
            P("row"),
            P("row"),
            P("row"),
            P("row"),
            P("row"),
        ),
        check_vma=False,
    )
```

```python
import jax
import jax.numpy as jnp
from jax import lax
from jax.experimental import pallas as pl
from jax.experimental.pallas import tpu as pltpu
from jax.sharding import PartitionSpec as P

HEAD_DIM = 64
EPSILON = 1e-05
MASKED = -1e30
F32 = jnp.float32
BF16 = jnp.bfloat16
SWAP = ((0, 1), (1, 0))
CUBIC = 0.044715
ROOT = 0.7978845608028654
MIB = 1024 * 1024
VMEM_START = 54
EXTRA = 16


def dot(left, right):
    return jnp.dot(left, right, preferred_element_type=F32)


def dot_nt(left, right):
    return lax.dot_general(left, right, (((1,), (1,)), ((), ())), preferred_element_type=F32)


def dot_tn(left, right):
    return lax.dot_general(left, right, (((0,), (0,)), ((), ())), preferred_element_type=F32)


def from_row(values):
    return lax.ppermute(values, "row", SWAP)


def from_col(values):
    return lax.ppermute(values, "col", SWAP)


def dp_pairs(bit):
    count = lax.axis_size("dp")
    return [(i, i ^ (1 << bit)) for i in range(count)]


def from_dp(values, bit):
    return lax.ppermute(values, "dp", dp_pairs(bit))


def hold(*values):
    return lax.optimization_barrier(values)


def shape(dims, kind):
    return jax.ShapeDtypeStruct(tuple(dims), kind)


def call(kernel, out_shape, *operands, scratch=(), smem=(), hbm=(), hbm_out=(), vmem=16):
    spaces = [
        pltpu.SMEM if i in smem else pltpu.HBM if i in hbm else pltpu.VMEM
        for i in range(len(operands))
    ]
    out_specs = jax.tree.map(lambda _: pl.BlockSpec(memory_space=pltpu.VMEM), out_shape)
    if hbm_out:
        out_specs = tuple(
            pl.BlockSpec(memory_space=pltpu.HBM if i in hbm_out else pltpu.VMEM)
            for i in range(len(out_shape))
        )
    return pl.pallas_call(
        kernel,
        out_shape=out_shape,
        in_specs=[pl.BlockSpec(memory_space=space) for space in spaces],
        out_specs=out_specs,
        scratch_shapes=list(scratch),
        compiler_params=pltpu.CompilerParams(vmem_limit_bytes=vmem * MIB),
        cost_estimate=pl.CostEstimate(flops=0, bytes_accessed=0, transcendentals=0),
    )(*operands)


def half_rows(index, size):
    return pl.ds(pl.multiple_of(index * size, size), size)


def start_copies(pairs, sems):
    copies = [
        pltpu.make_async_copy(source, target, sems.at[i]) for i, (source, target) in enumerate(pairs)
    ]
    for copy in copies:
        copy.start()
    return copies


GAIN_A, SHIFT_A, BIAS_O, GAIN_M, SHIFT_M, BIAS_QKV, BIAS_UP, BIAS_DOWN = 0, 1, 2, 3, 4, 5, 6, 8


def start_kernel(*refs):
    vectors, (w_q, w_k, w_v, w_out, w_up, w_down) = refs[:9], refs[9:15]
    kept, sent, out_sent, up_sent, down_sent = refs[15:20]
    held, held_w, extra, sems = refs[20:29], refs[29:32], refs[32], refs[33]
    row, side = lax.axis_index("row"), lax.axis_index("dp") % 2
    other_side = (lax.axis_index("dp") // 2) % 2
    units = up_sent.shape[1]
    copies = start_copies(
        list(zip((w_q, w_k, w_v), held_w))
        + list(zip(vectors, held))
        + [
            (w_out.at[half_rows(side, out_sent.shape[0])], out_sent),
            (w_up.at[half_rows(side, up_sent.shape[0]), half_rows(1 - row, units)], up_sent),
            (w_down.at[half_rows(2 * (1 - row) + other_side, down_sent.shape[0])], down_sent),
        ],
        sems,
    )
    first = row == 0
    half, third = w_q.shape[0], w_q.shape[1] // 2
    part = half // 2
    keeps, sends = [], []
    for ref, copy in zip(held_w, copies):
        copy.wait()
        low, high = ref[:, :third], ref[:, third:]
        keeps.append(jnp.where(first, low, high))
        away = jnp.where(first, high, low)
        sends.append(jnp.where(side == 0, away[:part], away[part:]))
    kept[:half] = jnp.concatenate(keeps, axis=1)
    sent[:part] = jnp.concatenate(sends, axis=1)
    for copy in copies[3:]:
        copy.wait()
    extra[...] = jnp.zeros_like(extra)
    lines = [ref[...].astype(F32).reshape(1, -1) for ref in held]
    for i in range(5):
        extra[i : i + 1, :half] = lines[i]
    b_q, b_v, b_u, b_d = lines[5:]
    extra[BIAS_QKV : BIAS_QKV + 1, :third] = b_q
    extra[BIAS_QKV : BIAS_QKV + 1, 2 * third :] = b_v
    for i in range(2):
        extra[BIAS_UP + i : BIAS_UP + i + 1, :half] = b_u[:, i * half : (i + 1) * half]
    extra[BIAS_DOWN : BIAS_DOWN + 1, :half] = b_d
    kept[half:] = extra[...].astype(BF16)
    sent[part:] = extra[...].astype(BF16)


def normed_parts(values):
    mean = jnp.mean(values, axis=1, keepdims=True)
    centered = values - mean
    variance = jnp.mean(centered * centered, axis=1, keepdims=True)
    inverse = lax.rsqrt(variance + EPSILON)
    return centered * inverse, inverse


def both_halves(mine, far):
    return jnp.concatenate([mine[...], far[...]], axis=1).astype(F32)


def vector_of(kept, i):
    return kept[kept.shape[0] - EXTRA :].astype(F32)[i : i + 1, : 2 * kept.shape[1] // 3]


def wide_vector(kept, got, i):
    return jnp.concatenate([vector_of(kept, i), vector_of(got, i)], axis=1)


def head_mask(width, head):
    lanes = lax.broadcasted_iota(jnp.int32, (1, width), 1)
    return lanes // HEAD_DIM == head


def allowed_block(lengths, keys, first_query, count):
    first, second = lengths[0, 0], lengths[0, 0] + lengths[0, 1]
    query = first_query + lax.broadcasted_iota(jnp.int32, (1, count), 1)
    begin = jnp.where(query >= second, second, jnp.where(query >= first, first, 0))
    key = lax.broadcasted_iota(jnp.int32, (keys, count), 0)
    return (key >= begin) & (key <= query)


def weights_got(got, got_side):
    part = got.shape[0] - EXTRA
    first = lax.axis_index("dp") % 2 == 0
    here, there = got[:part], got_side[:part]
    return jnp.concatenate([jnp.where(first, here, there), jnp.where(first, there, here)], axis=0)


def forward_kernel(lengths, own, own_far, col_own, col_far, w_kept, got, got_side, norm_hbm, q_hbm, k_hbm, v_hbm, o_out, lse,
                   norm_out, q_out, k_out, v_out, sems):
    own_rows, half = own.shape
    w_got = weights_got(got, got_side)
    third = q_out.shape[1]
    col = lax.axis_index("col")
    gain, shift = wide_vector(w_kept, got, GAIN_A), wide_vector(w_kept, got, SHIFT_A)
    bias = w_kept[half:].astype(F32)[BIAS_QKV : BIAS_QKV + 1]
    for ref, far, at in ((own, own_far, col), (col_own, col_far, 1 - col)):
        where = half_rows(at, own_rows)
        unit, _ = normed_parts(both_halves(ref, far))
        values = (unit * gain + shift).astype(BF16)
        norm_out[where] = values
        total = dot(values[:, :half], w_kept[:half]) + dot(values[:, half:], w_got)
        total = (total + bias).astype(BF16)
        q_out[where] = total[:, :third]
        k_out[where] = total[:, third : 2 * third]
        v_out[where] = total[:, 2 * third :]
    copies = start_copies(
        [(norm_out, norm_hbm), (q_out, q_hbm), (k_out, k_hbm), (v_out, v_hbm)], sems
    )
    lse[...] = jnp.zeros_like(lse)
    values_t = v_out[...].T
    for begin in (0, own_rows):
        keys = begin + own_rows
        allowed = allowed_block(lengths, keys, begin, own_rows)
        query = q_out[begin:keys] * BF16(HEAD_DIM ** (-0.5))
        parts = []
        for head in range(third // HEAD_DIM):
            key = jnp.where(head_mask(third, head), k_out[:keys], BF16(0))
            scores = jnp.where(allowed, dot_nt(key, query), MASKED)
            largest = jnp.max(scores, axis=0, keepdims=True)
            weights = jnp.exp(scores - largest)
            summed = jnp.sum(weights, axis=0, keepdims=True)
            lse[head : head + 1, begin:keys] = largest + jnp.log(summed)
            mixed = dot(
                values_t[head * HEAD_DIM : (head + 1) * HEAD_DIM, :keys], weights.astype(BF16)
            )
            parts.append(mixed / summed)
        o_out[begin:keys] = jnp.concatenate(parts, axis=0).T.astype(BF16)
    for copy in copies:
        copy.wait()


def split_tokens(total_of, keep, send, own_rows, col):
    keep[...] = total_of(half_rows(col, own_rows))
    send[...] = total_of(half_rows(1 - col, own_rows)).astype(BF16)


def branch_kernel(mixed, mixed_other, w_mine, got, got_side, keep, send, w_other):
    w_other[...] = both_sides(got, got_side, 0)
    row = lax.axis_index("row")
    third = mixed.shape[1]
    own, far = half_rows(row, third), half_rows(1 - row, third)

    for i, w in enumerate((w_mine, w_other)):
        lanes = slice(i * w.shape[1], (i + 1) * w.shape[1])
        part = dot(mixed[...], w[own]) + dot(mixed_other[...], w[far])
        keep[:, lanes] = part
        send[:, lanes] = part.astype(BF16)


def second_norm_kernel(own, own_far, col_own, col_far, keep, got, kept, sent, middle, normed, unit_out, inverse_out):
    own_rows = own.shape[0]
    col = lax.axis_index("col")
    bias, gain, shift = [wide_vector(kept, sent, i) for i in (BIAS_O, GAIN_M, SHIFT_M)]
    for ref, far, at in ((own, own_far, col), (col_own, col_far, 1 - col)):
        where = half_rows(at, own_rows)
        values = both_halves(ref, far) + (keep[where] + got[where].astype(F32) + bias)
        unit, inverse = normed_parts(values)
        normed[where] = (unit * gain + shift).astype(BF16)
        if ref is own:
            middle[...] = values[:, : middle.shape[1]]
            unit_out[...] = unit
            inverse_out[...] = jnp.broadcast_to(inverse, inverse_out.shape)


def both_sides(got, got_side, axis, bit=0):
    first = (lax.axis_index("dp") // (1 << bit)) % 2 == 0
    low = jnp.where(first, got[...], got_side[...])
    high = jnp.where(first, got_side[...], got[...])
    return jnp.concatenate([low, high], axis=axis)


def up_kernel(normed, w_up, got, got_side, kept, hidden_out, slope_out, w_other_out):
    rows, width = normed.shape
    half = width // 2
    units = got.shape[1]
    row = lax.axis_index("row")
    w_mine = w_up[:, pl.ds(pl.multiple_of(row * units, units), units)]
    w_other = both_sides(got, got_side, 0)
    w_other_out[...] = w_other
    bias = jnp.concatenate([vector_of(kept, BIAS_UP + i) for i in range(2)], axis=1)
    for begin in (0, rows // 2):
        where = slice(begin, begin + rows // 2)
        values = normed[where]
        u = dot(values[:, :half], w_mine) + dot(values[:, half:], w_other) + bias
        squared = u * u
        bent = jnp.tanh(ROOT * (u + CUBIC * (squared * u)))
        raised = 0.5 * (1.0 + bent)
        hidden_out[where] = (u * raised).astype(BF16)
        slope_out[where] = raised + 0.5 * u * (1.0 - bent * bent) * (
            ROOT * (1.0 + (3.0 * CUBIC) * squared)
        )


def split_rows(total, keep, send, bit):
    own = (lax.axis_index("dp") // (1 << bit)) % 2 == 0
    half = keep.shape[-2]
    low, high = total[..., :half, :], total[..., half:, :]
    keep[...] = jnp.where(own, low, high)
    send[...] = jnp.where(own, high, low)


def masked_top(lengths, mine, far, at):
    live = lengths[0, 0] + lengths[0, 1]
    own_rows = mine.shape[0]
    position = at * own_rows + lax.broadcasted_iota(jnp.int32, (own_rows, 1), 0)
    values = jnp.concatenate([mine[...], far[...]], axis=1)
    return jnp.where(position < live, values, BF16(0))


def down_kernel(bit_down, bit_up, lengths, top, top_far, top_col, top_far_col, hidden, slope, normed, w_down, got, got_side,
                w_up, w_up_other, down_keep, down_send, up_keep, up_send, keep, send, sums, w_other_out, top_all, grad_pre):
    own_rows, half = top.shape
    units = hidden.shape[1]
    row, col = lax.axis_index("row"), lax.axis_index("col")
    top_all[half_rows(col, own_rows)] = masked_top(lengths, top, top_far, col)
    top_all[half_rows(1 - col, own_rows)] = masked_top(lengths, top_col, top_far_col, 1 - col)
    top_rows = top_all[...]
    total = dot_tn(hidden[...], top_rows).astype(BF16)
    split_rows(jnp.stack([total[:, :half], total[:, half:]]), down_keep, down_send, bit_down)
    w_other = both_sides(got, got_side, 0, 1)
    w_other_out[...] = w_other
    grad_hidden = dot_nt(top_rows[:, :half], w_down[half_rows(row, units)]) + dot_nt(
        top_rows[:, half:], w_other
    )
    grads = (grad_hidden * slope[...]).astype(BF16)
    grad_pre[...] = grads
    w_mine = w_up[:, pl.ds(pl.multiple_of(row * units, units), units)]

    def total_of(rows):
        values = grad_pre[rows]
        return jnp.concatenate([dot_nt(values, w_mine), dot_nt(values, w_up_other[...])], axis=1)

    split_tokens(total_of, keep, send, own_rows, col)
    total = dot_tn(normed[...], grads).astype(BF16)
    total = total.reshape(2, half, units)
    total = jnp.concatenate([total[..., : units // 2], total[..., units // 2 :]], axis=1)
    split_rows(total, up_keep, up_send, bit_up)
    sums[...] = jnp.zeros_like(sums)
    sums[0:1] = jnp.sum(grads.astype(F32), axis=0, keepdims=True)
    sums[1:2, :half] = jnp.sum(top_rows[:, :half].astype(F32), axis=0, keepdims=True)


def output_kernel(hidden, w_down, w_other, keep, send):
    units = hidden.shape[1]
    row, col = lax.axis_index("row"), lax.axis_index("col")
    w_mine = w_down[half_rows(row, units)]

    def total_of(rows):
        values = hidden[rows]
        return jnp.concatenate([dot(values, w_mine), dot(values, w_other[...])], axis=1)

    split_tokens(total_of, keep, send, keep.shape[0], col)


def second_back_kernel(lengths, total, total_far, unit_ref, inverse_ref, kept, sent, top, top_far, middle_out, datt, sums):
    half = top.shape[1]
    got = total_far[...].astype(F32)
    grads = total[...].astype(F32) + jnp.concatenate([got[:, half:], got[:, :half]], axis=1)
    unit = unit_ref[...]
    scaled = grads * wide_vector(kept, sent, GAIN_M)
    mean_plain = jnp.mean(scaled, axis=1, keepdims=True)
    mean_unit = jnp.mean(scaled * unit, axis=1, keepdims=True)
    own = masked_top(lengths, top, top_far, lax.axis_index("col")).astype(F32)
    result = own + inverse_ref[:, :1] * (scaled - mean_plain - unit * mean_unit)
    middle_out[...] = result[:, :half]
    datt[...] = result.astype(BF16)
    sums[...] = jnp.zeros_like(sums)
    sums[0:1] = jnp.sum((grads * unit)[:, :half], axis=0, keepdims=True)
    sums[1:2] = jnp.sum(grads[:, :half], axis=0, keepdims=True)


def backward_kernel(bit_first, bit_second, lengths, own, other, w_mine, w_other, q_hbm, k_hbm, v_hbm, o_ref, lse, normed_hbm, w_kept, got, got_side,
                    first_keep, first_send, second_keep, second_send, keep, send, sums, datt, out, acc_k, acc_v, do_ref,
                    q_ref, k_ref, v_ref, normed, sems):
    copies = start_copies(
        [(q_hbm, q_ref), (k_hbm, k_ref), (v_hbm, v_ref), (normed_hbm, normed)], sems
    )
    own_rows, width = own.shape
    half = width // 2
    third = q_ref.shape[1]
    row, col = lax.axis_index("row"), lax.axis_index("col")
    quarter = half_rows(row, third)
    for ref, at in ((own, col), (other, 1 - col)):
        where = half_rows(at, own_rows)
        values = ref[...]
        datt[where] = values
        do_ref[where] = (
            dot_nt(values[:, :half], w_mine[quarter]) + dot_nt(values[:, half:], w_other[quarter])
        ).astype(BF16)
    for copy in copies:
        copy.wait()
    keys_t = k_ref[...].T
    acc_k[...] = jnp.zeros_like(acc_k)
    acc_v[...] = jnp.zeros_like(acc_v)
    scale = BF16(HEAD_DIM ** (-0.5))
    for begin in (0, own_rows):
        keys = begin + own_rows
        allowed = allowed_block(lengths, keys, begin, own_rows)
        query = q_ref[begin:keys] * scale
        grad_mixed = do_ref[begin:keys]
        parts = []
        for head in range(third // HEAD_DIM):
            mask = head_mask(third, head)
            key = jnp.where(mask, k_ref[:keys], BF16(0))
            scores = jnp.where(allowed, dot_nt(key, query), MASKED)
            probs = jnp.exp(scores - lse[head : head + 1, begin:keys])
            value = jnp.where(mask, v_ref[:keys], BF16(0))
            grad_probs = dot_nt(value, grad_mixed)
            both = probs * grad_probs
            inner = jnp.sum(both, axis=0, keepdims=True)
            grad_raw = (both - probs * inner).astype(BF16) * scale
            acc_v[:keys] += jnp.where(mask, dot(probs.astype(BF16), grad_mixed), 0.0)
            acc_k[:keys] += jnp.where(mask, dot(grad_raw, q_ref[begin:keys]), 0.0)
            parts.append(dot(keys_t[head * HEAD_DIM : (head + 1) * HEAD_DIM, :keys], grad_raw))
        out[begin:keys, :third] = jnp.concatenate(parts, axis=0).T.astype(BF16)
    out[:, third : 2 * third] = acc_k[...].astype(BF16)
    out[:, 2 * third :] = acc_v[...].astype(BF16)
    grads = out[...]
    weights = dot_tn(normed[...], grads).astype(BF16)
    grad_out = dot_tn(datt[...], o_ref[...]).astype(BF16)
    split_rows(weights[:, : 2 * third].reshape(2, half, 2 * third), first_keep, first_send, bit_first)
    last = jnp.concatenate([weights[:, 2 * third :], grad_out], axis=1)
    split_rows(last.reshape(2, half, 2 * third), second_keep, second_send, bit_second)

    w_got = weights_got(got, got_side)

    def total_of(rows):
        values = out[rows]
        return jnp.concatenate([dot_nt(values, w_kept[:half]), dot_nt(values, w_got)], axis=1)

    split_tokens(total_of, keep, send, own_rows, col)
    sums[...] = jnp.zeros_like(sums)
    sums[0:1, : 3 * third] = jnp.sum(grads.astype(F32), axis=0, keepdims=True)
    sums[1:2, :half] = jnp.sum(datt[:, :half].astype(F32), axis=0, keepdims=True)


def first_back_kernel(keep, got, raised_keep, raised_got, own, own_far, kept, sent, mine, raised, out, stats, unit_out, inverse_out):
    own_rows, half = mine.shape
    unit, inverse = normed_parts(both_halves(own, own_far))
    unit_out[...] = unit[:, :half]
    inverse_out[...] = jnp.broadcast_to(inverse, inverse_out.shape)
    grads = keep[...] + got[...].astype(F32)
    total = raised_keep[...] + raised_got[...].astype(F32)
    mine[...], raised[...] = grads[:, :half], total[:, :half]
    out[:own_rows] = grads[:, half:].astype(BF16)
    out[own_rows : 2 * own_rows] = total[:, half:].astype(BF16)
    scaled = grads * wide_vector(kept, sent, GAIN_A)
    plain = jnp.sum(scaled, axis=1, keepdims=True)
    crossed = jnp.sum(scaled * unit, axis=1, keepdims=True)
    lanes = lax.broadcasted_iota(jnp.int32, (1, 128), 1)
    both = jnp.where(lanes == 0, plain, jnp.where(lanes == 1, crossed, 0.0)).T[:8]
    stats[...] = both
    high = both.astype(BF16)
    low = (both - high.astype(F32)).astype(BF16)
    out[2 * own_rows :] = jnp.zeros((EXTRA, half), BF16)
    out[2 * own_rows :, :own_rows] = jnp.concatenate([high, low], axis=0)


def last_kernel(mine, raised, got, stats, unit_ref, inverse_ref, kept, middle, grad_middle, mid_sums, output, result, sums):
    own_rows, half = mine.shape
    unit = unit_ref[...]
    grads = mine[...] + got[:own_rows].astype(F32)
    pairs = got[2 * own_rows :, :own_rows].astype(F32)
    total = (stats[...] + (pairs[:8] + pairs[8:])) / (2 * half)
    columns = jnp.concatenate([total, jnp.zeros((120, total.shape[1]), F32)], axis=0).T
    grad_in = inverse_ref[:, :1] * (
        grads * vector_of(kept, GAIN_A) - columns[:, 0:1] - unit * columns[:, 1:2]
    )
    result[...] = (grad_middle[...] + grad_in).astype(BF16)
    far = got[own_rows : 2 * own_rows].astype(F32)
    output[...] = (middle[...] + (raised[...] + far) + vector_of(kept, BIAS_DOWN)).astype(BF16)
    sums[...] = jnp.zeros_like(sums)
    sums[0:1] = jnp.sum(grads * unit, axis=0, keepdims=True)
    sums[1:2] = jnp.sum(grads, axis=0, keepdims=True)
    sums[2:4] = mid_sums[0:2]


def bit_clear(bit):
    return (lax.axis_index("dp") // (1 << bit)) % 2 == 0


def total_of_pair(kept, got):
    return (kept[...].astype(F32) + got[...].astype(F32)).astype(BF16)


def halve_kernel(bit_a, bit_b, kept_a, got_a, kept_b, got_b, keep_a, send_a, keep_b, send_b):
    split_rows(total_of_pair(kept_a, got_a), keep_a, send_a, bit_a)
    split_rows(total_of_pair(kept_b, got_b), keep_b, send_b, bit_b)


def cross_kernel(bit, kept_a, got_a, kept_b, got_b, keep, to_dp, to_row, to_both):
    own = bit_clear(bit)
    half = keep.shape[1]
    for i, (kept, got) in enumerate(((kept_a, got_a), (kept_b, got_b))):
        total = total_of_pair(kept, got)
        low, high = total[:, :half], total[:, half:]
        here, there = jnp.where(own, low, high), jnp.where(own, high, low)
        keep[i], to_dp[i], to_row[i], to_both[i] = here[0], there[0], here[1], there[1]


def join_kernel(keep, from_dp_ref, from_row_ref, from_both_ref, out):
    mine = total_of_pair(keep, from_dp_ref)
    other = total_of_pair(from_row_ref, from_both_ref)
    for i in range(2):
        out[i, 0], out[i, 1] = mine[i], other[i]


def join_more_kernel(keep, from_dp_ref, from_row_ref, from_both_ref, halves, halves_col, mlp, attn, out):
    mine = total_of_pair(keep, from_dp_ref)
    other = total_of_pair(from_row_ref, from_both_ref)
    rows, half = mine.shape[1:]
    for i in range(2):
        out[2 * i * rows : (2 * i + 1) * rows] = mine[i]
        out[(2 * i + 1) * rows : (2 * i + 2) * rows] = other[i]
    third = half // 2
    lines = [
        (halves[...] + halves_col[...])[:4],
        jnp.concatenate([attn[0:1, :third], attn[0:1, 2 * third : 3 * third]], axis=1),
        attn[1:2, :half],
        mlp[0:1, :half],
        mlp[0:1, half : 2 * half],
        mlp[1:2, :half],
        jnp.zeros((EXTRA - 9, half), F32),
    ]
    out[4 * rows :] = jnp.concatenate(lines, axis=0).astype(BF16)


def extra_sum(mine, got):
    return mine[-EXTRA:].astype(F32) + got[-EXTRA:].astype(F32)


def ordered_rows(own, mine, got, begin, rows, out, at):
    low, high = mine[begin : begin + rows], got[begin : begin + rows]
    out[at : at + rows] = jnp.where(own, low, high)
    out[at + rows : at + 2 * rows] = jnp.where(own, high, low)


def part_more_kernel(bit, mine, got, out_a, out_b):
    own = bit_clear(bit)
    rows = out_b.shape[0] // 4
    for i, out in enumerate((out_a, out_b)):
        for p in range(2):
            ordered_rows(own, mine, got, (2 * i + p) * rows, rows, out, 2 * p * rows)
    out_a[4 * rows :] = extra_sum(mine, got).astype(BF16)


def double_more_kernel(bit_a, bit_b, mine_a, got_a, mine_b, got_b, out_a, out_b):
    rows = mine_b.shape[0] // 2
    for bit, mine, got, out in ((bit_a, mine_a, got_a, out_a), (bit_b, mine_b, got_b, out_b)):
        own = bit_clear(bit)
        for p in range(2):
            ordered_rows(own, mine, got, p * rows, rows, out, 2 * p * rows)
    out_a[4 * rows :] = extra_sum(mine_a, got_a).astype(BF16)


def doubled(bit, mine, got, out):
    own = bit_clear(bit)
    half = mine.shape[1]
    out[:, :half] = jnp.where(own, mine, got)
    out[:, half:] = jnp.where(own, got, mine)


def part_kernel(bit, mine, got, out_a, out_b):
    doubled(bit, mine[0], got[0], out_a)
    doubled(bit, mine[1], got[1], out_b)


def double_kernel(bit_a, bit_b, mine_a, got_a, mine_b, got_b, out_a, out_b):
    doubled(bit_a, mine_a[...], got_a[...], out_a)
    doubled(bit_b, mine_b[...], got_b[...], out_b)


def double_apart_kernel(bit_a, bit_b, mine_a, got_a, mine_b, got_b, *outs):
    for i in range(2):
        for bit, mine, got, out in ((bit_a, mine_a, got_a, outs[i]), (bit_b, mine_b, got_b, outs[2 + i])):
            own = bit_clear(bit)
            half = mine.shape[1]
            out[:half] = jnp.where(own, mine[i], got[i])
            out[half:] = jnp.where(own, got[i], mine[i])


def from_both(values, bit):
    count = lax.axis_size("dp")
    pairs = [(2 * i + r, 2 * (i ^ (1 << bit)) + 1 - r) for i in range(count) for r in range(2)]
    return lax.ppermute(values, ("dp", "row"), pairs)


class Pair:
    def __init__(self, keep_a, send_a, keep_b, send_b, bits_a, bits_b, apart):
        self.bits_a, self.bits_b = bits_a, bits_b
        self.apart = apart
        self.count = len(bits_a)
        self.stage = 0
        self.steps = 2 * self.count + apart
        self.state = (keep_a, from_dp(send_a, bits_a[0]), keep_b, from_dp(send_b, bits_b[0]))

    @property
    def on_last(self):
        return self.stage == self.steps - 1

    def step(self):
        self.stage += 1
        count, stage = self.count, self.stage
        last = self.bits_a[-1]
        if stage < count:
            rows, lanes = self.state[0].shape[1:]
            if stage < count - 1:
                bit_a, bit_b = self.bits_a[stage], self.bits_b[stage]
                keep_a, send_a, keep_b, send_b = call(
                    lambda *refs: halve_kernel(bit_a, bit_b, *refs),
                    (shape((2, rows // 2, lanes), BF16),) * 4,
                    *self.state,
                )
                self.state = (keep_a, from_dp(send_a, bit_a), keep_b, from_dp(send_b, bit_b))
            else:
                keep, to_dp, to_row, to_both = call(
                    lambda *refs: cross_kernel(last, *refs),
                    (shape((2, rows // 2, lanes), BF16),) * 4,
                    *self.state,
                )
                self.state = (keep, from_dp(to_dp, last), from_row(to_row), from_both(to_both, last))
        elif not self.apart:
            self.gather()
        elif stage == count:
            rows, lanes = self.state[0].shape[1:]
            mine = call(join_kernel, shape((2, 2, rows, lanes), BF16), *self.state)
            self.state = (mine, from_dp(mine, last))
        elif stage == 2 * count:
            mine_a, got_a, mine_b, got_b, next_a, next_b = self.state
            more_a, more_b = from_dp(next_a, self.bits_a[0]), from_dp(next_b, self.bits_b[0])
            self.state = (mine_a, got_a, mine_b, got_b, next_a, more_a, next_b, more_b)
        elif self.apart and stage == 2 * count - 1:
            rows, lanes = self.state[0].shape[-2:]
            before_a, before_b = self.bits_a[1], self.bits_b[1]
            a0, a1, b0, b1 = call(
                lambda *refs: double_apart_kernel(before_a, before_b, *refs),
                (shape((2 * rows, lanes), BF16),) * 4,
                *self.state,
            )
            self.state = (a0, from_dp(a0, self.bits_a[0]), b0, from_dp(b0, self.bits_b[0]), a1, b1)
        else:
            index = 2 * count - 1 - stage
            bit_a, bit_b = self.bits_a[index], self.bits_b[index]
            rows, lanes = self.state[0].shape[-2:]
            outs = (shape((2, 2 * rows, lanes), BF16),) * 2
            if stage == count + 1:
                mine_a, mine_b = call(lambda *refs: part_kernel(last, *refs), outs, *self.state)
            else:
                before_a, before_b = self.bits_a[index + 1], self.bits_b[index + 1]
                mine_a, mine_b = call(
                    lambda *refs: double_kernel(before_a, before_b, *refs), outs, *self.state
                )
            self.state = (mine_a, from_dp(mine_a, bit_a), mine_b, from_dp(mine_b, bit_b))


    def gather(self):
        count, stage = self.count, self.stage
        rows, lanes = self.state[0].shape[-2:]
        last = self.bits_a[-1]
        if stage == count:
            out = shape((4 * rows + EXTRA, lanes), BF16)
            mine = call(join_more_kernel, out, *self.state, *self.vectors)
            self.state = (mine, from_dp(mine, last))
            return
        index = 2 * count - 1 - stage
        if stage == count + 1:
            rows = rows - EXTRA
            kernel = lambda *refs: part_more_kernel(last, *refs)
        else:
            rows = 2 * (rows - EXTRA)
            before_a, before_b = self.bits_a[index + 1], self.bits_b[index + 1]
            kernel = lambda *refs: double_more_kernel(before_a, before_b, *refs)
        outs = (shape((rows + EXTRA, lanes), BF16), shape((rows, lanes), BF16))
        mine_a, mine_b = call(kernel, outs, *self.state)
        got_a, got_b = from_dp(mine_a, self.bits_a[index]), from_dp(mine_b, self.bits_b[index])
        self.state = (mine_a, got_a, mine_b, got_b)


def arrived(pairs, *others):
    states, others = lax.optimization_barrier(([pair.state for pair in pairs], others))
    for pair, state in zip(pairs, states):
        pair.state = state
    return others


def ordered_halves(bit, mine, got):
    own = (lax.axis_index("dp") // (1 << bit)) % 2 == 0
    return jnp.concatenate(
        [jnp.where(own, mine, got), jnp.where(own, got, mine)], axis=0
    )


def by_row(mine, far, axis):
    first = lax.axis_index("row") == 0
    return jnp.concatenate(
        [jnp.where(first, mine, far), jnp.where(first, far, mine)], axis=axis
    )


def feed_end_kernel(bit, mine_0, got_0, mine_1, got_1, out):
    own = (lax.axis_index("dp") // (1 << bit)) % 2
    here = pl.program_id(1) == own
    near = pl.program_id(0) == lax.axis_index("row")
    part = jnp.where(
        near,
        jnp.where(here, mine_0[...], got_0[...]),
        jnp.where(here, mine_1[...], got_1[...]),
    )
    out[...] = part.astype(F32)


def attention_end(bit, flip, mine, got, left, right):
    rows, half = left.shape[0], left.shape[1]
    own = bit_clear(bit)
    part = rows // 2
    sides = []
    for p in range(2):
        low, high = mine[p * part : (p + 1) * part], got[p * part : (p + 1) * part]
        sides.append(jnp.concatenate([jnp.where(own, low, high), jnp.where(own, high, low)], axis=0))
    near, far = sides
    third = half // 2
    left[...] = by_row(near[:, :third], far[:, :third], 1).astype(F32)
    last = by_row(near[:, third:], far[:, third:], 1).astype(F32)
    right[...] = last.T if flip else last


def end_kernel(bit_a, bit_b, mine, got, mine_b, got_b, left, right, left_b, right_b, *refs):
    outs, held, sems = refs[:9], refs[9:18], refs[18]
    small = extra_sum(mine, got)
    half = small.shape[1]
    third = half // 2
    lines = [
        small[4:5, :third],
        small[4:5, third:],
        small[5:6],
        jnp.concatenate([small[6:7], small[7:8]], axis=1),
        small[8:9],
    ] + [small[i : i + 1] for i in range(4)]
    for ref, line in zip(held, lines):
        ref[...] = line.reshape(line.shape[1])
    copies = start_copies(list(zip(held, outs)), sems)
    attention_end(bit_a, False, mine, got, left, right)
    attention_end(bit_b, True, mine_b, got_b, left_b, right_b)
    for copy in copies:
        copy.wait()


def end_call(kernel, grid, out_shape, block, index, *operands):
    whole = pl.BlockSpec(memory_space=pltpu.VMEM)
    return pl.pallas_call(
        kernel,
        grid=grid,
        out_shape=out_shape,
        in_specs=[whole] * len(operands),
        out_specs=pl.BlockSpec(block, index),
        compiler_params=pltpu.CompilerParams(vmem_limit_bytes=16 * MIB),
    )(*operands)


def body(
    tokens,
    out_grad,
    seq_lengths,
    w_query,
    w_key,
    w_value,
    w_out,
    w_up,
    w_down,
    b_query,
    b_value,
    b_out,
    b_up,
    b_down,
    gain_attn,
    shift_attn,
    gain_mlp,
    shift_mlp,
):
    row = lax.axis_index("row")
    own_rows, half = tokens.shape
    width = 2 * half
    rows = 2 * own_rows
    third = w_query.shape[1] // 2
    units = w_up.shape[1] // 2
    side = lax.axis_index("dp") % 2
    count = lax.axis_size("dp").bit_length() - 1
    bits = list(range(count))
    turned = [1, 0] + bits[2:] if count > 1 else bits
    tall = shape((own_rows, width), F32)
    tall_low = shape((own_rows, width), BF16)
    column = shape((own_rows, 128), F32)
    pair_sums = shape((8, half), F32)

    tokens_far = from_row(tokens)
    vectors = (gain_attn, shift_attn, b_out, gain_mlp, shift_mlp, b_query, b_value, b_up, b_down)
    block = pltpu.VMEM((half, 2 * third), BF16)
    w_kept, sent, sent_out, sent_up, sent_down = call(
        start_kernel,
        (
            shape((half + EXTRA, 3 * third), BF16),
            shape((half // 2 + EXTRA, 3 * third), BF16),
            shape((w_out.shape[0] // 2, half), BF16),
            shape((half // 2, units), BF16),
            shape((units // 2, half), BF16),
        ),
        *vectors, w_query, w_key, w_value, w_out, w_up, w_down,
        hbm=range(15),
        scratch=[pltpu.VMEM(x.shape, x.dtype) for x in vectors]
        + [block, block, block, pltpu.VMEM((EXTRA, 3 * third), F32), pltpu.SemaphoreType.DMA((15,))],
        vmem=VMEM_START,
    )
    tokens_col = from_col(tokens)
    w_got = from_row(sent)
    w_side = from_dp(w_got, 0)
    up_got = from_row(sent_up)
    tokens_far_col = from_col(tokens_far)
    (
        tokens_far, tokens_col, tokens_far_col, w_got, w_side, up_got, sent_out, sent_down, out_grad_col
    ) = hold(
        tokens_far, tokens_col, tokens_far_col, w_got, w_side, up_got, sent_out, sent_down, out_grad
    )
    top_col = from_col(out_grad_col)
    out_got = from_row(sent_out)
    down_got = from_row(sent_down)
    out_side = from_dp(out_got, 0)
    up_side = from_dp(up_got, 0)
    every_token = (tokens, tokens_far, tokens_col, tokens_far_col)

    like = shape((rows, third), BF16)
    normed_all, query, key, value, mixed, lse = call(
        forward_kernel,
        (shape((rows, width), BF16), like, like, like, like, shape((8, rows), F32)),
        seq_lengths,
        *every_token,
        w_kept,
        w_got,
        w_side,
        smem=(0,),
        hbm_out=range(4),
        scratch=[pltpu.VMEM((rows, width), BF16)]
        + [pltpu.VMEM((rows, third), BF16)] * 3
        + [pltpu.SemaphoreType.DMA((4,))],
    )
    mixed_far = from_row(mixed)
    mixed_gate = mixed
    mixed_far, out_side, up_side, down_got, out_grad_send = hold(
        mixed_far, out_side, up_side, down_got, out_grad
    )

    keep, send, w_out_far = call(
        branch_kernel,
        (shape((rows, width), F32), shape((rows, width), BF16), shape(w_out.shape, BF16)),
        mixed_gate, mixed_far, w_out, out_got, out_side,
    )
    got = from_col(send)
    top_far = from_row(out_grad_send)
    down_side = from_dp(down_got, 1)
    (got,) = hold(got)

    middle, normed_mlp_all, unit_mlp, inverse_mlp = call(
        second_norm_kernel,
        (shape((own_rows, half), F32), shape((rows, width), BF16), tall, column),
        *every_token, keep, got, w_kept, w_got,
    )
    hidden, slope, w_up_far = call(
        up_kernel,
        (shape((rows, units), BF16), shape((rows, units), F32), shape((half, units), BF16)),
        normed_mlp_all, w_up, up_got, up_side, w_kept,
    )
    hidden, top_far = hold(hidden, top_far)
    top_far_col = from_col(top_far)
    top_far_col, down_side = hold(top_far_col, down_side)

    split_down = shape((2, units // 2, half), BF16)
    split_up = shape((2, half, units // 2), BF16)
    down_keep, down_send, up_keep, up_send, keep, send, mlp_sums, w_down_far = call(
        lambda *refs: down_kernel(bits[0], turned[0], *refs),
        (
            split_down, split_down, split_up, split_up, tall, tall_low,
            shape((8, units), F32), shape((units, half), BF16),
        ),
        seq_lengths, out_grad, top_far, top_col, top_far_col, hidden, slope, normed_mlp_all,
        w_down, down_got, down_side, w_up, w_up_far,
        scratch=[pltpu.VMEM((rows, width), BF16), pltpu.VMEM((rows, units), BF16)],
        smem=(0,),
    )
    got = from_col(send)
    feed = Pair(down_keep, down_send, up_keep, up_send, bits, turned, True)
    (got,) = hold(got)

    total = (keep + got.astype(F32)).astype(BF16)
    total_far = from_row(total)
    keep, send = call(
        output_kernel, (tall, tall_low), hidden, w_down, w_down_far,
    )
    got = from_col(send)
    total_far, got = hold(total_far, got)

    grad_middle, datt, mid_sums = call(
        second_back_kernel,
        (shape((own_rows, half), F32), tall_low, pair_sums),
        seq_lengths, total, total_far, unit_mlp, inverse_mlp, w_kept, w_got, out_grad, top_far,
        smem=(0,),
    )
    datt_col = from_col(datt)
    raised_keep, raised_got = keep, got
    (datt_col,) = arrived([feed], datt_col)
    feed.step()

    split_pair = shape((2, half // 2, 2 * third), BF16)
    first_keep, first_send, second_keep, second_send, keep, send, attn_sums = call(
        lambda *refs: backward_kernel(bits[0], turned[0], *refs),
        (split_pair,) * 4 + (tall, tall_low, shape((8, width), F32)),
        seq_lengths, datt, datt_col, w_out, w_out_far, query, key, value, mixed, lse,
        normed_all, w_kept, w_got, w_side,
        scratch=[
            pltpu.VMEM((rows, width), BF16),
            pltpu.VMEM((rows, 3 * third), BF16),
            pltpu.VMEM((rows, third), F32),
            pltpu.VMEM((rows, third), F32),
        ]
        + [pltpu.VMEM((rows, third), BF16)] * 4
        + [pltpu.VMEM((rows, width), BF16), pltpu.SemaphoreType.DMA((4,))],
        smem=(0,),
        hbm=(5, 6, 7, 10),
    )
    keep, send = arrived([feed], keep, send)
    feed.step()
    feed_keep, first_send, second_send, send = hold(feed.state[0], first_send, second_send, send)
    feed.state = (feed_keep,) + feed.state[1:]
    got = from_col(send)
    attention = Pair(first_keep, first_send, second_keep, second_send, bits, turned, False)
    pairs = [feed, attention]

    mine, raised, out, stats, unit_attn, inverse_attn = call(
        first_back_kernel,
        (
            shape((own_rows, half), F32),
            shape((own_rows, half), F32),
            shape((rows + EXTRA, half), BF16),
            shape((8, own_rows), F32),
            shape((own_rows, half), F32),
            column,
        ),
        keep, got, raised_keep, raised_got, tokens, tokens_far, w_kept, w_got,
    )
    (out,) = arrived([attention], out)
    got = from_row(out)
    feed.step()
    attention.step()

    output, input_grad, halves = call(
        last_kernel,
        (shape((own_rows, half), BF16), shape((own_rows, half), BF16), pair_sums),
        mine, raised, got, stats, unit_attn, inverse_attn, w_kept, middle, grad_middle, mid_sums,
    )
    (halves,) = arrived(pairs, halves)
    halves_col = from_col(halves)
    feed.step()
    attention.step()
    (halves_col,) = arrived(pairs, halves_col)
    attention.vectors = (halves, halves_col, mlp_sums, attn_sums)
    while not attention.on_last:
        moving = [pair for pair in pairs if not pair.on_last]
        for pair in moving:
            pair.step()
        arrived(moving)

    wide = w_query.shape[1]
    outs = (shape((half, wide), F32),) * 2
    mine_a, got_a, mine_b, got_b = attention.state
    sizes = (third, third, half, 2 * half, half, half, half, half, half)
    grad_query, grad_key, grad_value, grad_out, *vector_grads = call(
        lambda *refs: end_kernel(bits[0], turned[0], *refs),
        outs + outs + tuple(shape((size,), F32) for size in sizes),
        mine_a,
        got_a,
        mine_b,
        got_b,
        hbm_out=range(4, 13),
        scratch=[pltpu.VMEM((size,), F32) for size in sizes] + [pltpu.SemaphoreType.DMA((9,))],
    )
    a_0, got_a_0, b_0, got_b_0, a_1, got_a_1, b_1, got_b_1 = feed.state
    grad_down = end_call(
        lambda *refs: feed_end_kernel(bits[0], *refs),
        (2, 2),
        shape((2 * units, half), F32),
        (units // 2, half),
        lambda i, j: (2 * i + j, 0),
        a_0,
        got_a_0,
        a_1,
        got_a_1,
    )
    grad_up = end_call(
        lambda *refs: feed_end_kernel(turned[0], *refs),
        (2, 2),
        shape((half, 2 * units), F32),
        (half, units // 2),
        lambda i, j: (0, 2 * i + j),
        b_0,
        got_b_0,
        b_1,
        got_b_1,
    )
    return (
        output,
        input_grad,
        grad_query,
        grad_key,
        grad_value,
        grad_out,
        grad_up,
        grad_down,
        *vector_grads,
    )


def solution(mesh):
    return jax.shard_map(
        body,
        mesh=mesh,
        in_specs=(
            P(("dp", "col"), "row"),
            P(("dp", "col"), "row"),
            P("dp", None),
            P("row", "col"),
            P("row", "col"),
            P("row", "col"),
            P("col", "row"),
            P("row", "col"),
            P("col", "row"),
            P(("col", "row")),
            P(("col", "row")),
            P("row"),
            P(("col", "row")),
            P("row"),
            P("row"),
            P("row"),
            P("row"),
            P("row"),
        ),
        out_specs=(
            P(("dp", "col"), "row"),
            P(("dp", "col"), "row"),
            P("row", "col"),
            P("row", "col"),
            P("row", "col"),
            P("col", "row"),
            P("row", "col"),
            P("col", "row"),
            P(("col", "row")),
            P(("col", "row")),
            P("row"),
            P(("col", "row")),
            P("row"),
            P("row"),
            P("row"),
            P("row"),
            P("row"),
        ),
        check_vma=False,
    )
```
